32 devices in a mesh: seq: 8 (over y, x, core), chan: 4 (over z).
Axes of the slice: x: 2, y: 2, z: 4, core: 2. Of those that a mesh axis runs over, the one named last changes fastest.
Arguments:
- post_gate: bfloat16 [1024, 4096], P('seq', 'chan'), may hold values from -6 to 6
- pre_gate: bfloat16 [1024, 4096], P('seq', 'chan'), may hold values from -6 to 6
- signal: bfloat16 [1024, 4096], P('seq', 'chan'), may hold values from -6 to 6
- decay_rates: float32 [4096, 16], P('chan'), may hold values from 0.00029296875 to 0.0333333333
- residues: float32 [4096, 16], P('chan'), may hold values from -4 to 4
- skip_gain: float32 [4096], P('chan'), may hold values from -6 to 6
- out_weight: bfloat16 [4096, 4096], P('chan'), may hold values from -0.125 to 0.125
Outputs:
- output: bfloat16 [1024, 4096], P('seq', 'chan')
The draws below stay inside these ranges and needn't reach their ends.
All inputs are finite; a program needn't handle non-finite values.
Results may differ from the reference program's by a relative error of at most 0.022.
Values may be sent and summed in bfloat16 or wider, within the bound.
No kernel may reach another device: no remote copies, remote signals or barrier semaphores. Data moves between devices by JAX's collectives and lax.ppermute only.
A program may use at most 64 MiB of HBM per device.

```python
import jax
import jax.numpy as jnp
from jax import lax

D = 4096
CONV = 4096
MODES = 16
SEQ = 1024
N_CHAN = 4


def draw_decay_rates(key, part):
    key = jax.random.fold_in(key, 11)
    uniform_draw = jax.random.uniform(key, (CONV, MODES), jnp.float32)
    lowest = 0.5 / SEQ
    highest = 1.0 / 30
    spread = jnp.log(highest) - jnp.log(lowest)
    return jnp.exp(jnp.log(lowest) + uniform_draw * spread).astype(jnp.float32)


def spiked(array, rng, source, target, parts, factor):
    owner, partner = [(jnp.arange(array.shape[axis_at]) // (array.shape[axis_at] // parts)).reshape([-1 if axis == axis_at else 1 for axis in range(array.ndim)]) for axis_at in (source, target)]
    chosen = jax.random.permutation(rng, parts)[partner]
    strong = (owner == chosen) | (owner == (partner + parts // 2) % parts)
    return jnp.where(strong, factor * array, array)


def steps_of(stream_key, extent, cuts, smallest, top_value):
    gain, own = 1.0, jax.random.fold_in(stream_key, 6)
    for dim, shards_of in cuts:
        heights = jnp.exp(jax.random.uniform(jax.random.fold_in(own, dim), (shards_of,), jnp.float32, smallest / len(cuts), top_value / len(cuts)))
        gain = gain * jnp.repeat(heights, extent[dim] // shards_of).reshape([-1 if axis == dim else 1 for axis in range(len(extent))])
    return gain


def bell_draw(key, extent, scale, reach, pieces=(), kind=jnp.bfloat16):
    loudness = steps_of(key, extent, pieces, -0.22, 0.18) if pieces else 1.0
    result = jax.random.normal(key, extent, jnp.float32) * scale * loudness
    return jnp.minimum(jnp.maximum(result, -reach), reach).astype(kind)


def heavy_noise(stream_key, dims, scale, limit, pieces, heavy, kind=jnp.bfloat16):
    array = scale * jax.random.normal(stream_key, dims, jnp.float32)
    if pieces:
        array = array * steps_of(stream_key, dims, pieces, -0.22, 0.18)
    return jnp.clip(spiked(array, jax.random.fold_in(stream_key, 3), *heavy), -limit, limit).astype(kind)


def setup_inputs(seed: int = 0) -> dict:
    key_list = jax.random.split(jax.random.key(seed), 8)
    return {
        "post_gate": bell_draw(key_list[0], (SEQ, CONV), 1.0, 6.0, ((0, 8), (1, 4))),
        "pre_gate": bell_draw(key_list[1], (SEQ, CONV), 1.0, 6.0, ((0, 8), (1, 4))),
        "signal": bell_draw(key_list[2], (SEQ, CONV), 1.0, 6.0, ((0, 8), (1, 4))),
        "decay_rates": draw_decay_rates(jax.random.fold_in(key_list[7], 71), 0),
        "residues": bell_draw(key_list[4], (CONV, MODES), (MODES ** -0.5), 4.0, ((0, 4),), jnp.float32),
        "skip_gain": bell_draw(key_list[5], (CONV,), 1.0, 6.0, ((0, 4),), jnp.float32),
        "out_weight": heavy_noise(key_list[6], (CONV, D), CONV ** -0.5, 0.125, ((0, 4),), (0, 1, 4, 2.0)),
    }


def reference(post_gate, pre_gate, signal, decay_rates, residues, skip_gain, out_weight):
    mixed = pre_gate.astype(jnp.float32) * signal.astype(jnp.float32)
    times = jnp.arange(SEQ, dtype=jnp.float32)[:, None]

    def add_mode(mode_index, kernel):
        rate_now = lax.dynamic_index_in_dim(decay_rates, mode_index, 1, False)[None, :]
        weight_now = lax.dynamic_index_in_dim(residues, mode_index, 1, False)[None, :]
        return kernel + weight_now * jnp.sqrt(2.0 * rate_now) * jnp.exp(-rate_now * times)
    kernel = lax.fori_loop(0, MODES, add_mode, jnp.zeros((SEQ, CONV), jnp.float32))
    spectrum = jnp.fft.rfft(mixed, n=2 * SEQ, axis=0) * jnp.fft.rfft(kernel, n=2 * SEQ, axis=0)
    conv = jnp.fft.irfft(spectrum, n=2 * SEQ, axis=0)[:SEQ]
    gated = (post_gate.astype(jnp.float32) * (conv + skip_gain[None, :] * mixed)).astype(jnp.bfloat16)
    block_width = CONV // N_CHAN

    def project(running, group_index):
        start = (group_index * block_width).astype(jnp.int32)
        columns = lax.dynamic_slice_in_dim(gated, start, block_width, 1)
        weight_rows = lax.dynamic_slice_in_dim(out_weight, start, block_width, 0)
        partial_sum = jnp.dot(columns, weight_rows, preferred_element_type=jnp.float32).astype(jnp.bfloat16)
        return (running + partial_sum.astype(jnp.float32), None)
    summed, unused = lax.scan(project, jnp.zeros((SEQ, D), jnp.float32), jnp.arange(N_CHAN, dtype=jnp.int32))
    return summed.astype(jnp.bfloat16)
```

```python
import jax
import jax.numpy as jnp
from jax import lax
from jax.experimental import pallas as pl
from jax.experimental.pallas import tpu as pltpu
from jax.sharding import PartitionSpec as P

SUB = 16
LANES = 128
F32 = jnp.float32
VMEM = pl.BlockSpec(memory_space=pltpu.VMEM)


def call(kernel, outs, scratch, flops, moved):
    return pl.pallas_call(
        kernel,
        out_shape=[jax.ShapeDtypeStruct(shape, kind) for shape, kind in outs],
        out_specs=[VMEM] * len(outs),
        scratch_shapes=scratch,
        compiler_params=pltpu.CompilerParams(vmem_limit_bytes=40 * 2**20),
        cost_estimate=pl.CostEstimate(flops=flops, bytes_accessed=moved, transcendentals=0),
    )


def state_kernel(pre_ref, signal_ref, rates_ref, starts_ref, end_ref, mixed_ref):
    mixed_ref[...] = pre_ref[...].astype(F32) * signal_ref[...].astype(F32)
    fade = jnp.exp(-rates_ref[...])
    state = jnp.zeros(end_ref.shape, F32)
    for sub in range(starts_ref.shape[0]):
        starts_ref[sub] = state
        for token in range(sub * SUB, (sub + 1) * SUB):
            state = fade * state + mixed_ref[token : token + 1, :]
    end_ref[...] = state


def near_kernel(pre_ref, signal_ref, rates_ref, residues_ref, skip_ref, near_ref, table_ref, padded_ref):
    subs = padded_ref.shape[0]
    modes, width = rates_ref.shape
    weights = residues_ref[...] * jnp.sqrt(2.0 * rates_ref[...])
    steps = lax.broadcasted_iota(jnp.int32, (SUB, width), 0).astype(F32) + 1.0
    taps = jnp.zeros((SUB, width), F32)
    for mode in range(modes):
        entry = weights[mode : mode + 1, :] * jnp.exp(-rates_ref[mode : mode + 1, :] * steps)
        table_ref[mode] = entry
        taps = taps + entry
    first = jnp.sum(weights, axis=0, keepdims=True) + skip_ref[...]
    for sub in range(subs):
        rows = slice(sub * SUB, (sub + 1) * SUB)
        mixed = pre_ref[rows, :].astype(F32) * signal_ref[rows, :].astype(F32)
        padded_ref[sub, :SUB, :] = jnp.zeros((SUB, width), F32)
        padded_ref[sub, SUB:, :] = mixed
    for sub in range(subs):
        total = first * padded_ref[sub, SUB:, :]
        for lag in range(1, SUB):
            total = total + taps[lag - 1 : lag, :] * padded_ref[sub, SUB - lag : 2 * SUB - lag, :]
        near_ref[sub * SUB : (sub + 1) * SUB, :] = total


def gate_kernel(post_ref, near_ref, starts_ref, table_ref, rates_ref, carry_ref, gated_ref, states_ref):
    subs, modes, width = starts_ref.shape
    carry = carry_ref[...]
    for sub in range(subs):
        states_ref[sub] = starts_ref[sub] + jnp.exp(rates_ref[...] * (-float(SUB * sub))) * carry
    for sub in range(subs):
        rows = slice(sub * SUB, (sub + 1) * SUB)
        for lane in range(0, width, LANES):
            cols = slice(lane, lane + LANES)
            total = near_ref[rows, cols]
            for mode in range(modes):
                total = total + table_ref[mode, :, cols] * states_ref[sub, mode : mode + 1, cols]
            gated_ref[rows, cols] = (post_ref[rows, cols].astype(F32) * total).astype(gated_ref.dtype)


def radices(size):
    factors = []
    while size > 1:
        factor = 2 if not factors or size % 4 else 4
        factors.append(factor)
        size //= factor
    return factors


def carried_state(total, rates, rows):
    size = lax.axis_size("seq")
    me = lax.axis_index("seq")
    carry = jnp.zeros_like(total)
    stride = 1
    for factor in radices(size):
        digit = (me // stride) % factor
        place = me % stride
        last = stride * factor == size
        joined = total * jnp.exp(-rates * (rows * stride * (factor - 1 - digit)).astype(F32))
        for hop in range(1, factor):
            pairs = []
            for source in range(size):
                target_digit = (source // stride) % factor + hop
                if target_digit < factor:
                    pairs.append((source, source + hop * stride))
                elif not last:
                    pairs.append((source, source + (hop - factor) * stride))
            arrived = lax.ppermute(total, "seq", pairs)
            origin = (digit - hop) % factor
            blocks = place + stride * (digit - 1 - origin)
            before = origin < digit
            entering = arrived * jnp.exp(-rates * (rows * jnp.maximum(blocks, 0)).astype(F32))
            carry = carry + jnp.where(before, entering, 0.0)
            if not last:
                joined = joined + arrived * jnp.exp(
                    -rates * (rows * stride * (factor - 1 - origin)).astype(F32)
                )
        total = joined
        stride *= factor
    return carry


def body(post_gate, pre_gate, signal, decay_rates, residues, skip_gain, out_weight):
    rows, width = post_gate.shape
    modes = decay_rates.shape[1]
    subs = rows // SUB
    rates = decay_rates.T
    starts, end = call(
        state_kernel,
        [((subs, modes, width), F32), ((modes, width), F32)],
        [pltpu.VMEM((rows, width), F32)],
        4 * rows * modes * width,
        8 * rows * width,
    )(pre_gate, signal, rates)
    near, table = call(
        near_kernel,
        [((rows, width), F32), ((modes, SUB, width), F32)],
        [pltpu.VMEM((subs, 2 * SUB, width), F32)],
        2 * rows * SUB * width,
        8 * rows * width,
    )(pre_gate, signal, rates, residues.T, skip_gain.reshape(1, width))
    carry = carried_state(end, rates, rows)
    (gated,) = call(
        gate_kernel,
        [((rows, width), jnp.bfloat16)],
        [pltpu.VMEM((subs, modes, width), F32)],
        2 * rows * modes * width,
        16 * rows * width,
    )(post_gate, near, starts, table, rates, carry)
    partial_terms = jnp.dot(gated, out_weight, preferred_element_type=F32)
    return lax.psum_scatter(
        partial_terms.astype(jnp.bfloat16), "chan", scatter_dimension=1, tiled=True
    )


def solution(mesh):
    return jax.shard_map(
        body,
        mesh=mesh,
        in_specs=(
            P("seq", "chan"),
            P("seq", "chan"),
            P("seq", "chan"),
            P("chan", None),
            P("chan", None),
            P("chan"),
            P("chan", None),
        ),
        out_specs=P("seq", "chan"),
        check_vma=False,
    )
```

```python
import jax
import jax.numpy as jnp
from jax import lax
from jax.experimental import pallas as pl
from jax.experimental.pallas import tpu as pltpu
from jax.sharding import PartitionSpec as P

SUB = 16
LANES = 128
PIECES = 2
F32 = jnp.float32
BF16 = jnp.bfloat16
VMEM = pl.BlockSpec(memory_space=pltpu.VMEM)
ANY = pl.BlockSpec(memory_space=pl.ANY)
DMA = pltpu.SemaphoreType.DMA


def call(kernel, ins, outs, scratch, flops, moved):
    return pl.pallas_call(
        kernel,
        in_specs=ins,
        out_shape=[jax.ShapeDtypeStruct(shape, kind) for shape, kind in outs],
        out_specs=[VMEM] * len(outs),
        scratch_shapes=scratch,
        compiler_params=pltpu.CompilerParams(vmem_limit_bytes=32 * 2**20),
        cost_estimate=pl.CostEstimate(flops=flops, bytes_accessed=moved, transcendentals=0),
    )


def state_kernel(
    pre_hbm, signal_hbm, rates_hbm, residues_hbm, skip_hbm, post_hbm,
    mixed_ref, starts_ref, end_ref, rates_ref, residues_ref, skip_ref, post_ref,
    pre_ref, signal_ref, sems,
):
    moves = [
        pltpu.make_async_copy(source, target, sems.at[index])
        for index, (source, target) in enumerate(
            [
                (pre_hbm, pre_ref),
                (signal_hbm, signal_ref),
                (rates_hbm, rates_ref),
                (residues_hbm, residues_ref),
                (skip_hbm, skip_ref),
                (post_hbm, post_ref),
            ]
        )
    ]
    for move in moves:
        move.start()
    for move in moves[:3]:
        move.wait()
    mixed_ref[...] = pre_ref[...].astype(F32) * signal_ref[...].astype(F32)
    fade = jnp.exp(-rates_ref[...])
    state = jnp.zeros(end_ref.shape, F32)
    for sub in range(starts_ref.shape[0]):
        starts_ref[sub] = state
        for token in range(sub * SUB, (sub + 1) * SUB):
            state = fade * state + mixed_ref[token : token + 1, :]
    end_ref[...] = state
    for move in moves[3:]:
        move.wait()


def near_kernel(
    mixed_ref, rates_ref, residues_ref, skip_ref, weight_hbm,
    near_ref, table_ref, weight_ref,
    padded_ref, sem,
):
    subs = padded_ref.shape[0]
    modes, width = rates_ref.shape
    columns = weight_ref.shape[1]
    groups = weight_hbm.shape[1] // columns
    block = groups - 1 - lax.axis_index("chan")
    start = pl.multiple_of(block * columns, LANES)
    move = pltpu.make_async_copy(weight_hbm.at[:, pl.ds(start, columns)], weight_ref, sem)
    move.start()
    weights = residues_ref[...] * jnp.sqrt(2.0 * rates_ref[...])
    steps = lax.broadcasted_iota(jnp.int32, (SUB, width), 0).astype(F32) + 1.0
    taps = jnp.zeros((SUB, width), F32)
    for mode in range(modes):
        entry = weights[mode : mode + 1, :] * jnp.exp(-rates_ref[mode : mode + 1, :] * steps)
        table_ref[mode] = entry
        taps = taps + entry
    first = jnp.sum(weights, axis=0, keepdims=True) + skip_ref[...]
    for sub in range(subs):
        padded_ref[sub, :SUB, :] = jnp.zeros((SUB, width), F32)
        padded_ref[sub, SUB:, :] = mixed_ref[sub * SUB : (sub + 1) * SUB, :]
    for sub in range(subs):
        total = first * padded_ref[sub, SUB:, :]
        for lag in range(1, SUB):
            total = total + taps[lag - 1 : lag, :] * padded_ref[sub, SUB - lag : 2 * SUB - lag, :]
        near_ref[sub * SUB : (sub + 1) * SUB, :] = total
    move.wait()


def gate_kernel(
    post_ref, near_ref, starts_ref, table_ref, rates_ref, carry_ref, weight_ref,
    gated_ref, *rest,
):
    first_refs, states_ref = rest[:-1], rest[-1]
    subs, modes, width = starts_ref.shape
    carry = carry_ref[...]
    for sub in range(subs):
        states_ref[sub] = starts_ref[sub] + jnp.exp(rates_ref[...] * (-float(SUB * sub))) * carry
    for sub in range(subs):
        rows = slice(sub * SUB, (sub + 1) * SUB)
        for lane in range(0, width, LANES):
            cols = slice(lane, lane + LANES)
            total = near_ref[rows, cols]
            for mode in range(modes):
                total = total + table_ref[mode, :, cols] * states_ref[sub, mode : mode + 1, cols]
            gated_ref[rows, cols] = (post_ref[rows, cols].astype(F32) * total).astype(BF16)
    product = jnp.dot(gated_ref[...], weight_ref[...], preferred_element_type=F32).astype(BF16)
    height = product.shape[0] // len(first_refs)
    for piece, first_ref in enumerate(first_refs):
        first_ref[...] = product[piece * height : (piece + 1) * height, :]


def project_kernel(order, pieces, gated_ref, weight_hbm, *rest):
    out_refs, held_ref, sems = rest[:-2], rest[-2], rest[-1]
    columns = held_ref.shape[2]
    me = lax.axis_index("chan")
    moves = []
    for slot, offset in enumerate(order):
        start = pl.multiple_of((me ^ offset) * columns, LANES)
        moves.append(
            pltpu.make_async_copy(
                weight_hbm.at[:, pl.ds(start, columns)], held_ref.at[slot], sems.at[slot]
            )
        )
    for move in moves:
        move.start()
    height = gated_ref.shape[0] // pieces
    for slot, move in enumerate(moves):
        move.wait()
        product = jnp.dot(gated_ref[...], held_ref[slot], preferred_element_type=F32)
        for piece in range(pieces):
            out_ref = out_refs[slot * pieces + piece]
            out_ref[...] = product[piece * height : (piece + 1) * height, :].astype(out_ref.dtype)


def radices(size):
    factors = []
    while size > 1:
        factor = 2 if not factors or size % 4 else 4
        factors.append(factor)
        size //= factor
    return factors


def carried_state(total, rates, rows):
    size = lax.axis_size("seq")
    me = lax.axis_index("seq")
    carry = jnp.zeros_like(total)
    stride = 1
    for factor in radices(size):
        digit = (me // stride) % factor
        place = me % stride
        last = stride * factor == size
        joined = total * jnp.exp(-rates * (rows * stride * (factor - 1 - digit)).astype(F32))
        for hop in range(1, factor):
            pairs = []
            for source in range(size):
                target_digit = (source // stride) % factor + hop
                if target_digit < factor:
                    pairs.append((source, source + hop * stride))
                elif not last:
                    pairs.append((source, source + (hop - factor) * stride))
            arrived = lax.ppermute(total, "seq", pairs)
            origin = (digit - hop) % factor
            blocks = place + stride * (digit - 1 - origin)
            before = origin < digit
            entering = arrived * jnp.exp(-rates * (rows * jnp.maximum(blocks, 0)).astype(F32))
            carry = carry + jnp.where(before, entering, 0.0)
            if not last:
                joined = joined + arrived * jnp.exp(
                    -rates * (rows * stride * (factor - 1 - origin)).astype(F32)
                )
        total = joined
        stride *= factor
    return carry


def body(post_gate, pre_gate, signal, decay_rates, residues, skip_gain, out_weight):
    rows, width = post_gate.shape
    modes = decay_rates.shape[1]
    subs = rows // SUB
    groups = lax.axis_size("chan")
    columns = out_weight.shape[1] // groups
    height = rows // PIECES
    mixed, starts, end, rates, residues, skip, post = call(
        state_kernel,
        [ANY] * 6,
        [
            ((rows, width), F32),
            ((subs, modes, width), F32),
            ((modes, width), F32),
            ((modes, width), F32),
            ((modes, width), F32),
            ((1, width), F32),
            ((rows, width), BF16),
        ],
        [pltpu.VMEM((rows, width), BF16), pltpu.VMEM((rows, width), BF16), DMA((6,))],
        4 * rows * modes * width,
        8 * rows * width,
    )(pre_gate, signal, decay_rates.T, residues.T, skip_gain.reshape(1, width), post_gate)
    near, table, weight = call(
        near_kernel,
        [VMEM] * 4 + [ANY],
        [((rows, width), F32), ((modes, SUB, width), F32), ((width, columns), BF16)],
        [pltpu.VMEM((subs, 2 * SUB, width), F32), DMA],
        2 * rows * SUB * width,
        8 * rows * width,
    )(mixed, rates, residues, skip, out_weight)
    carry = carried_state(end, rates, rows)
    gated, *firsts = call(
        gate_kernel,
        [VMEM] * 7,
        [((rows, width), BF16)] + [((height, columns), BF16)] * PIECES,
        [pltpu.VMEM((subs, modes, width), F32)],
        2 * rows * modes * width,
        16 * rows * width,
    )(post, near, starts, table, rates, carry, weight)
    order = list(range(groups - 2, -1, -1))
    others = call(
        lambda *refs: project_kernel(order, PIECES, *refs),
        [VMEM, ANY],
        [((height, columns), F32)] * (PIECES * len(order)),
        [pltpu.VMEM((len(order), width, columns), BF16), DMA((len(order),))],
        2 * rows * width * columns * len(order),
        2 * width * columns * len(order),
    )(gated, out_weight)
    values = {groups - 1: list(firsts)}
    for slot, offset in enumerate(order):
        values[offset] = list(others[slot * PIECES : (slot + 1) * PIECES])
    stride = 1
    while stride < groups:
        pairs = [(source, source ^ stride) for source in range(groups)]
        for offset in range(groups - stride, 0, -2 * stride):
            for piece in range(PIECES):
                sent = values[offset][piece].astype(BF16)
                arrived = lax.ppermute(sent, "chan", pairs).astype(F32)
                values[offset ^ stride][piece] = values[offset ^ stride][piece] + arrived
        stride *= 2
    return jnp.concatenate([value.astype(BF16) for value in values[0]], axis=0)


def solution(mesh):
    return jax.shard_map(
        body,
        mesh=mesh,
        in_specs=(
            P("seq", "chan"),
            P("seq", "chan"),
            P("seq", "chan"),
            P("chan", None),
            P("chan", None),
            P("chan"),
            P("chan", None),
        ),
        out_specs=P("seq", "chan"),
        check_vma=False,
    )
```

```python
import functools

import jax
import jax.numpy as jnp
from jax import lax
from jax.experimental import pallas as pl
from jax.experimental.pallas import tpu as pltpu
from jax.sharding import PartitionSpec as P

SUB = 8
LANES = 128
PIECES = 2
F32 = jnp.float32
BF16 = jnp.bfloat16
VMEM = pl.BlockSpec(memory_space=pltpu.VMEM)
HBM = pl.BlockSpec(memory_space=pltpu.HBM)
DMA = pltpu.SemaphoreType.DMA


def call(kernel, ins, outs, scratch, flops, moved):
    run = pl.pallas_call(
        kernel,
        in_specs=ins,
        out_shape=[jax.ShapeDtypeStruct(shape, kind) for shape, kind in outs],
        out_specs=[VMEM] * len(outs),
        scratch_shapes=scratch,
        compiler_params=pltpu.CompilerParams(vmem_limit_bytes=32 * 2**20),
        cost_estimate=pl.CostEstimate(flops=flops, bytes_accessed=moved, transcendentals=0),
    )
    return lambda *operands: run(
        *[
            pltpu.with_memory_space_constraint(operand, pltpu.HBM) if spec is HBM else operand
            for spec, operand in zip(ins, operands)
        ]
    )


def state_kernel(
    pre_hbm, signal_hbm, rates_hbm, residues_hbm, skip_hbm, post_hbm,
    mixed_ref, starts_ref, end_ref, rates_ref, residues_ref, skip_ref, post_ref,
    pre_ref, signal_ref, sems,
):
    moves = [
        pltpu.make_async_copy(source, target, sems.at[index])
        for index, (source, target) in enumerate(
            [
                (pre_hbm, pre_ref),
                (signal_hbm, signal_ref),
                (rates_hbm, rates_ref),
                (residues_hbm, residues_ref),
                (skip_hbm, skip_ref),
                (post_hbm, post_ref),
            ]
        )
    ]
    for move in moves:
        move.start()
    for move in moves[:3]:
        move.wait()
    mixed_ref[...] = pre_ref[...].astype(F32) * signal_ref[...].astype(F32)
    fade = jnp.exp(-rates_ref[...])
    state = jnp.zeros(end_ref.shape, F32)
    for sub in range(starts_ref.shape[0]):
        starts_ref[sub] = state
        for token in range(sub * SUB, (sub + 1) * SUB):
            state = fade * state + mixed_ref[token : token + 1, :]
    end_ref[...] = state
    for move in moves[3:]:
        move.wait()


def near_kernel(
    mixed_ref, rates_ref, residues_ref, skip_ref, weight_hbm,
    near_ref, table_ref, weight_ref,
    sem,
):
    rows, width = mixed_ref.shape
    modes = rates_ref.shape[0]
    columns = weight_ref.shape[1]
    groups = weight_hbm.shape[1] // columns
    block = groups - 1 - lax.axis_index("chan")
    start = pl.multiple_of(block * columns, LANES)
    move = pltpu.make_async_copy(weight_hbm.at[:, pl.ds(start, columns)], weight_ref, sem)
    move.start()
    row_ids = lax.broadcasted_iota(jnp.int32, (SUB, LANES), 0)
    steps = row_ids.astype(F32) + 1.0
    for lane in range(0, width, LANES):
        cols = slice(lane, lane + LANES)
        weights = residues_ref[:, cols] * jnp.sqrt(2.0 * rates_ref[:, cols])
        taps = jnp.zeros((SUB, LANES), F32)
        for mode in range(modes):
            entry = weights[mode : mode + 1, :] * jnp.exp(-rates_ref[mode : mode + 1, cols] * steps)
            table_ref[mode, :, cols] = entry
            taps = taps + entry
        first = jnp.sum(weights, axis=0, keepdims=True) + skip_ref[:, cols]
        masked = [jnp.where(row_ids >= lag, taps[lag - 1 : lag, :], 0.0) for lag in range(1, SUB)]
        for sub in range(0, rows, SUB):
            mixed = mixed_ref[sub : sub + SUB, cols]
            total = first * mixed
            for lag in range(1, SUB):
                total = total + masked[lag - 1] * pltpu.roll(mixed, lag, 0)
            near_ref[sub : sub + SUB, cols] = total
    move.wait()


def gate_kernel(
    piece, post_ref, near_ref, starts_ref, table_ref, rates_ref, carry_ref, weight_ref,
    gated_ref, first_ref, states_ref,
):
    height, width = gated_ref.shape
    modes = rates_ref.shape[0]
    subs = height // SUB
    base = piece * height
    rates = rates_ref[...]
    fade = jnp.exp(rates * (-float(SUB)))
    state = carry_ref[...]
    if piece:
        state = state * jnp.exp(rates * (-float(base)))
    for sub in range(subs):
        states_ref[sub] = starts_ref[piece * subs + sub] + state
        state = state * fade
    for lane in range(0, width, LANES):
        cols = slice(lane, lane + LANES)
        totals = [near_ref[base + sub * SUB : base + (sub + 1) * SUB, cols] for sub in range(subs)]
        for mode in range(modes):
            entry = table_ref[mode, :, cols]
            totals = [
                total + entry * states_ref[sub, mode : mode + 1, cols] for sub, total in enumerate(totals)
            ]
        for sub in range(0, subs, 2):
            rows = slice(base + sub * SUB, base + (sub + 2) * SUB)
            total = jnp.concatenate(totals[sub : sub + 2], axis=0)
            gated_ref[sub * SUB : (sub + 2) * SUB, cols] = (
                post_ref[rows, cols].astype(F32) * total
            ).astype(BF16)
    first_ref[...] = jnp.dot(gated_ref[...], weight_ref[...], preferred_element_type=F32).astype(BF16)


def project_kernel(order, pieces, *refs):
    gated_refs, weight_hbm, out_refs = refs[:pieces], refs[pieces], refs[pieces + 1 : -3]
    gated_ref, held_ref, sems = refs[-3:]
    columns = held_ref.shape[2]
    me = lax.axis_index("chan")
    moves = []
    for slot, offset in enumerate(order):
        start = pl.multiple_of((me ^ offset) * columns, LANES)
        moves.append(
            pltpu.make_async_copy(
                weight_hbm.at[:, pl.ds(start, columns)], held_ref.at[slot], sems.at[slot]
            )
        )
    for move in moves:
        move.start()
    height = gated_refs[0].shape[0]
    for piece in range(pieces):
        gated_ref[piece * height : (piece + 1) * height, :] = gated_refs[piece][...]
    for slot, move in enumerate(moves):
        move.wait()
        product = jnp.dot(gated_ref[...], held_ref[slot], preferred_element_type=F32)
        for piece in range(pieces):
            out_ref = out_refs[slot * pieces + piece]
            out_ref[...] = product[piece * height : (piece + 1) * height, :].astype(out_ref.dtype)


def radices(size):
    factors = []
    while size > 1:
        factor = 2 if not factors or size % 4 else 4
        factors.append(factor)
        size //= factor
    return factors


def carried_state(total, rates, rows):
    size = lax.axis_size("seq")
    me = lax.axis_index("seq")
    carry = jnp.zeros_like(total)
    stride = 1
    for factor in radices(size):
        digit = (me // stride) % factor
        place = me % stride
        last = stride * factor == size
        joined = total * jnp.exp(-rates * (rows * stride * (factor - 1 - digit)).astype(F32))
        for hop in range(1, factor):
            pairs = []
            for source in range(size):
                target_digit = (source // stride) % factor + hop
                if target_digit < factor:
                    pairs.append((source, source + hop * stride))
                elif not last:
                    pairs.append((source, source + (hop - factor) * stride))
            arrived = lax.ppermute(total, "seq", pairs)
            origin = (digit - hop) % factor
            blocks = place + stride * (digit - 1 - origin)
            before = origin < digit
            entering = arrived * jnp.exp(-rates * (rows * jnp.maximum(blocks, 0)).astype(F32))
            carry = carry + jnp.where(before, entering, 0.0)
            if not last:
                joined = joined + arrived * jnp.exp(
                    -rates * (rows * stride * (factor - 1 - origin)).astype(F32)
                )
        total = joined
        stride *= factor
    return carry


def body(post_gate, pre_gate, signal, decay_rates, residues, skip_gain, out_weight):
    rows, width = post_gate.shape
    modes = decay_rates.shape[1]
    subs = rows // SUB
    groups = lax.axis_size("chan")
    columns = out_weight.shape[1] // groups
    height = rows // PIECES
    mixed, starts, end, rates, residues, skip, post = call(
        state_kernel,
        [HBM] * 6,
        [
            ((rows, width), F32),
            ((subs, modes, width), F32),
            ((modes, width), F32),
            ((modes, width), F32),
            ((modes, width), F32),
            ((1, width), F32),
            ((rows, width), BF16),
        ],
        [pltpu.VMEM((rows, width), BF16), pltpu.VMEM((rows, width), BF16), DMA((6,))],
        4 * rows * modes * width,
        8 * rows * width,
    )(pre_gate, signal, decay_rates.T, residues.T, skip_gain.reshape(1, width), post_gate)
    near, table, weight = call(
        near_kernel,
        [VMEM] * 4 + [HBM],
        [((rows, width), F32), ((modes, SUB, width), F32), ((width, columns), BF16)],
        [DMA],
        2 * rows * SUB * width,
        8 * rows * width,
    )(mixed, rates, residues, skip, out_weight)
    carry = carried_state(end, rates, rows)
    gated, values = [], {groups - 1: []}
    for piece in range(PIECES):
        half, first = call(
            functools.partial(gate_kernel, piece),
            [VMEM] * 7,
            [((height, width), BF16), ((height, columns), BF16)],
            [pltpu.VMEM((subs // PIECES, modes, width), F32)],
            2 * height * modes * width,
            16 * height * width,
        )(post, near, starts, table, rates, carry, weight)
        gated.append(half)
        values[groups - 1].append(first)
    order = list(range(groups - 2, -1, -1))
    others = call(
        functools.partial(project_kernel, order, PIECES),
        [VMEM] * PIECES + [HBM],
        [((height, columns), F32)] * (PIECES * len(order)),
        [
            pltpu.VMEM((rows, width), BF16),
            pltpu.VMEM((len(order), width, columns), BF16),
            DMA((len(order),)),
        ],
        2 * rows * width * columns * len(order),
        2 * width * columns * len(order),
    )(*gated, out_weight)
    for slot, offset in enumerate(order):
        values[offset] = list(others[slot * PIECES : (slot + 1) * PIECES])
    stride = 1
    while stride < groups:
        pairs = [(source, source ^ stride) for source in range(groups)]
        offsets = list(range(groups - stride, 0, -2 * stride))
        for place, offset in enumerate(offsets):
            for piece in range(PIECES):
                sent = values[offset][piece].astype(BF16)
                arrived = lax.ppermute(sent, "chan", pairs)
                if place + 1 < len(offsets):
                    later = offsets[place + 1]
                    arrived, values[later][piece] = lax.optimization_barrier(
                        (arrived, values[later][piece])
                    )
                values[offset ^ stride][piece] = values[offset ^ stride][piece] + arrived.astype(F32)
        stride *= 2
    return jnp.concatenate([value.astype(BF16) for value in values[0]], axis=0)


def solution(mesh):
    return jax.shard_map(
        body,
        mesh=mesh,
        in_specs=(
            P("seq", "chan"),
            P("seq", "chan"),
            P("seq", "chan"),
            P("chan", None),
            P("chan", None),
            P("chan"),
            P("chan", None),
        ),
        out_specs=P("seq", "chan"),
        check_vma=False,
    )
```

```python
import functools

import jax
import jax.numpy as jnp
from jax import lax
from jax.experimental import pallas as pl
from jax.experimental.pallas import tpu as pltpu
from jax.sharding import PartitionSpec as P

SUB = 8
LANES = 128
PIECES = 2
F32 = jnp.float32
BF16 = jnp.bfloat16
VMEM = pl.BlockSpec(memory_space=pltpu.VMEM)
HBM = pl.BlockSpec(memory_space=pltpu.HBM)
DMA = pltpu.SemaphoreType.DMA


def call(kernel, ins, outs, scratch, flops, moved):
    run = pl.pallas_call(
        kernel,
        in_specs=ins,
        out_shape=[jax.ShapeDtypeStruct(shape, kind) for shape, kind in outs],
        out_specs=[VMEM] * len(outs),
        scratch_shapes=scratch,
        compiler_params=pltpu.CompilerParams(vmem_limit_bytes=32 * 2**20),
        cost_estimate=pl.CostEstimate(flops=flops, bytes_accessed=moved, transcendentals=0),
    )
    return lambda *operands: run(
        *[
            pltpu.with_memory_space_constraint(operand, pltpu.HBM) if spec is HBM else operand
            for spec, operand in zip(ins, operands)
        ]
    )


def state_kernel(
    pre_hbm, signal_hbm, rates_hbm, residues_hbm, skip_hbm, post_hbm,
    mixed_ref, starts_ref, end_ref, rates_ref, residues_ref, skip_ref, post_ref,
    pre_ref, signal_ref, sems,
):
    moves = [
        pltpu.make_async_copy(source, target, sems.at[index])
        for index, (source, target) in enumerate(
            [
                (pre_hbm, pre_ref),
                (signal_hbm, signal_ref),
                (rates_hbm, rates_ref),
                (residues_hbm, residues_ref),
                (skip_hbm, skip_ref),
                (post_hbm, post_ref),
            ]
        )
    ]
    for move in moves:
        move.start()
    for move in moves[:3]:
        move.wait()
    mixed_ref[...] = pre_ref[...].astype(F32) * signal_ref[...].astype(F32)
    fade = jnp.exp(-rates_ref[...])
    state = jnp.zeros(end_ref.shape, F32)
    for sub in range(starts_ref.shape[0]):
        starts_ref[sub] = state
        for token in range(sub * SUB, (sub + 1) * SUB):
            state = fade * state + mixed_ref[token : token + 1, :]
    end_ref[...] = state
    for move in moves[3:]:
        move.wait()


def fetch(weight_hbm, offsets, weight_refs, sems):
    moves = []
    for index, (offset, weight_ref) in enumerate(zip(offsets, weight_refs)):
        columns = weight_ref.shape[1]
        start = pl.multiple_of((lax.axis_index("chan") ^ offset) * columns, LANES)
        move = pltpu.make_async_copy(
            weight_hbm.at[:, pl.ds(start, columns)], weight_ref, sems.at[index]
        )
        move.start()
        moves.append(move)
    return moves


def table_kernel(offsets, rates_ref, residues_ref, skip_ref, weight_hbm, table_ref, taps_ref, *rest):
    moves = fetch(weight_hbm, offsets, rest[:-1], rest[-1])
    modes, width = rates_ref.shape
    steps = lax.broadcasted_iota(jnp.int32, (SUB, LANES), 0).astype(F32) + 1.0
    for lane in range(0, width, LANES):
        cols = slice(lane, lane + LANES)
        weights = residues_ref[:, cols] * jnp.sqrt(2.0 * rates_ref[:, cols])
        taps = jnp.zeros((SUB, LANES), F32)
        for mode in range(modes):
            entry = weights[mode : mode + 1, :] * jnp.exp(-rates_ref[mode : mode + 1, cols] * steps)
            table_ref[mode, :, cols] = entry
            taps = taps + entry
        first = jnp.sum(weights, axis=0, keepdims=True) + skip_ref[:, cols]
        taps_ref[:, cols] = jnp.concatenate([first, taps[: SUB - 1, :]], axis=0)
    for move in moves:
        move.wait()


def near_kernel(offsets, mixed_ref, taps_ref, weight_hbm, near_ref, *rest):
    moves = fetch(weight_hbm, offsets, rest[:-1], rest[-1])
    rows, width = mixed_ref.shape
    row_ids = lax.broadcasted_iota(jnp.int32, (SUB, LANES), 0)
    for lane in range(0, width, LANES):
        cols = slice(lane, lane + LANES)
        taps = taps_ref[:, cols]
        masked = [jnp.where(row_ids >= lag, taps[lag : lag + 1, :], 0.0) for lag in range(SUB)]
        for sub in range(0, rows, SUB):
            mixed = mixed_ref[sub : sub + SUB, cols]
            total = masked[0] * mixed
            for lag in range(1, SUB):
                total = total + masked[lag] * pltpu.roll(mixed, lag, 0)
            near_ref[sub : sub + SUB, cols] = total
    for move in moves:
        move.wait()


def gate_kernel(
    piece, post_ref, near_ref, starts_ref, table_ref, rates_ref, carry_ref, weight_ref,
    gated_ref, first_ref, states_ref,
):
    height, width = gated_ref.shape
    modes = rates_ref.shape[0]
    subs = height // SUB
    base = piece * height
    rates = rates_ref[...]
    fade = jnp.exp(rates * (-float(SUB)))
    state = carry_ref[...]
    if piece:
        state = state * jnp.exp(rates * (-float(base)))
    for sub in range(subs):
        states_ref[sub] = starts_ref[piece * subs + sub] + state
        state = state * fade
    for lane in range(0, width, LANES):
        cols = slice(lane, lane + LANES)
        totals = [near_ref[base + sub * SUB : base + (sub + 1) * SUB, cols] for sub in range(subs)]
        for mode in range(modes):
            entry = table_ref[mode, :, cols]
            totals = [
                total + entry * states_ref[sub, mode : mode + 1, cols] for sub, total in enumerate(totals)
            ]
        for sub in range(0, subs, 2):
            rows = slice(base + sub * SUB, base + (sub + 2) * SUB)
            total = jnp.concatenate(totals[sub : sub + 2], axis=0)
            gated_ref[sub * SUB : (sub + 2) * SUB, cols] = (
                post_ref[rows, cols].astype(F32) * total
            ).astype(BF16)
    first_ref[...] = jnp.dot(gated_ref[...], weight_ref[...], preferred_element_type=F32).astype(BF16)


def project_kernel(pieces, *refs):
    gated_refs, weight_ref, out_refs, gated_ref = refs[:pieces], refs[pieces], refs[pieces + 1 : -1], refs[-1]
    height = gated_refs[0].shape[0]
    for piece in range(pieces):
        gated_ref[piece * height : (piece + 1) * height, :] = gated_refs[piece][...]
    product = jnp.dot(gated_ref[...], weight_ref[...], preferred_element_type=F32)
    for piece in range(pieces):
        out_refs[piece][...] = product[piece * height : (piece + 1) * height, :].astype(out_refs[piece].dtype)


def fetch_kernel(offsets, weight_hbm, *rest):
    for move in fetch(weight_hbm, offsets, rest[:-1], rest[-1]):
        move.wait()


def carried_state(total, rates, rows, beside):
    size = lax.axis_size("seq")
    me = lax.axis_index("seq")
    carry = jnp.zeros_like(total)
    stride = 1
    while stride < size:
        upper = (me & stride) > 0
        place = me & (stride - 1)
        sent = total if stride == 1 else total.astype(BF16)
        pairs = [(source, source ^ stride) for source in range(size)]
        arrived = lax.ppermute(sent, "seq", pairs)
        if beside:
            arrived = after(arrived, beside.pop(0))
        arrived = arrived.astype(F32)
        entering = arrived * jnp.exp(-rates * (rows * place).astype(F32))
        carry = carry + jnp.where(upper, entering, 0.0)
        fade = jnp.exp(-rates * float(rows * stride))
        total = jnp.where(upper, total, arrived) + fade * jnp.where(upper, arrived, total)
        stride *= 2
    return carry


def after(value, earlier):
    return lax.optimization_barrier((value, earlier))[0]


def body(post_gate, pre_gate, signal, decay_rates, residues, skip_gain, out_weight):
    rows, width = post_gate.shape
    modes = decay_rates.shape[1]
    subs = rows // SUB
    groups = lax.axis_size("chan")
    columns = out_weight.shape[1] // groups
    height = rows // PIECES
    block = ((width, columns), BF16)
    mixed, starts, end, rates, residues, skip, post = call(
        state_kernel,
        [HBM] * 6,
        [
            ((rows, width), F32),
            ((subs, modes, width), F32),
            ((modes, width), F32),
            ((modes, width), F32),
            ((modes, width), F32),
            ((1, width), F32),
            ((rows, width), BF16),
        ],
        [pltpu.VMEM((rows, width), BF16), pltpu.VMEM((rows, width), BF16), DMA((6,))],
        4 * rows * modes * width,
        8 * rows * width,
    )(pre_gate, signal, decay_rates.T, residues.T, skip_gain.reshape(1, width), post_gate)
    weights = {}
    offsets = list(range(groups - 1, -1, -1))
    early, middle, late = offsets[:1], offsets[1:2], offsets[2:]
    table, taps, *blocks = call(
        functools.partial(table_kernel, early),
        [VMEM] * 3 + [HBM],
        [((modes, SUB, width), F32), ((SUB, width), F32)] + [block] * len(early),
        [DMA((len(early),))],
        2 * modes * SUB * width,
        2 * width * columns * len(early),
    )(rates, residues, skip, out_weight)
    weights.update(zip(early, blocks))
    near, *blocks = call(
        functools.partial(near_kernel, middle),
        [VMEM] * 2 + [HBM],
        [((rows, width), F32)] + [block] * len(middle),
        [DMA((len(middle),))],
        2 * rows * SUB * width,
        2 * width * columns * len(middle),
    )(mixed, taps, out_weight)
    weights.update(zip(middle, blocks))
    blocks = call(
        functools.partial(fetch_kernel, late),
        [HBM],
        [block] * len(late),
        [DMA((len(late),))],
        0,
        4 * width * columns * len(late),
    )(out_weight)
    weights.update(zip(late, blocks))
    carry = carried_state(end, rates, rows, [taps, near, blocks[0]])
    gated, values = [], {groups - 1: []}
    for piece in range(PIECES):
        half, first = call(
            functools.partial(gate_kernel, piece),
            [VMEM] * 7,
            [((height, width), BF16), ((height, columns), BF16)],
            [pltpu.VMEM((subs // PIECES, modes, width), F32)],
            2 * height * modes * width,
            16 * height * width,
        )(post, near, starts, table, rates, carry, weights[groups - 1])
        gated.append(half)
        values[groups - 1].append(first)
    for offset in offsets[1:]:
        shares = call(
            functools.partial(project_kernel, PIECES),
            [VMEM] * (PIECES + 1),
            [((height, columns), BF16 if offset % 2 else F32)] * PIECES,
            [pltpu.VMEM((rows, width), BF16)],
            2 * rows * width * columns,
            2 * width * columns,
        )(*gated, weights[offset])
        values[offset] = list(shares)
    stride = 1
    while stride < groups:
        pairs = [(source, source ^ stride) for source in range(groups)]
        before = None
        for offset in range(groups - stride, 0, -2 * stride):
            for piece in range(PIECES):
                sent = values[offset][piece].astype(BF16)
                if before is not None:
                    sent = after(sent, before[piece])
                arrived = lax.ppermute(sent, "chan", pairs).astype(F32)
                held = values[offset ^ stride][piece]
                if piece:
                    held = after(held, values[offset ^ stride][piece - 1])
                values[offset ^ stride][piece] = held + arrived
            before = [value.astype(BF16) for value in values[offset ^ stride]]
        stride *= 2
    return jnp.concatenate([value.astype(BF16) for value in values[0]], axis=0)


def solution(mesh):
    return jax.shard_map(
        body,
        mesh=mesh,
        in_specs=(
            P("seq", "chan"),
            P("seq", "chan"),
            P("seq", "chan"),
            P("chan", None),
            P("chan", None),
            P("chan"),
            P("chan", None),
        ),
        out_specs=P("seq", "chan"),
        check_vma=False,
    )
```

```python
import functools

import jax
import jax.numpy as jnp
from jax import lax
from jax.experimental import pallas as pl
from jax.experimental.pallas import tpu as pltpu
from jax.sharding import PartitionSpec as P

SUB = 8
LANES = 128
PIECES = 2
F32 = jnp.float32
BF16 = jnp.bfloat16
VMEM = pl.BlockSpec(memory_space=pltpu.VMEM)
HBM = pl.BlockSpec(memory_space=pltpu.HBM)
DMA = pltpu.SemaphoreType.DMA


def call(kernel, ins, outs, scratch, flops, moved):
    run = pl.pallas_call(
        kernel,
        in_specs=ins,
        out_shape=[jax.ShapeDtypeStruct(shape, kind) for shape, kind in outs],
        out_specs=[VMEM] * len(outs),
        scratch_shapes=scratch,
        compiler_params=pltpu.CompilerParams(vmem_limit_bytes=24 * 2**20),
        cost_estimate=pl.CostEstimate(flops=flops, bytes_accessed=moved, transcendentals=0),
    )
    return lambda *operands: run(
        *[
            pltpu.with_memory_space_constraint(operand, pltpu.HBM) if spec is HBM else operand
            for spec, operand in zip(ins, operands)
        ]
    )


def state_kernel(
    pre_hbm, signal_hbm, rates_hbm, residues_hbm, skip_hbm, post_hbm,
    mixed_ref, starts_ref, end_ref, rates_ref, residues_ref, skip_ref, post_ref,
    pre_ref, signal_ref, sems,
):
    moves = [
        pltpu.make_async_copy(source, target, sems.at[index])
        for index, (source, target) in enumerate(
            [
                (pre_hbm, pre_ref),
                (signal_hbm, signal_ref),
                (rates_hbm, rates_ref),
                (residues_hbm, residues_ref),
                (skip_hbm, skip_ref),
                (post_hbm, post_ref),
            ]
        )
    ]
    for move in moves:
        move.start()
    for move in moves[:3]:
        move.wait()
    mixed_ref[...] = pre_ref[...].astype(F32) * signal_ref[...].astype(F32)
    fade = jnp.exp(-rates_ref[...])
    state = jnp.zeros(end_ref.shape, F32)
    for sub in range(starts_ref.shape[0]):
        starts_ref[sub] = state
        for token in range(sub * SUB, (sub + 1) * SUB):
            state = fade * state + mixed_ref[token : token + 1, :]
    end_ref[...] = state
    for move in moves[3:]:
        move.wait()


def fetch(weight_hbm, offsets, weight_refs, sems):
    moves = []
    for index, (offset, weight_ref) in enumerate(zip(offsets, weight_refs)):
        columns = weight_ref.shape[1]
        start = pl.multiple_of((lax.axis_index("chan") ^ offset) * columns, LANES)
        move = pltpu.make_async_copy(
            weight_hbm.at[:, pl.ds(start, columns)], weight_ref, sems.at[index]
        )
        move.start()
        moves.append(move)
    return moves


def table_kernel(offsets, rates_ref, residues_ref, skip_ref, weight_hbm, table_ref, taps_ref, *rest):
    moves = fetch(weight_hbm, offsets, rest[:-1], rest[-1])
    modes, width = rates_ref.shape
    steps = lax.broadcasted_iota(jnp.int32, (SUB, LANES), 0).astype(F32) + 1.0
    for lane in range(0, width, LANES):
        cols = slice(lane, lane + LANES)
        weights = residues_ref[:, cols] * jnp.sqrt(2.0 * rates_ref[:, cols])
        taps = jnp.zeros((SUB, LANES), F32)
        for mode in range(modes):
            entry = weights[mode : mode + 1, :] * jnp.exp(-rates_ref[mode : mode + 1, cols] * steps)
            table_ref[mode, :, cols] = entry
            taps = taps + entry
        first = jnp.sum(weights, axis=0, keepdims=True) + skip_ref[:, cols]
        taps_ref[:, cols] = jnp.concatenate([first, taps[: SUB - 1, :]], axis=0)
    for move in moves:
        move.wait()


def near_kernel(offsets, mixed_ref, taps_ref, weight_hbm, near_ref, *rest):
    moves = fetch(weight_hbm, offsets, rest[:-1], rest[-1])
    rows, width = mixed_ref.shape
    row_ids = lax.broadcasted_iota(jnp.int32, (SUB, LANES), 0)
    for lane in range(0, width, LANES):
        cols = slice(lane, lane + LANES)
        taps = taps_ref[:, cols]
        masked = [jnp.where(row_ids >= lag, taps[lag : lag + 1, :], 0.0) for lag in range(SUB)]
        for sub in range(0, rows, SUB):
            mixed = mixed_ref[sub : sub + SUB, cols]
            total = masked[0] * mixed
            for lag in range(1, SUB):
                total = total + masked[lag] * pltpu.roll(mixed, lag, 0)
            near_ref[sub : sub + SUB, cols] = total
    for move in moves:
        move.wait()


def gate_kernel(
    piece, last, post_ref, near_ref, starts_ref, table_ref, rates_ref, carry_ref, arrived_ref, weight_ref,
    gated_ref, first_ref, states_ref,
):
    height, width = gated_ref.shape
    modes = rates_ref.shape[0]
    subs = height // SUB
    base = piece * height
    rates = rates_ref[...]
    fade = jnp.exp(rates * (-float(SUB)))
    state = carry_ref[...] + entering(last, arrived_ref, rates, post_ref.shape[0])
    if piece:
        state = state * jnp.exp(rates * (-float(base)))
    for sub in range(subs):
        states_ref[sub] = starts_ref[piece * subs + sub] + state
        state = state * fade
    for lane in range(0, width, LANES):
        cols = slice(lane, lane + LANES)
        totals = [near_ref[base + sub * SUB : base + (sub + 1) * SUB, cols] for sub in range(subs)]
        for mode in range(modes):
            entry = table_ref[mode, :, cols]
            totals = [
                total + entry * states_ref[sub, mode : mode + 1, cols] for sub, total in enumerate(totals)
            ]
        for sub in range(0, subs, 2):
            rows = slice(base + sub * SUB, base + (sub + 2) * SUB)
            total = jnp.concatenate(totals[sub : sub + 2], axis=0)
            gated_ref[sub * SUB : (sub + 2) * SUB, cols] = (
                post_ref[rows, cols].astype(F32) * total
            ).astype(BF16)
    first_ref[...] = jnp.dot(gated_ref[...], weight_ref[...], preferred_element_type=F32).astype(BF16)


def project_kernel(pieces, *refs):
    gated_refs, weight_ref, out_refs, gated_ref = refs[:pieces], refs[pieces], refs[pieces + 1 : -1], refs[-1]
    height = gated_refs[0].shape[0]
    for piece in range(pieces):
        gated_ref[piece * height : (piece + 1) * height, :] = gated_refs[piece][...]
    product = jnp.dot(gated_ref[...], weight_ref[...], preferred_element_type=F32)
    for piece in range(pieces):
        out_refs[piece][...] = product[piece * height : (piece + 1) * height, :].astype(out_refs[piece].dtype)


def fetch_kernel(offsets, weight_hbm, *rest):
    for move in fetch(weight_hbm, offsets, rest[:-1], rest[-1]):
        move.wait()


def entering(stride, arrived_ref, rates, rows):
    me = lax.axis_index("seq")
    place = me & (stride - 1)
    fade = jnp.exp(-rates * (rows * place).astype(F32))
    return jnp.where((me & stride) > 0, fade, 0.0) * arrived_ref[...].astype(F32)


def join_kernel(stride, rows, *refs):
    total_ref, arrived_ref, rates_ref, *before, joined_ref, sent_ref, carry_ref = refs
    rates = rates_ref[...]
    carry = entering(stride, arrived_ref, rates, rows)
    for carried_ref in before:
        carry = carry + carried_ref[...]
    carry_ref[...] = carry
    total = total_ref[...]
    arrived = arrived_ref[...].astype(F32)
    upper = (lax.axis_index("seq") & stride) > 0
    fade = jnp.exp(-rates * float(rows * stride))
    joined = jnp.where(upper, total, arrived) + fade * jnp.where(upper, arrived, total)
    joined_ref[...] = joined
    sent_ref[...] = joined.astype(BF16)


def carried_state(total, rates, rows, beside):
    size = lax.axis_size("seq")
    shape = total.shape
    sent, before, stride = total, [], 1
    while True:
        pairs = [(source, source ^ stride) for source in range(size)]
        arrived = lax.ppermute(sent, "seq", pairs)
        if beside:
            arrived = after(arrived, beside.pop(0))
        if 2 * stride >= size:
            return before[0], arrived, stride
        total, sent, carry = call(
            functools.partial(join_kernel, stride, rows),
            [VMEM] * (3 + len(before)),
            [(shape, F32), (shape, BF16), (shape, F32)],
            [],
            8 * total.size,
            16 * total.size,
        )(total, arrived, rates, *before)
        before, stride = [carry], 2 * stride


def after(value, earlier):
    return lax.optimization_barrier((value, earlier))[0]


def body(post_gate, pre_gate, signal, decay_rates, residues, skip_gain, out_weight):
    rows, width = post_gate.shape
    modes = decay_rates.shape[1]
    subs = rows // SUB
    groups = lax.axis_size("chan")
    columns = out_weight.shape[1] // groups
    height = rows // PIECES
    block = ((width, columns), BF16)
    mixed, starts, end, rates, residues, skip, post = call(
        state_kernel,
        [HBM] * 6,
        [
            ((rows, width), F32),
            ((subs, modes, width), F32),
            ((modes, width), F32),
            ((modes, width), F32),
            ((modes, width), F32),
            ((1, width), F32),
            ((rows, width), BF16),
        ],
        [pltpu.VMEM((rows, width), BF16), pltpu.VMEM((rows, width), BF16), DMA((6,))],
        4 * rows * modes * width,
        8 * rows * width,
    )(pre_gate, signal, decay_rates.T, residues.T, skip_gain.reshape(1, width), post_gate)
    weights = {}
    offsets = list(range(groups - 1, -1, -1))
    early, middle, late = offsets[:1], offsets[1:2], offsets[2:]
    table, taps, *blocks = call(
        functools.partial(table_kernel, early),
        [VMEM] * 3 + [HBM],
        [((modes, SUB, width), F32), ((SUB, width), F32)] + [block] * len(early),
        [DMA((len(early),))],
        2 * modes * SUB * width,
        2 * width * columns * len(early),
    )(rates, residues, skip, out_weight)
    weights.update(zip(early, blocks))
    near, *blocks = call(
        functools.partial(near_kernel, middle),
        [VMEM] * 2 + [HBM],
        [((rows, width), F32)] + [block] * len(middle),
        [DMA((len(middle),))],
        2 * rows * SUB * width,
        2 * width * columns * len(middle),
    )(mixed, taps, out_weight)
    weights.update(zip(middle, blocks))
    blocks = call(
        functools.partial(fetch_kernel, late),
        [HBM],
        [block] * len(late),
        [DMA((len(late),))],
        0,
        4 * width * columns * len(late),
    )(out_weight)
    weights.update(zip(late, blocks))
    carry, arrived, last = carried_state(end, rates, rows, [taps, near, blocks[0]])
    gated, values = [], {groups - 1: []}
    for piece in range(PIECES):
        half, first = call(
            functools.partial(gate_kernel, piece, last),
            [VMEM] * 8,
            [((height, width), BF16), ((height, columns), BF16)],
            [pltpu.VMEM((subs // PIECES, modes, width), F32)],
            2 * height * modes * width,
            16 * height * width,
        )(post, near, starts, table, rates, carry, arrived, weights[groups - 1])
        gated.append(half)
        values[groups - 1].append(first)
    for offset in offsets[1:]:
        shares = call(
            functools.partial(project_kernel, PIECES),
            [VMEM] * (PIECES + 1),
            [((height, columns), BF16 if offset % 2 else F32)] * PIECES,
            [pltpu.VMEM((rows, width), BF16)],
            2 * rows * width * columns,
            2 * width * columns,
        )(*gated, weights[offset])
        values[offset] = list(shares)
    stride = 1
    while stride < groups:
        pairs = [(source, source ^ stride) for source in range(groups)]
        before = None
        for offset in range(groups - stride, 0, -2 * stride):
            for piece in range(PIECES):
                sent = values[offset][piece].astype(BF16)
                if before is not None:
                    sent = after(sent, before[piece])
                arrived = lax.ppermute(sent, "chan", pairs).astype(F32)
                held = values[offset ^ stride][piece]
                if piece:
                    held = after(held, values[offset ^ stride][piece - 1])
                values[offset ^ stride][piece] = held + arrived
            before = [value.astype(BF16) for value in values[offset ^ stride]]
        stride *= 2
    return jnp.concatenate([value.astype(BF16) for value in values[0]], axis=0)


def solution(mesh):
    return jax.shard_map(
        body,
        mesh=mesh,
        in_specs=(
            P("seq", "chan"),
            P("seq", "chan"),
            P("seq", "chan"),
            P("chan", None),
            P("chan", None),
            P("chan"),
            P("chan", None),
        ),
        out_specs=P("seq", "chan"),
        check_vma=False,
    )
```

```python
import functools

import jax
import jax.numpy as jnp
from jax import lax
from jax.experimental import pallas as pl
from jax.experimental.pallas import tpu as pltpu
from jax.sharding import PartitionSpec as P

SUB = 8
LANES = 128
PIECES = 2
F32 = jnp.float32
BF16 = jnp.bfloat16
VMEM = pl.BlockSpec(memory_space=pltpu.VMEM)
HBM = pl.BlockSpec(memory_space=pltpu.HBM)
DMA = pltpu.SemaphoreType.DMA


def call(kernel, ins, outs, scratch, flops, moved):
    run = pl.pallas_call(
        kernel,
        in_specs=ins,
        out_shape=[jax.ShapeDtypeStruct(shape, kind) for shape, kind in outs],
        out_specs=[VMEM] * len(outs),
        scratch_shapes=scratch,
        compiler_params=pltpu.CompilerParams(vmem_limit_bytes=24 * 2**20),
        cost_estimate=pl.CostEstimate(flops=flops, bytes_accessed=moved, transcendentals=0),
    )
    return lambda *operands: run(
        *[
            pltpu.with_memory_space_constraint(operand, pltpu.HBM) if spec is HBM else operand
            for spec, operand in zip(ins, operands)
        ]
    )


def fetch(weight_hbm, offsets, weight_refs, sems):
    moves = []
    for index, (offset, weight_ref) in enumerate(zip(offsets, weight_refs)):
        columns = weight_ref.shape[1]
        start = pl.multiple_of((lax.axis_index("chan") ^ offset) * columns, LANES)
        move = pltpu.make_async_copy(
            weight_hbm.at[:, pl.ds(start, columns)], weight_ref, sems.at[index]
        )
        move.start()
        moves.append(move)
    return moves


def state_kernel(
    offsets, pre_hbm, signal_hbm, rates_hbm, residues_hbm, skip_hbm, post_hbm, weight_hbm,
    mixed_ref, starts_ref, ends_ref, rates_ref, residues_ref, skip_ref, post_ref, *rest,
):
    *weight_refs, pre_ref, signal_ref, sems, weight_sems = rest
    moves = [
        pltpu.make_async_copy(source, target, sems.at[index])
        for index, (source, target) in enumerate(
            [
                (pre_hbm, pre_ref),
                (signal_hbm, signal_ref),
                (rates_hbm, rates_ref),
                (residues_hbm, residues_ref),
                (skip_hbm, skip_ref),
                (post_hbm, post_ref),
            ]
        )
    ]
    for move in moves:
        move.start()
    moves += fetch(weight_hbm, offsets, weight_refs, weight_sems)
    for move in moves[:3]:
        move.wait()
    mixed_ref[...] = pre_ref[...].astype(F32) * signal_ref[...].astype(F32)
    fade = jnp.exp(-rates_ref[...])
    state = jnp.zeros(rates_ref.shape, F32)
    for sub in range(starts_ref.shape[0]):
        starts_ref[sub] = state
        for token in range(sub * SUB, (sub + 1) * SUB):
            state = fade * state + mixed_ref[token : token + 1, :]
    for block in range(ends_ref.shape[0]):
        ends_ref[block] = state.astype(BF16)
    for move in moves[3:]:
        move.wait()


def table_kernel(rates_ref, residues_ref, skip_ref, table_ref, taps_ref):
    modes, width = rates_ref.shape
    steps = lax.broadcasted_iota(jnp.int32, (SUB, LANES), 0).astype(F32) + 1.0
    for lane in range(0, width, LANES):
        cols = slice(lane, lane + LANES)
        weights = residues_ref[:, cols] * jnp.sqrt(2.0 * rates_ref[:, cols])
        taps = jnp.zeros((SUB, LANES), F32)
        for mode in range(modes):
            entry = weights[mode : mode + 1, :] * jnp.exp(-rates_ref[mode : mode + 1, cols] * steps)
            table_ref[mode, :, cols] = entry
            taps = taps + entry
        first = jnp.sum(weights, axis=0, keepdims=True) + skip_ref[:, cols]
        taps_ref[:, cols] = jnp.concatenate([first, taps[: SUB - 1, :]], axis=0)


def near_kernel(offsets, mixed_ref, taps_ref, weight_hbm, near_ref, *rest):
    moves = fetch(weight_hbm, offsets, rest[:-1], rest[-1])
    rows, width = mixed_ref.shape
    row_ids = lax.broadcasted_iota(jnp.int32, (SUB, LANES), 0)
    for lane in range(0, width, LANES):
        cols = slice(lane, lane + LANES)
        taps = taps_ref[:, cols]
        masked = [jnp.where(row_ids >= lag, taps[lag : lag + 1, :], 0.0) for lag in range(SUB)]
        for sub in range(0, rows, SUB):
            mixed = mixed_ref[sub : sub + SUB, cols]
            total = masked[0] * mixed
            for lag in range(1, SUB):
                total = total + masked[lag] * pltpu.roll(mixed, lag, 0)
            near_ref[sub : sub + SUB, cols] = total
    for move in moves:
        move.wait()


def gate_kernel(
    piece, post_ref, near_ref, starts_ref, table_ref, rates_ref, ends_ref, weight_ref,
    gated_ref, first_ref, states_ref,
):
    height, width = gated_ref.shape
    modes = rates_ref.shape[0]
    subs = height // SUB
    base = piece * height
    rates = rates_ref[...]
    fade = jnp.exp(rates * (-float(SUB)))
    across = jnp.exp(rates * (-float(post_ref.shape[0])))
    state = jnp.zeros(rates.shape, F32)
    me = lax.axis_index("seq")
    for block in range(ends_ref.shape[0]):
        state = jnp.where(block < me, across * state + ends_ref[block].astype(F32), state)
    if piece:
        state = state * jnp.exp(rates * (-float(base)))
    for sub in range(subs):
        states_ref[sub] = starts_ref[piece * subs + sub] + state
        state = state * fade
    for lane in range(0, width, LANES):
        cols = slice(lane, lane + LANES)
        totals = [near_ref[base + sub * SUB : base + (sub + 1) * SUB, cols] for sub in range(subs)]
        for mode in range(modes):
            entry = table_ref[mode, :, cols]
            totals = [
                total + entry * states_ref[sub, mode : mode + 1, cols] for sub, total in enumerate(totals)
            ]
        for sub in range(0, subs, 2):
            rows = slice(base + sub * SUB, base + (sub + 2) * SUB)
            total = jnp.concatenate(totals[sub : sub + 2], axis=0)
            gated_ref[sub * SUB : (sub + 2) * SUB, cols] = (
                post_ref[rows, cols].astype(F32) * total
            ).astype(BF16)
    first_ref[...] = jnp.dot(gated_ref[...], weight_ref[...], preferred_element_type=F32).astype(BF16)


def project_kernel(pieces, offsets, *refs):
    gated_refs, weight_ref, out_refs = refs[:pieces], refs[pieces], refs[pieces + 1 : 2 * pieces + 1]
    gated_ref, *rest = refs[2 * pieces + 1 :]
    moves = fetch(weight_ref, offsets, rest[:-1], rest[-1]) if offsets else []
    weight_ref = rest[0] if offsets else weight_ref
    height = gated_refs[0].shape[0]
    for piece in range(pieces):
        gated_ref[piece * height : (piece + 1) * height, :] = gated_refs[piece][...]
    for move in moves:
        move.wait()
    product = jnp.dot(gated_ref[...], weight_ref[...], preferred_element_type=F32)
    for piece in range(pieces):
        out_refs[piece][...] = product[piece * height : (piece + 1) * height, :].astype(out_refs[piece].dtype)


def after(value, earlier):
    return lax.optimization_barrier((value, earlier))[0]


def body(post_gate, pre_gate, signal, decay_rates, residues, skip_gain, out_weight):
    rows, width = post_gate.shape
    modes = decay_rates.shape[1]
    subs = rows // SUB
    groups = lax.axis_size("chan")
    columns = out_weight.shape[1] // groups
    height = rows // PIECES
    block = ((width, columns), BF16)
    offsets = list(range(groups - 1, -1, -1))
    early, middle, late = offsets[:1], offsets[1:3], offsets[3:]
    mixed, starts, ends, rates, residues, skip, post, *blocks = call(
        functools.partial(state_kernel, early),
        [HBM] * 7,
        [
            ((rows, width), F32),
            ((subs, modes, width), F32),
            ((lax.axis_size("seq"), modes, width), BF16),
            ((modes, width), F32),
            ((modes, width), F32),
            ((1, width), F32),
            ((rows, width), BF16),
        ]
        + [block] * len(early),
        [
            pltpu.VMEM((rows, width), BF16),
            pltpu.VMEM((rows, width), BF16),
            DMA((6,)),
            DMA((len(early),)),
        ],
        4 * rows * modes * width,
        8 * rows * width,
    )(pre_gate, signal, decay_rates.T, residues.T, skip_gain.reshape(1, width), post_gate, out_weight)
    weights = dict(zip(early, blocks))
    ends = lax.all_to_all(ends, "seq", 0, 0)
    table, taps = call(
        table_kernel,
        [VMEM] * 3,
        [((modes, SUB, width), F32), ((SUB, width), F32)],
        [],
        2 * modes * SUB * width,
        8 * modes * SUB * width,
    )(rates, residues, skip)
    near, *blocks = call(
        functools.partial(near_kernel, middle),
        [VMEM] * 2 + [HBM],
        [((rows, width), F32)] + [block] * len(middle),
        [DMA((len(middle),))],
        2 * rows * SUB * width,
        2 * width * columns * len(middle),
    )(mixed, taps, out_weight)
    weights.update(zip(middle, blocks))
    ends = after(ends, near)
    gated, values = [], {groups - 1: []}
    for piece in range(PIECES):
        half, first = call(
            functools.partial(gate_kernel, piece),
            [VMEM] * 7,
            [((height, width), BF16), ((height, columns), BF16)],
            [pltpu.VMEM((subs // PIECES, modes, width), F32)],
            2 * height * modes * width,
            16 * height * width,
        )(post, near, starts, table, rates, ends, weights[groups - 1])
        gated.append(half)
        values[groups - 1].append(first)
    for offset in offsets[1:]:
        held = [offset] if offset in late else []
        shares = call(
            functools.partial(project_kernel, PIECES, held),
            [VMEM] * PIECES + [HBM if held else VMEM],
            [((height, columns), BF16 if offset % 2 else F32)] * PIECES,
            [pltpu.VMEM((rows, width), BF16)]
            + ([pltpu.VMEM((width, columns), BF16), DMA((1,))] if held else []),
            2 * rows * width * columns,
            2 * width * columns,
        )(*gated, out_weight if held else weights[offset])
        values[offset] = list(shares)
    stride = 1
    while stride < groups:
        pairs = [(source, source ^ stride) for source in range(groups)]
        before = None
        for offset in range(groups - stride, 0, -2 * stride):
            for piece in range(PIECES):
                sent = values[offset][piece].astype(BF16)
                if before is not None:
                    sent = after(sent, before[piece])
                arrived = lax.ppermute(sent, "chan", pairs).astype(F32)
                held = values[offset ^ stride][piece]
                if piece:
                    held = after(held, values[offset ^ stride][piece - 1])
                values[offset ^ stride][piece] = held + arrived
            before = [value.astype(BF16) for value in values[offset ^ stride]]
        stride *= 2
    return jnp.concatenate([value.astype(BF16) for value in values[0]], axis=0)


def solution(mesh):
    return jax.shard_map(
        body,
        mesh=mesh,
        in_specs=(
            P("seq", "chan"),
            P("seq", "chan"),
            P("seq", "chan"),
            P("chan", None),
            P("chan", None),
            P("chan"),
            P("chan", None),
        ),
        out_specs=P("seq", "chan"),
        check_vma=False,
    )
```

```python
import functools

import jax
import jax.numpy as jnp
from jax import lax
from jax.experimental import pallas as pl
from jax.experimental.pallas import tpu as pltpu
from jax.sharding import PartitionSpec as P

SUB = 8
LANES = 128
PIECES = 2
F32 = jnp.float32
BF16 = jnp.bfloat16
VMEM = pl.BlockSpec(memory_space=pltpu.VMEM)
HBM = pl.BlockSpec(memory_space=pltpu.HBM)
DMA = pltpu.SemaphoreType.DMA


def call(kernel, ins, outs, scratch, flops, moved):
    run = pl.pallas_call(
        kernel,
        in_specs=ins,
        out_shape=[jax.ShapeDtypeStruct(shape, kind) for shape, kind in outs],
        out_specs=[VMEM] * len(outs),
        scratch_shapes=scratch,
        compiler_params=pltpu.CompilerParams(vmem_limit_bytes=24 * 2**20),
        cost_estimate=pl.CostEstimate(flops=flops, bytes_accessed=moved, transcendentals=0),
    )
    return lambda *operands: run(
        *[
            pltpu.with_memory_space_constraint(operand, pltpu.HBM) if spec is HBM else operand
            for spec, operand in zip(ins, operands)
        ]
    )


def fetch(weight_hbm, offset, piece, weight_ref, sem):
    columns = weight_ref.shape[1]
    block = lax.axis_index("chan") ^ offset
    start = pl.multiple_of((block * PIECES + piece) * columns, LANES)
    move = pltpu.make_async_copy(weight_hbm.at[:, pl.ds(start, columns)], weight_ref, sem)
    move.start()
    return move


def state_kernel(
    pre_hbm, signal_hbm, rates_hbm, residues_hbm, skip_hbm, post_hbm,
    mixed_ref, starts_ref, ends_ref, rates_ref, residues_ref, skip_ref, post_ref,
    pre_ref, signal_ref, sems,
):
    moves = [
        pltpu.make_async_copy(source, target, sems.at[index])
        for index, (source, target) in enumerate(
            [
                (pre_hbm, pre_ref),
                (signal_hbm, signal_ref),
                (rates_hbm, rates_ref),
                (residues_hbm, residues_ref),
                (skip_hbm, skip_ref),
                (post_hbm, post_ref),
            ]
        )
    ]
    for move in moves:
        move.start()
    for move in moves[:3]:
        move.wait()
    mixed_ref[...] = pre_ref[...].astype(F32) * signal_ref[...].astype(F32)
    fade = jnp.exp(-rates_ref[...])
    state = jnp.zeros(rates_ref.shape, F32)
    for sub in range(starts_ref.shape[0]):
        starts_ref[sub] = state
        for token in range(sub * SUB, (sub + 1) * SUB):
            state = fade * state + mixed_ref[token : token + 1, :]
    for block in range(ends_ref.shape[0]):
        ends_ref[block] = state.astype(BF16)
    for move in moves[3:]:
        move.wait()


def local_kernel(
    offset, mixed_ref, starts_ref, rates_ref, residues_ref, skip_ref, weight_hbm,
    local_ref, table_ref, weight_ref,
    sem,
):
    move = fetch(weight_hbm, offset, 0, weight_ref, sem)
    rows, width = mixed_ref.shape
    modes = rates_ref.shape[0]
    row_ids = lax.broadcasted_iota(jnp.int32, (SUB, LANES), 0)
    steps = row_ids.astype(F32) + 1.0
    for lane in range(0, width, LANES):
        cols = slice(lane, lane + LANES)
        weights = residues_ref[:, cols] * jnp.sqrt(2.0 * rates_ref[:, cols])
        taps = jnp.zeros((SUB, LANES), F32)
        for mode in range(modes):
            entry = weights[mode : mode + 1, :] * jnp.exp(-rates_ref[mode : mode + 1, cols] * steps)
            table_ref[mode, :, cols] = entry
            taps = taps + entry
        first = jnp.sum(weights, axis=0, keepdims=True) + skip_ref[:, cols]
        masked = [jnp.where(row_ids >= lag, taps[lag - 1 : lag, :], 0.0) for lag in range(1, SUB)]
        totals = []
        for sub in range(0, rows, SUB):
            mixed = mixed_ref[sub : sub + SUB, cols]
            total = first * mixed
            for lag in range(1, SUB):
                total = total + masked[lag - 1] * pltpu.roll(mixed, lag, 0)
            totals.append(total)
        for mode in range(modes):
            entry = table_ref[mode, :, cols]
            totals = [
                total + entry * starts_ref[sub, mode : mode + 1, cols] if sub else total
                for sub, total in enumerate(totals)
            ]
        for sub, total in enumerate(totals):
            local_ref[sub * SUB : (sub + 1) * SUB, cols] = total
    move.wait()


def gate_kernel(
    offset, post_ref, local_ref, table_ref, rates_ref, ends_ref, weight_ref, weight_hbm,
    gated_ref, first_ref, next_ref,
    states_ref, sem,
):
    move = fetch(weight_hbm, offset, 1, next_ref, sem)
    rows, width = gated_ref.shape
    modes = rates_ref.shape[0]
    subs = rows // SUB
    rates = rates_ref[...]
    across = jnp.exp(rates * (-float(rows)))
    state = jnp.zeros(rates.shape, F32)
    me = lax.axis_index("seq")
    for block in range(ends_ref.shape[0]):
        state = jnp.where(block < me, across * state + ends_ref[block].astype(F32), state)
    fade = jnp.exp(rates * (-float(SUB)))
    for sub in range(subs):
        states_ref[sub] = state
        state = state * fade
    for lane in range(0, width, LANES):
        cols = slice(lane, lane + LANES)
        totals = [local_ref[sub * SUB : (sub + 1) * SUB, cols] for sub in range(subs)]
        for mode in range(modes):
            entry = table_ref[mode, :, cols]
            totals = [
                total + entry * states_ref[sub, mode : mode + 1, cols] for sub, total in enumerate(totals)
            ]
        for sub in range(0, subs, 2):
            part = slice(sub * SUB, (sub + 2) * SUB)
            total = jnp.concatenate(totals[sub : sub + 2], axis=0)
            gated_ref[part, cols] = (post_ref[part, cols].astype(F32) * total).astype(BF16)
    first_ref[...] = jnp.dot(gated_ref[...], weight_ref[...], preferred_element_type=F32).astype(BF16)
    move.wait()


def held_project_kernel(gated_ref, weight_ref, out_ref):
    out_ref[...] = jnp.dot(
        gated_ref[...], weight_ref[...], preferred_element_type=F32
    ).astype(out_ref.dtype)


def project_kernel(offset, gated_ref, weight_hbm, *refs):
    out_refs, weight_ref, sems = refs[:PIECES], refs[PIECES], refs[PIECES + 1]
    moves = [
        fetch(weight_hbm, offset, piece, weight_ref.at[piece], sems.at[piece]) for piece in range(PIECES)
    ]
    for piece, move in enumerate(moves):
        move.wait()
        held_project_kernel(gated_ref, weight_ref.at[piece], out_refs[piece])


def after(value, earlier):
    return lax.optimization_barrier((value, earlier))[0]


def body(post_gate, pre_gate, signal, decay_rates, residues, skip_gain, out_weight):
    rows, width = post_gate.shape
    modes = decay_rates.shape[1]
    subs = rows // SUB
    groups = lax.axis_size("chan")
    columns = out_weight.shape[1] // groups // PIECES
    held = ((width, columns), BF16)
    mixed, starts, ends, rates, residues, skip, post = call(
        state_kernel,
        [HBM] * 6,
        [
            ((rows, width), F32),
            ((subs, modes, width), F32),
            ((lax.axis_size("seq"), modes, width), BF16),
            ((modes, width), F32),
            ((modes, width), F32),
            ((1, width), F32),
            ((rows, width), BF16),
        ],
        [pltpu.VMEM((rows, width), BF16), pltpu.VMEM((rows, width), BF16), DMA((6,))],
        4 * rows * modes * width,
        8 * rows * width,
    )(pre_gate, signal, decay_rates.T, residues.T, skip_gain.reshape(1, width), post_gate)
    ends = lax.all_to_all(ends, "seq", 0, 0)
    local, table, weight = call(
        functools.partial(local_kernel, groups - 1),
        [VMEM] * 5 + [HBM],
        [((rows, width), F32), ((modes, SUB, width), F32), held],
        [DMA],
        2 * rows * (SUB + modes) * width,
        2 * width * columns,
    )(mixed, starts, rates, residues, skip, out_weight)
    ends = after(ends, local)
    gated, first, weight = call(
        functools.partial(gate_kernel, groups - 1),
        [VMEM] * 6 + [HBM],
        [((rows, width), BF16), ((rows, columns), BF16), held],
        [pltpu.VMEM((subs, modes, width), F32), DMA],
        2 * rows * modes * width,
        16 * rows * width,
    )(post, local, table, rates, ends, weight, out_weight)
    (second,) = call(
        held_project_kernel,
        [VMEM] * 2,
        [((rows, columns), BF16)],
        [],
        2 * rows * width * columns,
        2 * width * columns,
    )(gated, weight)

    def project(offset, earlier=None):
        return list(
            call(
                functools.partial(project_kernel, offset),
                [VMEM, HBM],
                [((rows, columns), BF16 if offset % 2 else F32)] * PIECES,
                [pltpu.VMEM((PIECES, width, columns), BF16), DMA((PIECES,))],
                2 * rows * width * columns * PIECES,
                2 * width * columns * PIECES,
            )(gated if earlier is None else after(gated, earlier), out_weight)
        )

    values = {groups - 1: [first, second]}
    stride = 1
    while stride < groups:
        pairs = [(source, source ^ stride) for source in range(groups)]
        before = [None] * PIECES
        for offset in range(groups - stride, 0, -2 * stride):
            if offset not in values:
                values[offset] = project(offset, before[0])
            if offset ^ stride not in values:
                values[offset ^ stride] = project(offset ^ stride, before[-1])
            for piece in range(PIECES):
                sent = values[offset][piece].astype(BF16)
                if before[piece] is not None:
                    sent = after(sent, before[piece])
                arrived = lax.ppermute(sent, "chan", pairs).astype(F32)
                kept = values[offset ^ stride][piece]
                if piece:
                    kept = after(kept, values[offset ^ stride][piece - 1])
                values[offset ^ stride][piece] = kept + arrived
            before = [value.astype(BF16) for value in values[offset ^ stride]]
        stride *= 2
    return jnp.concatenate([value.astype(BF16) for value in values[0]], axis=1)


def solution(mesh):
    return jax.shard_map(
        body,
        mesh=mesh,
        in_specs=(
            P("seq", "chan"),
            P("seq", "chan"),
            P("seq", "chan"),
            P("chan", None),
            P("chan", None),
            P("chan"),
            P("chan", None),
        ),
        out_specs=P("seq", "chan"),
        check_vma=False,
    )
```

```python
import functools

import jax
import jax.numpy as jnp
from jax import lax
from jax.experimental import pallas as pl
from jax.experimental.pallas import tpu as pltpu
from jax.sharding import PartitionSpec as P

SUB = 8
LANES = 128
PIECES = 2
IN_FLIGHT = 3
F32 = jnp.float32
BF16 = jnp.bfloat16
VMEM = pl.BlockSpec(memory_space=pltpu.VMEM)
HBM = pl.BlockSpec(memory_space=pltpu.HBM)
DMA = pltpu.SemaphoreType.DMA


def call(kernel, ins, outs, scratch, flops, moved):
    run = pl.pallas_call(
        kernel,
        in_specs=ins,
        out_shape=[jax.ShapeDtypeStruct(shape, kind) for shape, kind in outs],
        out_specs=[VMEM] * len(outs),
        scratch_shapes=scratch,
        compiler_params=pltpu.CompilerParams(vmem_limit_bytes=24 * 2**20),
        cost_estimate=pl.CostEstimate(flops=flops, bytes_accessed=moved, transcendentals=0),
    )
    return lambda *operands: run(
        *[
            pltpu.with_memory_space_constraint(operand, pltpu.HBM) if spec is HBM else operand
            for spec, operand in zip(ins, operands)
        ]
    )


def fetch(weight_hbm, offset, weight_ref, sem):
    columns = weight_ref.shape[1]
    start = pl.multiple_of((lax.axis_index("chan") ^ offset) * columns, LANES)
    move = pltpu.make_async_copy(weight_hbm.at[:, pl.ds(start, columns)], weight_ref, sem)
    move.start()
    return move


def state_kernel(
    offset, pre_hbm, signal_hbm, rates_hbm, residues_hbm, skip_hbm, post_hbm, weight_hbm,
    mixed_ref, starts_ref, end_ref, rates_ref, residues_ref, skip_ref, post_ref, weight_ref,
    pre_ref, signal_ref, sems, weight_sem,
):
    moves = [
        pltpu.make_async_copy(source, target, sems.at[index])
        for index, (source, target) in enumerate(
            [
                (pre_hbm, pre_ref),
                (signal_hbm, signal_ref),
                (rates_hbm, rates_ref),
                (residues_hbm, residues_ref),
                (skip_hbm, skip_ref),
                (post_hbm, post_ref),
            ]
        )
    ]
    for move in moves:
        move.start()
    moves.append(fetch(weight_hbm, offset, weight_ref, weight_sem))
    for move in moves[:3]:
        move.wait()
    mixed_ref[...] = pre_ref[...].astype(F32) * signal_ref[...].astype(F32)
    fade = jnp.exp(-rates_ref[...])
    state = jnp.zeros(rates_ref.shape, F32)
    for sub in range(starts_ref.shape[0]):
        starts_ref[sub] = state
        for token in range(sub * SUB, (sub + 1) * SUB):
            state = fade * state + mixed_ref[token : token + 1, :]
    end_ref[...] = state
    for move in moves[3:]:
        move.wait()


def local_kernel(mixed_ref, starts_ref, rates_ref, residues_ref, skip_ref, local_ref, table_ref):
    rows, width = mixed_ref.shape
    modes = rates_ref.shape[0]
    row_ids = lax.broadcasted_iota(jnp.int32, (SUB, LANES), 0)
    steps = row_ids.astype(F32) + 1.0
    for lane in range(0, width, LANES):
        cols = slice(lane, lane + LANES)
        weights = residues_ref[:, cols] * jnp.sqrt(2.0 * rates_ref[:, cols])
        taps = jnp.zeros((SUB, LANES), F32)
        for mode in range(modes):
            entry = weights[mode : mode + 1, :] * jnp.exp(-rates_ref[mode : mode + 1, cols] * steps)
            table_ref[mode, :, cols] = entry
            taps = taps + entry
        first = jnp.sum(weights, axis=0, keepdims=True) + skip_ref[:, cols]
        masked = [jnp.where(row_ids >= lag, taps[lag - 1 : lag, :], 0.0) for lag in range(1, SUB)]
        totals = []
        for sub in range(0, rows, SUB):
            mixed = mixed_ref[sub : sub + SUB, cols]
            total = first * mixed
            for lag in range(1, SUB):
                total = total + masked[lag - 1] * pltpu.roll(mixed, lag, 0)
            totals.append(total)
        for mode in range(modes):
            entry = table_ref[mode, :, cols]
            totals = [
                total + entry * starts_ref[sub, mode : mode + 1, cols] if sub else total
                for sub, total in enumerate(totals)
            ]
        for sub, total in enumerate(totals):
            local_ref[sub * SUB : (sub + 1) * SUB, cols] = total


def fetch_kernel(offsets, weight_hbm, *refs):
    weight_refs, sems = refs[:-1], refs[-1]
    moves = [
        fetch(weight_hbm, offset, weight_ref, sems.at[index])
        for index, (offset, weight_ref) in enumerate(zip(offsets, weight_refs))
    ]
    for move in moves:
        move.wait()


def stages(size):
    steps, stride = [], 1
    while stride < size:
        radix = 4 if stride > 1 and size // stride % 4 == 0 else 2
        steps.append((stride, radix))
        stride *= radix
    return steps


def entering(stride, rows, arrived_refs, rates):
    me = lax.axis_index("seq")
    digit = (me // stride) % (len(arrived_refs) + 1)
    state = jnp.zeros(rates.shape, F32)
    for index, arrived_ref in enumerate(arrived_refs):
        other = digit ^ (index + 1)
        blocks = me % stride + stride * (digit - 1 - other)
        fade = jnp.exp(-rates * (rows * jnp.maximum(blocks, 0)).astype(F32))
        state = state + jnp.where(other < digit, fade, 0.0) * arrived_ref[...].astype(F32)
    return state


def join_kernel(stride, radix, rows, outs, total_ref, rates_ref, *refs):
    arrived_refs, before_refs, out_refs = refs[: radix - 1], refs[radix - 1 : -outs], refs[-outs:]
    rates = rates_ref[...]
    carry = entering(stride, rows, arrived_refs, rates)
    for before_ref in before_refs:
        carry = carry + before_ref[...]
    digit = (lax.axis_index("seq") // stride) % radix
    joined = jnp.zeros(rates.shape, F32)
    for index, group_ref in enumerate((total_ref, *arrived_refs)):
        blocks = stride * (radix - 1 - (digit ^ index))
        joined = joined + jnp.exp(-rates * (rows * blocks).astype(F32)) * group_ref[...].astype(F32)
    for out_ref, value in zip(out_refs, (carry, joined, joined)):
        out_ref[...] = value.astype(out_ref.dtype)


def gate_kernel(
    piece, stride, post_ref, local_ref, table_ref, rates_ref, carry_ref, weight_ref, *refs
):
    *arrived_refs, gated_ref, first_ref, states_ref = refs
    height, width = gated_ref.shape
    modes = rates_ref.shape[0]
    subs = height // SUB
    base = piece * height
    rates = rates_ref[...]
    state = carry_ref[...] + entering(stride, post_ref.shape[0], arrived_refs, rates)
    if piece:
        state = state * jnp.exp(rates * (-float(base)))
    fade = jnp.exp(rates * (-float(SUB)))
    for sub in range(subs):
        states_ref[sub] = state
        state = state * fade
    for lane in range(0, width, LANES):
        cols = slice(lane, lane + LANES)
        totals = [local_ref[base + sub * SUB : base + (sub + 1) * SUB, cols] for sub in range(subs)]
        for mode in range(modes):
            entry = table_ref[mode, :, cols]
            totals = [
                total + entry * states_ref[sub, mode : mode + 1, cols] for sub, total in enumerate(totals)
            ]
        for sub in range(0, subs, 2):
            part = slice(base + sub * SUB, base + (sub + 2) * SUB)
            total = jnp.concatenate(totals[sub : sub + 2], axis=0)
            gated_ref[sub * SUB : (sub + 2) * SUB, cols] = (
                post_ref[part, cols].astype(F32) * total
            ).astype(BF16)
    first_ref[...] = jnp.dot(gated_ref[...], weight_ref[...], preferred_element_type=F32).astype(BF16)


def project_kernel(offsets, *refs):
    gated_refs, weight_ref, out_refs = refs[:PIECES], refs[PIECES], refs[PIECES + 1 : 2 * PIECES + 1]
    gated_ref, *rest = refs[2 * PIECES + 1 :]
    if offsets:
        move = fetch(weight_ref, offsets[0], *rest)
        weight_ref = rest[0]
    height = gated_refs[0].shape[0]
    for piece in range(PIECES):
        gated_ref[piece * height : (piece + 1) * height, :] = gated_refs[piece][...]
    if offsets:
        move.wait()
    product = jnp.dot(gated_ref[...], weight_ref[...], preferred_element_type=F32)
    for piece in range(PIECES):
        out_refs[piece][...] = product[piece * height : (piece + 1) * height, :].astype(out_refs[piece].dtype)


def after(value, earlier):
    return lax.optimization_barrier((value, earlier))[0]


def body(post_gate, pre_gate, signal, decay_rates, residues, skip_gain, out_weight):
    rows, width = post_gate.shape
    modes = decay_rates.shape[1]
    subs = rows // SUB
    size = lax.axis_size("seq")
    groups = lax.axis_size("chan")
    columns = out_weight.shape[1] // groups
    height = rows // PIECES
    block = ((width, columns), BF16)
    whole = ((modes, width), F32)
    mixed, starts, end, rates, residues, skip, post, weight = call(
        functools.partial(state_kernel, groups - 1),
        [HBM] * 7,
        [
            ((rows, width), F32),
            ((subs, modes, width), F32),
            whole,
            whole,
            whole,
            ((1, width), F32),
            ((rows, width), BF16),
            block,
        ],
        [pltpu.VMEM((rows, width), BF16), pltpu.VMEM((rows, width), BF16), DMA((6,)), DMA],
        4 * rows * modes * width,
        8 * rows * width,
    )(pre_gate, signal, decay_rates.T, residues.T, skip_gain.reshape(1, width), post_gate, out_weight)
    local, table = call(
        local_kernel,
        [VMEM] * 5,
        [((rows, width), F32), ((modes, SUB, width), F32)],
        [],
        2 * rows * (SUB + modes) * width,
        8 * rows * width,
    )(mixed, starts, rates, residues, skip)
    ready = list(range(groups - 2, max(groups - 4, 0), -1))
    blocks = call(
        functools.partial(fetch_kernel, ready),
        [HBM],
        [block] * len(ready),
        [DMA((len(ready),))],
        0,
        2 * width * columns * len(ready),
    )(out_weight)
    weights = dict(zip(ready, blocks))

    beside = [local] + [None] * (len(stages(size)) - 2) + [blocks[0]]
    total, sent, before = [end], end, []
    for (stride, radix), other in zip(stages(size), beside):
        arrived = [
            lax.ppermute(sent, "seq", [(source, source ^ (stride * hop)) for source in range(size)])
            for hop in range(1, radix)
        ]
        if other is not None:
            arrived[0] = after(arrived[0], other)
        if stride * radix < size:
            outs = [whole, ((modes, width), BF16)]
            if stride * radix < stages(size)[-1][0]:
                outs.append(whole)
            carry, sent, *total = call(
                functools.partial(join_kernel, stride, radix, rows, len(outs)),
                [VMEM] * (1 + radix + len(before)),
                outs,
                [],
                8 * radix * modes * width,
                16 * modes * width,
            )(*total, rates, *arrived, *before)
            before = [carry]

    gated, values = [], {groups - 1: []}
    for piece in range(PIECES):
        half, first = call(
            functools.partial(gate_kernel, piece, stride),
            [VMEM] * (6 + len(arrived)),
            [((height, width), BF16), ((height, columns), BF16)],
            [pltpu.VMEM((subs // PIECES, modes, width), F32)],
            2 * height * modes * width,
            16 * height * width,
        )(post, local, table, rates, carry, weight, *arrived)
        gated.append(half)
        values[groups - 1].append(first)

    def project(offset, earlier):
        held = [] if offset in weights else [offset]
        mine = gated if earlier is None else [after(half, earlier) for half in gated]
        return list(
            call(
                functools.partial(project_kernel, held),
                [VMEM] * PIECES + [HBM if held else VMEM],
                [((height, columns), BF16 if offset % 2 else F32)] * PIECES,
                [pltpu.VMEM((rows, width), BF16)]
                + ([pltpu.VMEM((width, columns), BF16), DMA] if held else []),
                2 * rows * width * columns,
                2 * width * columns,
            )(*mine, out_weight if held else weights[offset])
        )

    arrivals = []
    for offset in range(groups - 1, 0, -1):
        stride = offset & -offset
        pairs = [(source, source ^ stride) for source in range(groups)]
        for piece in range(PIECES):
            index = len(arrivals)
            if offset not in values:
                values[offset] = project(offset, arrivals[max(index - 4, 0)])
            sent = values[offset][piece].astype(BF16)
            if index >= IN_FLIGHT:
                sent = after(sent, arrivals[index - IN_FLIGHT])
            arrived = lax.ppermute(sent, "chan", pairs)
            target = offset ^ stride
            if target not in values:
                values[target] = project(target, arrivals[index - 1] if index else None)
            kept = values[target][piece]
            if piece:
                kept = after(kept, values[target][piece - 1])
            values[target][piece] = kept + arrived.astype(F32)
            arrivals.append(arrived)
    return jnp.concatenate([value.astype(BF16) for value in values[0]], axis=0)


def solution(mesh):
    return jax.shard_map(
        body,
        mesh=mesh,
        in_specs=(
            P("seq", "chan"),
            P("seq", "chan"),
            P("seq", "chan"),
            P("chan", None),
            P("chan", None),
            P("chan"),
            P("chan", None),
        ),
        out_specs=P("seq", "chan"),
        check_vma=False,
    )
```

```python
import functools

import jax
import jax.numpy as jnp
from jax import lax
from jax.experimental import pallas as pl
from jax.experimental.pallas import tpu as pltpu
from jax.sharding import PartitionSpec as P

SUB = 8
LANES = 128
PIECES = 2
F32 = jnp.float32
BF16 = jnp.bfloat16
VMEM = pl.BlockSpec(memory_space=pltpu.VMEM)
HBM = pl.BlockSpec(memory_space=pltpu.HBM)
DMA = pltpu.SemaphoreType.DMA


def call(kernel, ins, outs, scratch, flops, moved):
    run = pl.pallas_call(
        kernel,
        in_specs=ins,
        out_shape=[jax.ShapeDtypeStruct(shape, kind) for shape, kind in outs],
        out_specs=[VMEM] * len(outs),
        scratch_shapes=scratch,
        compiler_params=pltpu.CompilerParams(vmem_limit_bytes=24 * 2**20),
        cost_estimate=pl.CostEstimate(flops=flops, bytes_accessed=moved, transcendentals=0),
    )
    return lambda *operands: run(
        *[
            pltpu.with_memory_space_constraint(operand, pltpu.HBM) if spec is HBM else operand
            for spec, operand in zip(ins, operands)
        ]
    )


def fetch(weight_hbm, offset, weight_ref, sem):
    columns = weight_ref.shape[1]
    start = pl.multiple_of((lax.axis_index("chan") ^ offset) * columns, LANES)
    move = pltpu.make_async_copy(weight_hbm.at[:, pl.ds(start, columns)], weight_ref, sem)
    move.start()
    return move


def state_kernel(
    offset, pre_hbm, signal_hbm, rates_hbm, residues_hbm, skip_hbm, post_hbm, weight_hbm,
    mixed_ref, starts_ref, end_ref, rates_ref, residues_ref, skip_ref, post_ref, weight_ref,
    pre_ref, signal_ref, sems, weight_sem,
):
    moves = [
        pltpu.make_async_copy(source, target, sems.at[index])
        for index, (source, target) in enumerate(
            [
                (pre_hbm, pre_ref),
                (signal_hbm, signal_ref),
                (rates_hbm, rates_ref),
                (residues_hbm, residues_ref),
                (skip_hbm, skip_ref),
                (post_hbm, post_ref),
            ]
        )
    ]
    for move in moves:
        move.start()
    moves.append(fetch(weight_hbm, offset, weight_ref, weight_sem))
    for move in moves[:3]:
        move.wait()
    mixed_ref[...] = pre_ref[...].astype(F32) * signal_ref[...].astype(F32)
    fade = jnp.exp(-rates_ref[...])
    state = jnp.zeros(rates_ref.shape, F32)
    for sub in range(starts_ref.shape[0]):
        starts_ref[sub] = state
        for token in range(sub * SUB, (sub + 1) * SUB):
            state = fade * state + mixed_ref[token : token + 1, :]
    end_ref[...] = state
    for move in moves[3:]:
        move.wait()


def local_kernel(mixed_ref, starts_ref, rates_ref, residues_ref, skip_ref, local_ref, table_ref):
    rows, width = mixed_ref.shape
    modes = rates_ref.shape[0]
    row_ids = lax.broadcasted_iota(jnp.int32, (SUB, LANES), 0)
    steps = row_ids.astype(F32) + 1.0
    for lane in range(0, width, LANES):
        cols = slice(lane, lane + LANES)
        weights = residues_ref[:, cols] * jnp.sqrt(2.0 * rates_ref[:, cols])
        taps = jnp.zeros((SUB, LANES), F32)
        for mode in range(modes):
            entry = weights[mode : mode + 1, :] * jnp.exp(-rates_ref[mode : mode + 1, cols] * steps)
            table_ref[mode, :, cols] = entry
            taps = taps + entry
        first = jnp.sum(weights, axis=0, keepdims=True) + skip_ref[:, cols]
        masked = [jnp.where(row_ids >= lag, taps[lag - 1 : lag, :], 0.0) for lag in range(1, SUB)]
        totals = []
        for sub in range(0, rows, SUB):
            mixed = mixed_ref[sub : sub + SUB, cols]
            total = first * mixed
            for lag in range(1, SUB):
                total = total + masked[lag - 1] * pltpu.roll(mixed, lag, 0)
            totals.append(total)
        for mode in range(modes):
            entry = table_ref[mode, :, cols]
            totals = [
                total + entry * starts_ref[sub, mode : mode + 1, cols] if sub else total
                for sub, total in enumerate(totals)
            ]
        for sub, total in enumerate(totals):
            local_ref[sub * SUB : (sub + 1) * SUB, cols] = total


def fetch_kernel(offsets, weight_hbm, *refs):
    weight_refs, sems = refs[:-1], refs[-1]
    moves = [
        fetch(weight_hbm, offset, weight_ref, sems.at[index])
        for index, (offset, weight_ref) in enumerate(zip(offsets, weight_refs))
    ]
    for move in moves:
        move.wait()


def stages(size):
    steps, stride = [], 1
    while stride < size:
        radix = 4 if stride > 1 and size // stride % 4 == 0 else 2
        steps.append((stride, radix))
        stride *= radix
    return steps


def entering(stride, rows, arrived_refs, rates):
    me = lax.axis_index("seq")
    digit = (me // stride) % (len(arrived_refs) + 1)
    state = jnp.zeros(rates.shape, F32)
    for index, arrived_ref in enumerate(arrived_refs):
        other = digit ^ (index + 1)
        blocks = me % stride + stride * (digit - 1 - other)
        fade = jnp.exp(-rates * (rows * jnp.maximum(blocks, 0)).astype(F32))
        state = state + jnp.where(other < digit, fade, 0.0) * arrived_ref[...].astype(F32)
    return state


def join_kernel(stride, radix, rows, outs, total_ref, rates_ref, *refs):
    arrived_refs, before_refs, out_refs = refs[: radix - 1], refs[radix - 1 : -outs], refs[-outs:]
    rates = rates_ref[...]
    carry = entering(stride, rows, arrived_refs, rates)
    for before_ref in before_refs:
        carry = carry + before_ref[...]
    digit = (lax.axis_index("seq") // stride) % radix
    joined = jnp.zeros(rates.shape, F32)
    for index, group_ref in enumerate((total_ref, *arrived_refs)):
        blocks = stride * (radix - 1 - (digit ^ index))
        joined = joined + jnp.exp(-rates * (rows * blocks).astype(F32)) * group_ref[...].astype(F32)
    for out_ref, value in zip(out_refs, (carry, joined, joined)):
        out_ref[...] = value.astype(out_ref.dtype)


def gate_kernel(
    piece, stride, post_ref, local_ref, table_ref, rates_ref, carry_ref, weight_ref, *refs
):
    *arrived_refs, gated_ref, first_ref, states_ref = refs
    height, width = gated_ref.shape
    modes = rates_ref.shape[0]
    subs = height // SUB
    base = piece * height
    rates = rates_ref[...]
    state = carry_ref[...] + entering(stride, post_ref.shape[0], arrived_refs, rates)
    if piece:
        state = state * jnp.exp(rates * (-float(base)))
    fade = jnp.exp(rates * (-float(SUB)))
    for sub in range(subs):
        states_ref[sub] = state
        state = state * fade
    for lane in range(0, width, LANES):
        cols = slice(lane, lane + LANES)
        totals = [local_ref[base + sub * SUB : base + (sub + 1) * SUB, cols] for sub in range(subs)]
        for mode in range(modes):
            entry = table_ref[mode, :, cols]
            totals = [
                total + entry * states_ref[sub, mode : mode + 1, cols] for sub, total in enumerate(totals)
            ]
        for sub in range(0, subs, 2):
            part = slice(base + sub * SUB, base + (sub + 2) * SUB)
            total = jnp.concatenate(totals[sub : sub + 2], axis=0)
            gated_ref[sub * SUB : (sub + 2) * SUB, cols] = (
                post_ref[part, cols].astype(F32) * total
            ).astype(BF16)
    first_ref[...] = jnp.dot(gated_ref[...], weight_ref[...], preferred_element_type=F32).astype(BF16)


def project_kernel(offsets, *refs):
    gated_refs, weight_ref, out_refs = refs[:PIECES], refs[PIECES], refs[PIECES + 1 : 2 * PIECES + 1]
    gated_ref, *rest = refs[2 * PIECES + 1 :]
    if offsets:
        move = fetch(weight_ref, offsets[0], *rest)
        weight_ref = rest[0]
    height = gated_refs[0].shape[0]
    for piece in range(PIECES):
        gated_ref[piece * height : (piece + 1) * height, :] = gated_refs[piece][...]
    if offsets:
        move.wait()
    product = jnp.dot(gated_ref[...], weight_ref[...], preferred_element_type=F32)
    for piece in range(PIECES):
        out_refs[piece][...] = product[piece * height : (piece + 1) * height, :].astype(out_refs[piece].dtype)


def after(value, earlier):
    return lax.optimization_barrier((value, earlier))[0]


def body(post_gate, pre_gate, signal, decay_rates, residues, skip_gain, out_weight):
    rows, width = post_gate.shape
    modes = decay_rates.shape[1]
    subs = rows // SUB
    size = lax.axis_size("seq")
    groups = lax.axis_size("chan")
    columns = out_weight.shape[1] // groups
    height = rows // PIECES
    block = ((width, columns), BF16)
    whole = ((modes, width), F32)
    mixed, starts, end, rates, residues, skip, post, weight = call(
        functools.partial(state_kernel, groups - 1),
        [HBM] * 7,
        [
            ((rows, width), F32),
            ((subs, modes, width), F32),
            whole,
            whole,
            whole,
            ((1, width), F32),
            ((rows, width), BF16),
            block,
        ],
        [pltpu.VMEM((rows, width), BF16), pltpu.VMEM((rows, width), BF16), DMA((6,)), DMA],
        4 * rows * modes * width,
        8 * rows * width,
    )(pre_gate, signal, decay_rates.T, residues.T, skip_gain.reshape(1, width), post_gate, out_weight)
    local, table = call(
        local_kernel,
        [VMEM] * 5,
        [((rows, width), F32), ((modes, SUB, width), F32)],
        [],
        2 * rows * (SUB + modes) * width,
        8 * rows * width,
    )(mixed, starts, rates, residues, skip)
    ready = list(range(groups - 2, max(groups - 4, 0), -1))
    blocks = call(
        functools.partial(fetch_kernel, ready),
        [HBM],
        [block] * len(ready),
        [DMA((len(ready),))],
        0,
        2 * width * columns * len(ready),
    )(out_weight)
    weights = dict(zip(ready, blocks))

    beside = [local] + [None] * (len(stages(size)) - 2) + [blocks[0]]
    total, sent, before = [end], end, []
    for (stride, radix), other in zip(stages(size), beside):
        arrived = [
            lax.ppermute(sent, "seq", [(source, source ^ (stride * hop)) for source in range(size)])
            for hop in range(1, radix)
        ]
        if other is not None:
            arrived[0] = after(arrived[0], other)
        if stride * radix < size:
            outs = [whole, ((modes, width), BF16)]
            if stride * radix < stages(size)[-1][0]:
                outs.append(whole)
            carry, sent, *total = call(
                functools.partial(join_kernel, stride, radix, rows, len(outs)),
                [VMEM] * (1 + radix + len(before)),
                outs,
                [],
                8 * radix * modes * width,
                16 * modes * width,
            )(*total, rates, *arrived, *before)
            before = [carry]

    gated, values = [], {groups - 1: []}
    for piece in range(PIECES):
        half, first = call(
            functools.partial(gate_kernel, piece, stride),
            [VMEM] * (6 + len(arrived)),
            [((height, width), BF16), ((height, columns), BF16)],
            [pltpu.VMEM((subs // PIECES, modes, width), F32)],
            2 * height * modes * width,
            16 * height * width,
        )(post, local, table, rates, carry, weight, *arrived)
        gated.append(half)
        values[groups - 1].append(first)

    def project(offset, earlier):
        held = [] if offset in weights else [offset]
        mine = gated if earlier is None else [after(half, earlier) for half in gated]
        return list(
            call(
                functools.partial(project_kernel, held),
                [VMEM] * PIECES + [HBM if held else VMEM],
                [((height, columns), BF16 if offset % 2 else F32)] * PIECES,
                [pltpu.VMEM((rows, width), BF16)]
                + ([pltpu.VMEM((width, columns), BF16), DMA] if held else []),
                2 * rows * width * columns,
                2 * width * columns,
            )(*mine, out_weight if held else weights[offset])
        )

    sums = []
    for offset in range(groups - 1, 0, -1):
        stride = offset & -offset
        pairs = [(source, source ^ stride) for source in range(groups)]
        for piece in range(PIECES):
            index = len(sums)
            if offset not in values:
                values[offset] = project(offset, None)
            sent = values[offset][piece].astype(BF16)
            if index >= 2 * PIECES:
                sent = after(sent, sums[index - 2 * PIECES])
            arrived = lax.ppermute(sent, "chan", pairs)
            target = offset ^ stride
            if target not in values:
                values[target] = project(target, sums[-1] if sums else None)
            kept = values[target][piece]
            if piece:
                kept = after(kept, values[target][piece - 1])
            values[target][piece] = kept + arrived.astype(F32)
            sums.append(values[target][piece].astype(BF16))
    return jnp.concatenate([value.astype(BF16) for value in values[0]], axis=0)


def solution(mesh):
    return jax.shard_map(
        body,
        mesh=mesh,
        in_specs=(
            P("seq", "chan"),
            P("seq", "chan"),
            P("seq", "chan"),
            P("chan", None),
            P("chan", None),
            P("chan"),
            P("chan", None),
        ),
        out_specs=P("seq", "chan"),
        check_vma=False,
    )
```

```python
import functools

import jax
import jax.numpy as jnp
from jax import lax
from jax.experimental import pallas as pl
from jax.experimental.pallas import tpu as pltpu
from jax.sharding import PartitionSpec as P

SUB = 8
LANES = 128
PIECES = 2
CHUNKS = 4
F32 = jnp.float32
BF16 = jnp.bfloat16
VMEM = pl.BlockSpec(memory_space=pltpu.VMEM)
HBM = pl.BlockSpec(memory_space=pltpu.HBM)
DMA = pltpu.SemaphoreType.DMA


def call(kernel, ins, outs, scratch, flops, moved):
    run = pl.pallas_call(
        kernel,
        in_specs=ins,
        out_shape=[jax.ShapeDtypeStruct(shape, kind) for shape, kind in outs],
        out_specs=[VMEM] * len(outs),
        scratch_shapes=scratch,
        compiler_params=pltpu.CompilerParams(vmem_limit_bytes=24 * 2**20),
        cost_estimate=pl.CostEstimate(flops=flops, bytes_accessed=moved, transcendentals=0),
    )
    return lambda *operands: run(
        *[
            pltpu.with_memory_space_constraint(operand, pltpu.HBM) if spec is HBM else operand
            for spec, operand in zip(ins, operands)
        ]
    )


def fetch(weight_hbm, offset, weight_ref, sems):
    columns = weight_ref.shape[1]
    start = pl.multiple_of((lax.axis_index("chan") ^ offset) * columns, LANES)
    height = weight_ref.shape[0] // CHUNKS
    moves = []
    for chunk in range(CHUNKS):
        part = pl.ds(chunk * height, height)
        moves.append(
            pltpu.make_async_copy(
                weight_hbm.at[part, pl.ds(start, columns)], weight_ref.at[part, :], sems.at[chunk]
            )
        )
    for move in moves:
        move.start()
    return moves


def state_kernel(
    offset, pre_hbm, signal_hbm, rates_hbm, residues_hbm, skip_hbm, post_hbm, weight_hbm,
    mixed_ref, starts_ref, end_ref, sent_ref, rates_ref, residues_ref, skip_ref, post_ref, weight_ref,
    pre_ref, signal_ref, sems, weight_sems,
):
    moves = [
        pltpu.make_async_copy(source, target, sems.at[index])
        for index, (source, target) in enumerate(
            [
                (pre_hbm, pre_ref),
                (signal_hbm, signal_ref),
                (rates_hbm, rates_ref),
                (residues_hbm, residues_ref),
                (skip_hbm, skip_ref),
                (post_hbm, post_ref),
            ]
        )
    ]
    for move in moves:
        move.start()
    moves += fetch(weight_hbm, offset, weight_ref, weight_sems)
    for move in moves[:3]:
        move.wait()
    mixed_ref[...] = pre_ref[...].astype(F32) * signal_ref[...].astype(F32)
    fade = jnp.exp(-rates_ref[...])
    state = jnp.zeros(rates_ref.shape, F32)
    for sub in range(starts_ref.shape[0]):
        starts_ref[sub] = state
        for token in range(sub * SUB, (sub + 1) * SUB):
            state = fade * state + mixed_ref[token : token + 1, :]
    end_ref[...] = state
    sent_ref[...] = state.astype(BF16)
    for move in moves[3:]:
        move.wait()


def local_kernel(
    offset, mixed_ref, starts_ref, rates_ref, residues_ref, skip_ref, weight_hbm,
    local_ref, table_ref, weight_ref,
    sems,
):
    moves = fetch(weight_hbm, offset, weight_ref, sems)
    rows, width = mixed_ref.shape
    modes = rates_ref.shape[0]
    row_ids = lax.broadcasted_iota(jnp.int32, (SUB, LANES), 0)
    steps = row_ids.astype(F32) + 1.0
    for lane in range(0, width, LANES):
        cols = slice(lane, lane + LANES)
        weights = residues_ref[:, cols] * jnp.sqrt(2.0 * rates_ref[:, cols])
        taps = jnp.zeros((SUB, LANES), F32)
        for mode in range(modes):
            entry = weights[mode : mode + 1, :] * jnp.exp(-rates_ref[mode : mode + 1, cols] * steps)
            table_ref[mode, :, cols] = entry
            taps = taps + entry
        first = jnp.sum(weights, axis=0, keepdims=True) + skip_ref[:, cols]
        masked = [jnp.where(row_ids >= lag, taps[lag - 1 : lag, :], 0.0) for lag in range(1, SUB)]
        totals = []
        for sub in range(0, rows, SUB):
            mixed = mixed_ref[sub : sub + SUB, cols]
            total = first * mixed
            for lag in range(1, SUB):
                total = total + masked[lag - 1] * pltpu.roll(mixed, lag, 0)
            totals.append(total)
        for mode in range(modes):
            entry = table_ref[mode, :, cols]
            totals = [
                total + entry * starts_ref[sub, mode : mode + 1, cols] if sub else total
                for sub, total in enumerate(totals)
            ]
        for sub, total in enumerate(totals):
            local_ref[sub * SUB : (sub + 1) * SUB, cols] = total
    for move in moves:
        move.wait()


def fetch_kernel(offset, earlier_ref, weight_hbm, weight_ref, sems):
    for move in fetch(weight_hbm, offset, weight_ref, sems):
        move.wait()


def stages(size):
    steps, stride = [], 1
    while stride < size:
        radix = 4 if stride > 1 and size // stride % 4 == 0 else 2
        steps.append((stride, radix))
        stride *= radix
    return steps


def groups_of(paired, rows, arrived_refs, rates):
    states = [arrived_ref[...].astype(F32) for arrived_ref in arrived_refs]
    if paired:
        mine, other, *rest = states
        first = (lax.axis_index("seq") & 1) == 0
        fade = jnp.exp(rates * (-float(rows)))
        states = [fade * jnp.where(first, mine, other) + jnp.where(first, other, mine), *rest]
    return states


def entering(stride, rows, states, rates):
    me = lax.axis_index("seq")
    digit = (me // stride) % (len(states) + 1)
    total = jnp.zeros(rates.shape, F32)
    for index, state in enumerate(states):
        other = digit ^ (index + 1)
        blocks = me % stride + stride * (digit - 1 - other)
        fade = jnp.exp(-rates * (rows * jnp.maximum(blocks, 0)).astype(F32))
        total = total + jnp.where(other < digit, fade, 0.0) * state
    return total


def join_kernel(stride, paired, rows, arrivals, outs, total_ref, rates_ref, *refs):
    arrived_refs, before_refs, out_refs = refs[:arrivals], refs[arrivals:-outs], refs[-outs:]
    rates = rates_ref[...]
    states = groups_of(paired, rows, arrived_refs, rates)
    carry = entering(stride, rows, states, rates)
    for before_ref in before_refs:
        carry = carry + before_ref[...]
    digit = (lax.axis_index("seq") // stride) % (len(states) + 1)
    joined = jnp.zeros(rates.shape, F32)
    for index, state in enumerate((total_ref[...], *states)):
        blocks = stride * (len(states) - (digit ^ index))
        joined = joined + jnp.exp(-rates * (rows * blocks).astype(F32)) * state
    for out_ref, value in zip(out_refs, (carry, joined, joined)):
        out_ref[...] = value.astype(out_ref.dtype)


def gate_kernel(
    piece, stride, paired, post_ref, local_ref, table_ref, rates_ref, carry_ref, weight_ref, *refs
):
    *arrived_refs, gated_ref, first_ref, states_ref = refs
    height, width = gated_ref.shape
    modes = rates_ref.shape[0]
    subs = height // SUB
    base = piece * height
    rates = rates_ref[...]
    states = groups_of(paired, post_ref.shape[0], arrived_refs, rates)
    state = carry_ref[...] + entering(stride, post_ref.shape[0], states, rates)
    if piece:
        state = state * jnp.exp(rates * (-float(base)))
    fade = jnp.exp(rates * (-float(SUB)))
    for sub in range(subs):
        states_ref[sub] = state
        state = state * fade
    for lane in range(0, width, LANES):
        cols = slice(lane, lane + LANES)
        totals = [local_ref[base + sub * SUB : base + (sub + 1) * SUB, cols] for sub in range(subs)]
        for mode in range(modes):
            entry = table_ref[mode, :, cols]
            totals = [
                total + entry * states_ref[sub, mode : mode + 1, cols] for sub, total in enumerate(totals)
            ]
        for sub in range(0, subs, 2):
            part = slice(base + sub * SUB, base + (sub + 2) * SUB)
            total = jnp.concatenate(totals[sub : sub + 2], axis=0)
            gated_ref[sub * SUB : (sub + 2) * SUB, cols] = (
                post_ref[part, cols].astype(F32) * total
            ).astype(BF16)
    first_ref[...] = jnp.dot(gated_ref[...], weight_ref[...], preferred_element_type=F32).astype(BF16)


def project_kernel(offsets, *refs):
    gated_refs, weight_ref, out_refs = refs[:PIECES], refs[PIECES], refs[PIECES + 1 : 2 * PIECES + 1]
    gated_ref, *rest = refs[2 * PIECES + 1 :]
    moves = []
    if offsets:
        moves = fetch(weight_ref, offsets[0], *rest)
        weight_ref = rest[0]
    height = gated_refs[0].shape[0]
    for piece in range(PIECES):
        gated_ref[piece * height : (piece + 1) * height, :] = gated_refs[piece][...]
    for move in moves:
        move.wait()
    product = jnp.dot(gated_ref[...], weight_ref[...], preferred_element_type=F32)
    for piece in range(PIECES):
        out_refs[piece][...] = product[piece * height : (piece + 1) * height, :].astype(out_refs[piece].dtype)


def after(value, *earlier):
    return lax.optimization_barrier((value, *earlier))[0]


def body(post_gate, pre_gate, signal, decay_rates, residues, skip_gain, out_weight):
    rows, width = post_gate.shape
    modes = decay_rates.shape[1]
    subs = rows // SUB
    size = lax.axis_size("seq")
    groups = lax.axis_size("chan")
    columns = out_weight.shape[1] // groups
    height = rows // PIECES
    block = ((width, columns), BF16)
    whole = ((modes, width), F32)
    mixed, starts, end, own, rates, residues, skip, post, weight = call(
        functools.partial(state_kernel, groups - 1),
        [HBM] * 7,
        [
            ((rows, width), F32),
            ((subs, modes, width), F32),
            whole,
            ((modes, width), BF16),
            whole,
            whole,
            ((1, width), F32),
            ((rows, width), BF16),
            block,
        ],
        [pltpu.VMEM((rows, width), BF16), pltpu.VMEM((rows, width), BF16), DMA((6,)), DMA((CHUNKS,))],
        4 * rows * modes * width,
        8 * rows * width,
    )(pre_gate, signal, decay_rates.T, residues.T, skip_gain.reshape(1, width), post_gate, out_weight)
    def swap(state, distance):
        return lax.ppermute(state, "seq", [(source, source ^ distance) for source in range(size)])

    levels = stages(size)
    arrived, total, before, weights = [swap(end, 1)], [end], [], {}
    mine = swap(own, 2)
    for level, (stride, radix) in enumerate(levels):
        paired = level == 1
        if paired:
            local, table, weights[groups - 2] = call(
                functools.partial(local_kernel, groups - 2),
                [VMEM] * 5 + [HBM],
                [((rows, width), F32), ((modes, SUB, width), F32), block],
                [DMA((CHUNKS,))],
                2 * rows * (SUB + modes) * width,
                8 * rows * width,
            )(after(mixed, sent), starts, rates, residues, skip, out_weight)
            others = [swap(sent, stride * hop) for hop in range(2, radix)]
            mine = after(mine, others[0], local)
            arrived = [mine, swap(mine, 1)] + others
            (weights[groups - 3],) = call(
                functools.partial(fetch_kernel, groups - 3),
                [VMEM, HBM],
                [block],
                [DMA((CHUNKS,))],
                0,
                2 * width * columns,
            )(mine, out_weight)
        elif level:
            arrived = [swap(sent, stride * hop) for hop in range(1, radix)]
        if level + 1 < len(levels):
            outs = [whole, ((modes, width), BF16)] + [whole] * (level + 2 < len(levels))
            carry, sent, *total = call(
                functools.partial(join_kernel, stride, paired, rows, len(arrived), len(outs)),
                [VMEM] * (2 + len(arrived) + len(before)),
                outs,
                [],
                8 * radix * modes * width,
                16 * modes * width,
            )(*total, rates, *arrived, *before)
            before = [carry]
    arrived[-1] = after(arrived[-1], weights[groups - 3])

    gated, values = [], {groups - 1: []}
    for piece in range(PIECES):
        half, first = call(
            functools.partial(gate_kernel, piece, stride, paired),
            [VMEM] * (6 + len(arrived)),
            [((height, width), BF16), ((height, columns), BF16)],
            [pltpu.VMEM((subs // PIECES, modes, width), F32)],
            2 * height * modes * width,
            16 * height * width,
        )(post, local, table, rates, carry, weight, *arrived)
        gated.append(half)
        values[groups - 1].append(first)

    def project(offset, earlier):
        held = [] if offset in weights else [offset]
        mine = gated if earlier is None else [after(half, earlier) for half in gated]
        return list(
            call(
                functools.partial(project_kernel, held),
                [VMEM] * PIECES + [HBM if held else VMEM],
                [((height, columns), BF16 if offset % 2 else F32)] * PIECES,
                [pltpu.VMEM((rows, width), BF16)]
                + ([pltpu.VMEM((width, columns), BF16), DMA((CHUNKS,))] if held else []),
                2 * rows * width * columns,
                2 * width * columns,
            )(*mine, out_weight if held else weights[offset])
        )

    sums = []
    for offset in range(groups - 1, 0, -1):
        stride = offset & -offset
        pairs = [(source, source ^ stride) for source in range(groups)]
        for piece in range(PIECES):
            index = len(sums)
            if offset not in values:
                values[offset] = project(offset, None)
            sent = values[offset][piece].astype(BF16)
            if index >= 2 * PIECES:
                sent = after(sent, sums[index - 2 * PIECES])
            arrived = lax.ppermute(sent, "chan", pairs)
            target = offset ^ stride
            if target not in values:
                values[target] = project(target, sums[-1] if sums else None)
            kept = values[target][piece]
            if piece:
                kept = after(kept, values[target][piece - 1])
            values[target][piece] = kept + arrived.astype(F32)
            sums.append(values[target][piece].astype(BF16))
    return jnp.concatenate([value.astype(BF16) for value in values[0]], axis=0)


def solution(mesh):
    return jax.shard_map(
        body,
        mesh=mesh,
        in_specs=(
            P("seq", "chan"),
            P("seq", "chan"),
            P("seq", "chan"),
            P("chan", None),
            P("chan", None),
            P("chan"),
            P("chan", None),
        ),
        out_specs=P("seq", "chan"),
        check_vma=False,
    )
```

```python
import functools

import jax
import jax.numpy as jnp
from jax import lax
from jax.experimental import pallas as pl
from jax.experimental.pallas import tpu as pltpu
from jax.sharding import PartitionSpec as P

SUB = 8
LANES = 128
PIECES = 2
F32 = jnp.float32
BF16 = jnp.bfloat16
VMEM = pl.BlockSpec(memory_space=pltpu.VMEM)
HBM = pl.BlockSpec(memory_space=pltpu.HBM)
DMA = pltpu.SemaphoreType.DMA


def call(kernel, ins, outs, scratch, flops, moved):
    run = pl.pallas_call(
        kernel,
        in_specs=ins,
        out_shape=[jax.ShapeDtypeStruct(shape, kind) for shape, kind in outs],
        out_specs=[VMEM] * len(outs),
        scratch_shapes=scratch,
        compiler_params=pltpu.CompilerParams(vmem_limit_bytes=24 * 2**20),
        cost_estimate=pl.CostEstimate(flops=flops, bytes_accessed=moved, transcendentals=0),
    )
    return lambda *operands: run(
        *[
            pltpu.with_memory_space_constraint(operand, pltpu.HBM) if spec is HBM else operand
            for spec, operand in zip(ins, operands)
        ]
    )


def fetch(weight_hbm, offset, weight_ref, sem):
    columns = weight_ref.shape[1]
    start = pl.multiple_of((lax.axis_index("chan") ^ offset) * columns, LANES)
    move = pltpu.make_async_copy(weight_hbm.at[:, pl.ds(start, columns)], weight_ref, sem)
    move.start()
    return move


def state_kernel(
    offset, pre_hbm, signal_hbm, rates_hbm, residues_hbm, skip_hbm, post_hbm, weight_hbm,
    mixed_ref, starts_ref, end_ref, sent_ref, rates_ref, residues_ref, skip_ref, post_ref, weight_ref,
    pre_ref, signal_ref, sems, weight_sem,
):
    moves = [
        pltpu.make_async_copy(source, target, sems.at[index])
        for index, (source, target) in enumerate(
            [
                (pre_hbm, pre_ref),
                (signal_hbm, signal_ref),
                (rates_hbm, rates_ref),
                (residues_hbm, residues_ref),
                (skip_hbm, skip_ref),
                (post_hbm, post_ref),
            ]
        )
    ]
    for move in moves:
        move.start()
    moves.append(fetch(weight_hbm, offset, weight_ref, weight_sem))
    for move in moves[:3]:
        move.wait()
    mixed_ref[...] = pre_ref[...].astype(F32) * signal_ref[...].astype(F32)
    fade = jnp.exp(-rates_ref[...])
    state = jnp.zeros(rates_ref.shape, F32)
    for sub in range(starts_ref.shape[0]):
        starts_ref[sub] = state
        for token in range(sub * SUB, (sub + 1) * SUB):
            state = fade * state + mixed_ref[token : token + 1, :]
    end_ref[...] = state
    sent_ref[...] = state.astype(BF16)
    for move in moves[3:]:
        move.wait()


def local_kernel(mixed_ref, starts_ref, rates_ref, residues_ref, skip_ref, local_ref, table_ref):
    rows, width = mixed_ref.shape
    modes = rates_ref.shape[0]
    row_ids = lax.broadcasted_iota(jnp.int32, (SUB, LANES), 0)
    steps = row_ids.astype(F32) + 1.0
    for lane in range(0, width, LANES):
        cols = slice(lane, lane + LANES)
        weights = residues_ref[:, cols] * jnp.sqrt(2.0 * rates_ref[:, cols])
        taps = jnp.zeros((SUB, LANES), F32)
        for mode in range(modes):
            entry = weights[mode : mode + 1, :] * jnp.exp(-rates_ref[mode : mode + 1, cols] * steps)
            table_ref[mode, :, cols] = entry
            taps = taps + entry
        first = jnp.sum(weights, axis=0, keepdims=True) + skip_ref[:, cols]
        masked = [jnp.where(row_ids >= lag, taps[lag - 1 : lag, :], 0.0) for lag in range(1, SUB)]
        totals = []
        for sub in range(0, rows, SUB):
            mixed = mixed_ref[sub : sub + SUB, cols]
            total = first * mixed
            for lag in range(1, SUB):
                total = total + masked[lag - 1] * pltpu.roll(mixed, lag, 0)
            totals.append(total)
        for mode in range(modes):
            entry = table_ref[mode, :, cols]
            totals = [
                total + entry * starts_ref[sub, mode : mode + 1, cols] if sub else total
                for sub, total in enumerate(totals)
            ]
        for sub, total in enumerate(totals):
            local_ref[sub * SUB : (sub + 1) * SUB, cols] = total


def stages(size):
    steps, stride = [], 1
    while stride < size:
        radix = 4 if stride > 1 and size // stride % 4 == 0 else 2
        steps.append((stride, radix))
        stride *= radix
    return steps


def groups_of(paired, rows, arrived_refs, rates):
    states = [arrived_ref[...].astype(F32) for arrived_ref in arrived_refs]
    if paired:
        mine, other, *rest = states
        first = (lax.axis_index("seq") & 1) == 0
        fade = jnp.exp(rates * (-float(rows)))
        states = [fade * jnp.where(first, mine, other) + jnp.where(first, other, mine), *rest]
    return states


def entering(stride, rows, states, rates):
    me = lax.axis_index("seq")
    digit = (me // stride) % (len(states) + 1)
    total = jnp.zeros(rates.shape, F32)
    for index, state in enumerate(states):
        other = digit ^ (index + 1)
        blocks = me % stride + stride * (digit - 1 - other)
        fade = jnp.exp(-rates * (rows * jnp.maximum(blocks, 0)).astype(F32))
        total = total + jnp.where(other < digit, fade, 0.0) * state
    return total


def join_kernel(stride, paired, rows, arrivals, outs, total_ref, rates_ref, *refs):
    arrived_refs, before_refs, out_refs = refs[:arrivals], refs[arrivals:-outs], refs[-outs:]
    rates = rates_ref[...]
    states = groups_of(paired, rows, arrived_refs, rates)
    carry = entering(stride, rows, states, rates)
    for before_ref in before_refs:
        carry = carry + before_ref[...]
    digit = (lax.axis_index("seq") // stride) % (len(states) + 1)
    joined = jnp.zeros(rates.shape, F32)
    for index, state in enumerate((total_ref[...], *states)):
        blocks = stride * (len(states) - (digit ^ index))
        joined = joined + jnp.exp(-rates * (rows * blocks).astype(F32)) * state
    for out_ref, value in zip(out_refs, (carry, joined, joined)):
        out_ref[...] = value.astype(out_ref.dtype)


def gate_kernel(
    piece, stride, paired, fetched,
    post_ref, local_ref, table_ref, rates_ref, carry_ref, weight_ref, *refs,
):
    if fetched:
        *refs, sem = refs
        *arrived_refs, weight_hbm, gated_ref, first_ref, next_ref, states_ref = refs
        move = fetch(weight_hbm, fetched[0], next_ref, sem)
    else:
        *arrived_refs, gated_ref, first_ref, states_ref = refs
    height, width = gated_ref.shape
    modes = rates_ref.shape[0]
    subs = height // SUB
    base = piece * height
    rates = rates_ref[...]
    states = groups_of(paired, post_ref.shape[0], arrived_refs, rates)
    state = carry_ref[...] + entering(stride, post_ref.shape[0], states, rates)
    if piece:
        state = state * jnp.exp(rates * (-float(base)))
    fade = jnp.exp(rates * (-float(SUB)))
    for sub in range(subs):
        states_ref[sub] = state
        state = state * fade
    for lane in range(0, width, LANES):
        cols = slice(lane, lane + LANES)
        totals = [local_ref[base + sub * SUB : base + (sub + 1) * SUB, cols] for sub in range(subs)]
        for mode in range(modes):
            entry = table_ref[mode, :, cols]
            totals = [
                total + entry * states_ref[sub, mode : mode + 1, cols] for sub, total in enumerate(totals)
            ]
        for sub in range(0, subs, 2):
            part = slice(base + sub * SUB, base + (sub + 2) * SUB)
            total = jnp.concatenate(totals[sub : sub + 2], axis=0)
            gated_ref[sub * SUB : (sub + 2) * SUB, cols] = (
                post_ref[part, cols].astype(F32) * total
            ).astype(BF16)
    first_ref[...] = jnp.dot(gated_ref[...], weight_ref[...], preferred_element_type=F32).astype(BF16)
    if fetched:
        move.wait()


def project_kernel(held, fetched, *refs):
    gated_refs, weight_ref, *refs = refs[:PIECES], *refs[PIECES:]
    moves = []
    if fetched:
        weight_hbm, *refs, next_sem = refs
        moves.append(fetch(weight_hbm, fetched[0], refs[PIECES], next_sem))
    if held:
        *refs, held_ref, sem = refs
        fetch(weight_ref, held[0], held_ref, sem).wait()
        weight_ref = held_ref
    gated_ref = refs[-1]
    height = gated_refs[0].shape[0]
    for piece in range(PIECES):
        gated_ref[piece * height : (piece + 1) * height, :] = gated_refs[piece][...]
    product = jnp.dot(gated_ref[...], weight_ref[...], preferred_element_type=F32)
    for piece in range(PIECES):
        out_ref = refs[piece]
        out_ref[...] = product[piece * height : (piece + 1) * height, :].astype(out_ref.dtype)
    for move in moves:
        move.wait()


def after(value, *earlier):
    return lax.optimization_barrier((value, *earlier))[0]


def body(post_gate, pre_gate, signal, decay_rates, residues, skip_gain, out_weight):
    rows, width = post_gate.shape
    modes = decay_rates.shape[1]
    subs = rows // SUB
    size = lax.axis_size("seq")
    groups = lax.axis_size("chan")
    columns = out_weight.shape[1] // groups
    height = rows // PIECES
    block = ((width, columns), BF16)
    whole = ((modes, width), F32)
    mixed, starts, end, own, rates, residues, skip, post, weight = call(
        functools.partial(state_kernel, groups - 1),
        [HBM] * 7,
        [
            ((rows, width), F32),
            ((subs, modes, width), F32),
            whole,
            ((modes, width), BF16),
            whole,
            whole,
            ((1, width), F32),
            ((rows, width), BF16),
            block,
        ],
        [pltpu.VMEM((rows, width), BF16), pltpu.VMEM((rows, width), BF16), DMA((6,)), DMA],
        4 * rows * modes * width,
        8 * rows * width,
    )(pre_gate, signal, decay_rates.T, residues.T, skip_gain.reshape(1, width), post_gate, out_weight)
    def swap(state, distance):
        return lax.ppermute(state, "seq", [(source, source ^ distance) for source in range(size)])

    levels = stages(size)
    arrived, total, before, weights = [swap(end, 1)], [end], [], {}
    mine = swap(own, 2)
    for level, (stride, radix) in enumerate(levels):
        paired = level == 1
        if paired:
            local, table = call(
                local_kernel,
                [VMEM] * 5,
                [((rows, width), F32), ((modes, SUB, width), F32)],
                [],
                2 * rows * (SUB + modes) * width,
                8 * rows * width,
            )(after(mixed, sent), starts, rates, residues, skip)
            others = [swap(sent, stride * hop) for hop in range(2, radix)]
            mine = after(mine, others[0], local)
            arrived = [mine, swap(mine, 1)] + others
        elif level:
            arrived = [swap(sent, stride * hop) for hop in range(1, radix)]
        if level + 1 < len(levels):
            outs = [whole, ((modes, width), BF16)] + [whole] * (level + 2 < len(levels))
            carry, sent, *total = call(
                functools.partial(join_kernel, stride, paired, rows, len(arrived), len(outs)),
                [VMEM] * (2 + len(arrived) + len(before)),
                outs,
                [],
                8 * radix * modes * width,
                16 * modes * width,
            )(*total, rates, *arrived, *before)
            before = [carry]

    gated, values = [], {groups - 1: []}
    for piece in range(PIECES):
        fetched = [groups - 2] if piece + 1 == PIECES else []
        half, first, *blocks = call(
            functools.partial(gate_kernel, piece, stride, paired, fetched),
            [VMEM] * (6 + len(arrived)) + [HBM] * len(fetched),
            [((height, width), BF16), ((height, columns), BF16)] + [block] * len(fetched),
            [pltpu.VMEM((subs // PIECES, modes, width), F32)] + [DMA] * len(fetched),
            2 * height * modes * width,
            16 * height * width,
        )(post, local, table, rates, carry, weight, *arrived, *[out_weight] * len(fetched))
        gated.append(half)
        values[groups - 1].append(first)
        weights.update(zip(fetched, blocks))

    def project(offset, earlier):
        held = [] if offset in weights else [offset]
        fetched = [offset - 1] if offset == groups - 2 else []
        mine = gated if earlier is None else [after(half, earlier) for half in gated]
        shares = call(
            functools.partial(project_kernel, held, fetched),
            [VMEM] * PIECES + [HBM if held else VMEM] + [HBM] * len(fetched),
            [((height, columns), BF16 if offset % 2 else F32)] * PIECES + [block] * len(fetched),
            [pltpu.VMEM((rows, width), BF16)]
            + ([pltpu.VMEM((width, columns), BF16), DMA] if held else [])
            + [DMA] * len(fetched),
            2 * rows * width * columns,
            2 * width * columns,
        )(*mine, out_weight if held else weights[offset], *[out_weight] * len(fetched))
        weights.update(zip(fetched, shares[PIECES:]))
        return list(shares[:PIECES])

    sums = []
    for offset in range(groups - 1, 0, -1):
        stride = offset & -offset
        pairs = [(source, source ^ stride) for source in range(groups)]
        for piece in range(PIECES):
            index = len(sums)
            if offset not in values:
                values[offset] = project(offset, sums[index - 2 * PIECES])
            sent = values[offset][piece].astype(BF16)
            if index >= 2 * PIECES:
                sent = after(sent, sums[index - 2 * PIECES])
            arrived = lax.ppermute(sent, "chan", pairs)
            target = offset ^ stride
            if target not in values:
                values[target] = project(target, sums[-1] if sums else None)
            kept = values[target][piece]
            if piece:
                kept = after(kept, values[target][piece - 1])
            values[target][piece] = kept + arrived.astype(F32)
            sums.append(values[target][piece].astype(BF16))
    return jnp.concatenate([value.astype(BF16) for value in values[0]], axis=0)


def solution(mesh):
    return jax.shard_map(
        body,
        mesh=mesh,
        in_specs=(
            P("seq", "chan"),
            P("seq", "chan"),
            P("seq", "chan"),
            P("chan", None),
            P("chan", None),
            P("chan"),
            P("chan", None),
        ),
        out_specs=P("seq", "chan"),
        check_vma=False,
    )
```

```python
import functools

import jax
import jax.numpy as jnp
from jax import lax
from jax.experimental import pallas as pl
from jax.experimental.pallas import tpu as pltpu
from jax.sharding import PartitionSpec as P

SUB = 8
LANES = 128
PIECES = 2
F32 = jnp.float32
BF16 = jnp.bfloat16
VMEM = pl.BlockSpec(memory_space=pltpu.VMEM)
HBM = pl.BlockSpec(memory_space=pltpu.HBM)
DMA = pltpu.SemaphoreType.DMA


def call(kernel, ins, outs, scratch, flops, moved):
    run = pl.pallas_call(
        kernel,
        in_specs=ins,
        out_shape=[jax.ShapeDtypeStruct(shape, kind) for shape, kind in outs],
        out_specs=[VMEM] * len(outs),
        scratch_shapes=scratch,
        compiler_params=pltpu.CompilerParams(vmem_limit_bytes=24 * 2**20),
        cost_estimate=pl.CostEstimate(flops=flops, bytes_accessed=moved, transcendentals=0),
    )
    return lambda *operands: run(
        *[
            pltpu.with_memory_space_constraint(operand, pltpu.HBM) if spec is HBM else operand
            for spec, operand in zip(ins, operands)
        ]
    )


def fetch(weight_hbm, offset, weight_ref, sem):
    columns = weight_ref.shape[1]
    start = pl.multiple_of((lax.axis_index("chan") ^ offset) * columns, LANES)
    move = pltpu.make_async_copy(weight_hbm.at[:, pl.ds(start, columns)], weight_ref, sem)
    move.start()
    return move


def state_kernel(
    offset, pre_hbm, signal_hbm, rates_hbm, residues_hbm, skip_hbm, post_hbm, weight_hbm,
    mixed_ref, starts_ref, end_ref, sent_ref, rates_ref, residues_ref, skip_ref, post_ref, weight_ref,
    pre_ref, signal_ref, sems, weight_sem,
):
    moves = [
        pltpu.make_async_copy(source, target, sems.at[index])
        for index, (source, target) in enumerate(
            [
                (pre_hbm, pre_ref),
                (signal_hbm, signal_ref),
                (rates_hbm, rates_ref),
                (residues_hbm, residues_ref),
                (skip_hbm, skip_ref),
                (post_hbm, post_ref),
            ]
        )
    ]
    for move in moves:
        move.start()
    moves.append(fetch(weight_hbm, offset, weight_ref, weight_sem))
    for move in moves[:3]:
        move.wait()
    mixed_ref[...] = pre_ref[...].astype(F32) * signal_ref[...].astype(F32)
    fade = jnp.exp(-rates_ref[...])
    state = jnp.zeros(rates_ref.shape, F32)
    for sub in range(starts_ref.shape[0]):
        starts_ref[sub] = state
        for token in range(sub * SUB, (sub + 1) * SUB):
            state = fade * state + mixed_ref[token : token + 1, :]
    end_ref[...] = state
    sent_ref[...] = state.astype(BF16)
    for move in moves[3:]:
        move.wait()


def local_kernel(mixed_ref, starts_ref, rates_ref, residues_ref, skip_ref, local_ref, table_ref):
    rows, width = mixed_ref.shape
    modes = rates_ref.shape[0]
    row_ids = lax.broadcasted_iota(jnp.int32, (SUB, LANES), 0)
    steps = row_ids.astype(F32) + 1.0
    for lane in range(0, width, LANES):
        cols = slice(lane, lane + LANES)
        weights = residues_ref[:, cols] * jnp.sqrt(2.0 * rates_ref[:, cols])
        taps = jnp.zeros((SUB, LANES), F32)
        for mode in range(modes):
            entry = weights[mode : mode + 1, :] * jnp.exp(-rates_ref[mode : mode + 1, cols] * steps)
            table_ref[mode, :, cols] = entry
            taps = taps + entry
        first = jnp.sum(weights, axis=0, keepdims=True) + skip_ref[:, cols]
        masked = [jnp.where(row_ids >= lag, taps[lag - 1 : lag, :], 0.0) for lag in range(1, SUB)]
        totals = []
        for sub in range(0, rows, SUB):
            mixed = mixed_ref[sub : sub + SUB, cols]
            total = first * mixed
            for lag in range(1, SUB):
                total = total + masked[lag - 1] * pltpu.roll(mixed, lag, 0)
            totals.append(total)
        for mode in range(modes):
            entry = table_ref[mode, :, cols]
            totals = [
                total + entry * starts_ref[sub, mode : mode + 1, cols] if sub else total
                for sub, total in enumerate(totals)
            ]
        for sub, total in enumerate(totals):
            local_ref[sub * SUB : (sub + 1) * SUB, cols] = total


def stages(size):
    steps, stride = [], 1
    while stride < size:
        radix = 4 if stride > 1 and size // stride % 4 == 0 else 2
        steps.append((stride, radix))
        stride *= radix
    return steps


def groups_of(paired, rows, arrived_refs, rates):
    states = [arrived_ref[...].astype(F32) for arrived_ref in arrived_refs]
    if paired:
        mine, other, *rest = states
        first = (lax.axis_index("seq") & 1) == 0
        fade = jnp.exp(rates * (-float(rows)))
        states = [fade * jnp.where(first, mine, other) + jnp.where(first, other, mine), *rest]
    return states


def entering(stride, rows, states, rates):
    me = lax.axis_index("seq")
    digit = (me // stride) % (len(states) + 1)
    total = jnp.zeros(rates.shape, F32)
    for index, state in enumerate(states):
        other = digit ^ (index + 1)
        blocks = me % stride + stride * (digit - 1 - other)
        fade = jnp.exp(-rates * (rows * jnp.maximum(blocks, 0)).astype(F32))
        total = total + jnp.where(other < digit, fade, 0.0) * state
    return total


def join_kernel(stride, paired, rows, arrivals, outs, total_ref, rates_ref, *refs):
    arrived_refs, before_refs, out_refs = refs[:arrivals], refs[arrivals:-outs], refs[-outs:]
    rates = rates_ref[...]
    states = groups_of(paired, rows, arrived_refs, rates)
    carry = entering(stride, rows, states, rates)
    for before_ref in before_refs:
        carry = carry + before_ref[...]
    digit = (lax.axis_index("seq") // stride) % (len(states) + 1)
    joined = jnp.zeros(rates.shape, F32)
    for index, state in enumerate((total_ref[...], *states)):
        blocks = stride * (len(states) - (digit ^ index))
        joined = joined + jnp.exp(-rates * (rows * blocks).astype(F32)) * state
    for out_ref, value in zip(out_refs, (carry, joined, joined)):
        out_ref[...] = value.astype(out_ref.dtype)


def gate_kernel(
    piece, stride, paired,
    post_ref, local_ref, table_ref, rates_ref, carry_ref, weight_ref, *refs,
):
    *arrived_refs, gated_ref, first_ref, states_ref = refs
    height, width = gated_ref.shape
    modes = rates_ref.shape[0]
    subs = height // SUB
    base = piece * height
    rates = rates_ref[...]
    states = groups_of(paired, post_ref.shape[0], arrived_refs, rates)
    state = carry_ref[...] + entering(stride, post_ref.shape[0], states, rates)
    if piece:
        state = state * jnp.exp(rates * (-float(base)))
    fade = jnp.exp(rates * (-float(SUB)))
    for sub in range(subs):
        states_ref[sub] = state
        state = state * fade
    for lane in range(0, width, LANES):
        cols = slice(lane, lane + LANES)
        totals = [local_ref[base + sub * SUB : base + (sub + 1) * SUB, cols] for sub in range(subs)]
        for mode in range(modes):
            entry = table_ref[mode, :, cols]
            totals = [
                total + entry * states_ref[sub, mode : mode + 1, cols] for sub, total in enumerate(totals)
            ]
        for sub in range(0, subs, 2):
            part = slice(base + sub * SUB, base + (sub + 2) * SUB)
            total = jnp.concatenate(totals[sub : sub + 2], axis=0)
            gated_ref[sub * SUB : (sub + 2) * SUB, cols] = (
                post_ref[part, cols].astype(F32) * total
            ).astype(BF16)
    first_ref[...] = jnp.dot(gated_ref[...], weight_ref[...], preferred_element_type=F32).astype(BF16)


def project_kernel(offsets, held, *refs):
    gated_refs, weight_ref, out_refs = refs[:PIECES], refs[PIECES], refs[PIECES + 1 :]
    columns = out_refs[0].shape[1]
    gated_ref = refs[PIECES + 1 + len(offsets) * PIECES]
    height = gated_refs[0].shape[0]
    for piece in range(PIECES):
        gated_ref[piece * height : (piece + 1) * height, :] = gated_refs[piece][...]
    for slot, offset in enumerate(offsets):
        if held:
            start = pl.multiple_of((lax.axis_index("chan") ^ offset) * columns, LANES)
            block = weight_ref[:, pl.ds(start, columns)]
        else:
            block_ref, sem = refs[-2:]
            fetch(weight_ref, offset, block_ref, sem).wait()
            block = block_ref[...]
        product = jnp.dot(gated_ref[...], block, preferred_element_type=F32)
        for piece in range(PIECES):
            out_ref = out_refs[slot * PIECES + piece]
            out_ref[...] = product[piece * height : (piece + 1) * height, :].astype(out_ref.dtype)


def after(value, *earlier):
    return lax.optimization_barrier((value, *earlier))[0]


def body(post_gate, pre_gate, signal, decay_rates, residues, skip_gain, out_weight):
    rows, width = post_gate.shape
    modes = decay_rates.shape[1]
    subs = rows // SUB
    size = lax.axis_size("seq")
    groups = lax.axis_size("chan")
    columns = out_weight.shape[1] // groups
    height = rows // PIECES
    block = ((width, columns), BF16)
    whole = ((modes, width), F32)
    mixed, starts, end, own, rates, residues, skip, post, weight = call(
        functools.partial(state_kernel, groups - 1),
        [HBM] * 7,
        [
            ((rows, width), F32),
            ((subs, modes, width), F32),
            whole,
            ((modes, width), BF16),
            whole,
            whole,
            ((1, width), F32),
            ((rows, width), BF16),
            block,
        ],
        [pltpu.VMEM((rows, width), BF16), pltpu.VMEM((rows, width), BF16), DMA((6,)), DMA],
        4 * rows * modes * width,
        8 * rows * width,
    )(pre_gate, signal, decay_rates.T, residues.T, skip_gain.reshape(1, width), post_gate, out_weight)
    def swap(state, distance):
        return lax.ppermute(state, "seq", [(source, source ^ distance) for source in range(size)])

    levels = stages(size)
    arrived, total, before = [swap(end, 1)], [end], []
    mine = swap(own, 2)
    for level, (stride, radix) in enumerate(levels):
        paired = level == 1
        if paired:
            local, table = call(
                local_kernel,
                [VMEM] * 5,
                [((rows, width), F32), ((modes, SUB, width), F32)],
                [],
                2 * rows * (SUB + modes) * width,
                8 * rows * width,
            )(after(mixed, sent), starts, rates, residues, skip)
            others = [swap(sent, stride * hop) for hop in range(2, radix)]
            mine = after(mine, others[0], local)
            arrived = [mine, swap(mine, 1)] + others
        elif level:
            arrived = [swap(sent, stride * hop) for hop in range(1, radix)]
        if level + 1 < len(levels):
            outs = [whole, ((modes, width), BF16)] + [whole] * (level + 2 < len(levels))
            carry, sent, *total = call(
                functools.partial(join_kernel, stride, paired, rows, len(arrived), len(outs)),
                [VMEM] * (2 + len(arrived) + len(before)),
                outs,
                [],
                8 * radix * modes * width,
                16 * modes * width,
            )(*total, rates, *arrived, *before)
            before = [carry]

    gated, values = [], {groups - 1: []}
    for piece in range(PIECES):
        half, first = call(
            functools.partial(gate_kernel, piece, stride, paired),
            [VMEM] * (6 + len(arrived)),
            [((height, width), BF16), ((height, columns), BF16)],
            [pltpu.VMEM((subs // PIECES, modes, width), F32)],
            2 * height * modes * width,
            16 * height * width,
        )(post, local, table, rates, carry, weight, *arrived)
        gated.append(half)
        values[groups - 1].append(first)

    def project(offsets, held, earlier=None):
        mine = gated if earlier is None else [after(half, earlier) for half in gated]
        shares = call(
            functools.partial(project_kernel, offsets, held),
            [VMEM] * PIECES + [VMEM if held else HBM],
            [
                ((height, columns), BF16 if offset % 2 else F32)
                for offset in offsets
                for piece in range(PIECES)
            ],
            [pltpu.VMEM((rows, width), BF16)]
            + ([] if held else [pltpu.VMEM((width, columns), BF16), DMA]),
            2 * rows * width * columns * len(offsets),
            2 * width * columns * len(offsets),
        )(*mine, out_weight)
        for slot, offset in enumerate(offsets):
            values[offset] = list(shares[slot * PIECES : (slot + 1) * PIECES])

    project(list(range(groups - 2, max(groups - 4, 0), -1)), True)
    sums = []
    for offset in range(groups - 1, 0, -1):
        stride = offset & -offset
        pairs = [(source, source ^ stride) for source in range(groups)]
        for piece in range(PIECES):
            index = len(sums)
            if offset not in values:
                project([offset], False, sums[index - 2 * PIECES])
            sent = values[offset][piece].astype(BF16)
            if index >= 2 * PIECES:
                sent = after(sent, sums[index - 2 * PIECES])
            arrived = lax.ppermute(sent, "chan", pairs)
            target = offset ^ stride
            if target not in values:
                project([target], False, sums[-1])
            kept = values[target][piece]
            if piece:
                kept = after(kept, values[target][piece - 1])
            values[target][piece] = kept + arrived.astype(F32)
            sums.append(values[target][piece].astype(BF16))
    return jnp.concatenate([value.astype(BF16) for value in values[0]], axis=0)


def solution(mesh):
    return jax.shard_map(
        body,
        mesh=mesh,
        in_specs=(
            P("seq", "chan"),
            P("seq", "chan"),
            P("seq", "chan"),
            P("chan", None),
            P("chan", None),
            P("chan"),
            P("chan", None),
        ),
        out_specs=P("seq", "chan"),
        check_vma=False,
    )
```

```python
import functools

import jax
import jax.numpy as jnp
from jax import lax
from jax.experimental import pallas as pl
from jax.experimental.pallas import tpu as pltpu
from jax.sharding import PartitionSpec as P

SUB = 8
LANES = 128
PIECES = 2
F32 = jnp.float32
BF16 = jnp.bfloat16
VMEM = pl.BlockSpec(memory_space=pltpu.VMEM)
HBM = pl.BlockSpec(memory_space=pltpu.HBM)
DMA = pltpu.SemaphoreType.DMA


def call(kernel, ins, outs, scratch, flops, moved):
    run = pl.pallas_call(
        kernel,
        in_specs=ins,
        out_shape=[jax.ShapeDtypeStruct(shape, kind) for shape, kind in outs],
        out_specs=[VMEM] * len(outs),
        scratch_shapes=scratch,
        compiler_params=pltpu.CompilerParams(vmem_limit_bytes=24 * 2**20),
        cost_estimate=pl.CostEstimate(flops=flops, bytes_accessed=moved, transcendentals=0),
    )
    return lambda *operands: run(
        *[
            pltpu.with_memory_space_constraint(operand, pltpu.HBM) if spec is HBM else operand
            for spec, operand in zip(ins, operands)
        ]
    )


def block_of(weight_ref, offset, columns):
    start = pl.multiple_of((lax.axis_index("chan") ^ offset) * columns, LANES)
    return weight_ref.at[:, pl.ds(start, columns)]


def state_kernel(
    offset, pre_hbm, signal_hbm, rates_hbm, residues_hbm, skip_hbm, post_hbm, weight_hbm,
    mixed_ref, starts_ref, end_ref, sent_ref, rates_ref, residues_ref, skip_ref, post_ref, weight_ref,
    pre_ref, signal_ref, sems,
):
    moves = [
        pltpu.make_async_copy(source, target, sems.at[index])
        for index, (source, target) in enumerate(
            [
                (pre_hbm, pre_ref),
                (signal_hbm, signal_ref),
                (rates_hbm, rates_ref),
                (residues_hbm, residues_ref),
                (skip_hbm, skip_ref),
                (post_hbm, post_ref),
                (block_of(weight_hbm, offset, weight_ref.shape[1]), weight_ref),
            ]
        )
    ]
    for move in moves:
        move.start()
    for move in moves[:3]:
        move.wait()
    mixed_ref[...] = pre_ref[...].astype(F32) * signal_ref[...].astype(F32)
    fade = jnp.exp(-rates_ref[...])
    state = jnp.zeros(rates_ref.shape, F32)
    for sub in range(starts_ref.shape[0]):
        starts_ref[sub] = state
        for token in range(sub * SUB, (sub + 1) * SUB):
            state = fade * state + mixed_ref[token : token + 1, :]
    end_ref[...] = state
    sent_ref[...] = state.astype(BF16)
    for move in moves[3:]:
        move.wait()


def local_kernel(mixed_ref, starts_ref, rates_ref, residues_ref, skip_ref, local_ref, table_ref):
    rows, width = mixed_ref.shape
    modes = rates_ref.shape[0]
    row_ids = lax.broadcasted_iota(jnp.int32, (SUB, LANES), 0)
    steps = row_ids.astype(F32) + 1.0
    for lane in range(0, width, LANES):
        cols = slice(lane, lane + LANES)
        weights = residues_ref[:, cols] * jnp.sqrt(2.0 * rates_ref[:, cols])
        taps = jnp.zeros((SUB, LANES), F32)
        for mode in range(modes):
            entry = weights[mode : mode + 1, :] * jnp.exp(-rates_ref[mode : mode + 1, cols] * steps)
            table_ref[mode, :, cols] = entry
            taps = taps + entry
        first = jnp.sum(weights, axis=0, keepdims=True) + skip_ref[:, cols]
        masked = [jnp.where(row_ids >= lag, taps[lag - 1 : lag, :], 0.0) for lag in range(1, SUB)]
        totals = []
        for sub in range(0, rows, SUB):
            mixed = mixed_ref[sub : sub + SUB, cols]
            total = first * mixed
            for lag in range(1, SUB):
                total = total + masked[lag - 1] * pltpu.roll(mixed, lag, 0)
            totals.append(total)
        for mode in range(modes):
            entry = table_ref[mode, :, cols]
            totals = [
                total + entry * starts_ref[sub, mode : mode + 1, cols] if sub else total
                for sub, total in enumerate(totals)
            ]
        for sub, total in enumerate(totals):
            local_ref[sub * SUB : (sub + 1) * SUB, cols] = total


def stages(size):
    steps, stride = [], 1
    while stride < size:
        radix = 4 if stride > 1 and size // stride % 4 == 0 else 2
        steps.append((stride, radix))
        stride *= radix
    return steps


def groups_of(paired, rows, arrived_refs, rates):
    states = [arrived_ref[...].astype(F32) for arrived_ref in arrived_refs]
    if paired:
        mine, other, *rest = states
        first = (lax.axis_index("seq") & 1) == 0
        fade = jnp.exp(rates * (-float(rows)))
        states = [fade * jnp.where(first, mine, other) + jnp.where(first, other, mine), *rest]
    return states


def entering(stride, rows, states, rates):
    me = lax.axis_index("seq")
    digit = (me // stride) % (len(states) + 1)
    total = jnp.zeros(rates.shape, F32)
    for index, state in enumerate(states):
        other = digit ^ (index + 1)
        blocks = me % stride + stride * (digit - 1 - other)
        fade = jnp.exp(-rates * (rows * jnp.maximum(blocks, 0)).astype(F32))
        total = total + jnp.where(other < digit, fade, 0.0) * state
    return total


def join_kernel(stride, paired, rows, arrivals, outs, total_ref, rates_ref, *refs):
    arrived_refs, before_refs, out_refs = refs[:arrivals], refs[arrivals:-outs], refs[-outs:]
    rates = rates_ref[...]
    states = groups_of(paired, rows, arrived_refs, rates)
    carry = entering(stride, rows, states, rates)
    for before_ref in before_refs:
        carry = carry + before_ref[...]
    digit = (lax.axis_index("seq") // stride) % (len(states) + 1)
    joined = jnp.zeros(rates.shape, F32)
    for index, state in enumerate((total_ref[...], *states)):
        blocks = stride * (len(states) - (digit ^ index))
        joined = joined + jnp.exp(-rates * (rows * blocks).astype(F32)) * state
    for out_ref, value in zip(out_refs, (carry, joined, joined)):
        out_ref[...] = value.astype(out_ref.dtype)


def gate_kernel(
    piece, stride, paired,
    post_ref, local_ref, table_ref, rates_ref, carry_ref, weight_ref, *refs,
):
    *arrived_refs, gated_ref, first_ref, states_ref = refs
    height, width = gated_ref.shape
    modes = rates_ref.shape[0]
    subs = height // SUB
    base = piece * height
    rates = rates_ref[...]
    states = groups_of(paired, post_ref.shape[0], arrived_refs, rates)
    state = carry_ref[...] + entering(stride, post_ref.shape[0], states, rates)
    if piece:
        state = state * jnp.exp(rates * (-float(base)))
    fade = jnp.exp(rates * (-float(SUB)))
    for sub in range(subs):
        states_ref[sub] = state
        state = state * fade
    for lane in range(0, width, LANES):
        cols = slice(lane, lane + LANES)
        totals = [local_ref[base + sub * SUB : base + (sub + 1) * SUB, cols] for sub in range(subs)]
        for mode in range(modes):
            entry = table_ref[mode, :, cols]
            totals = [
                total + entry * states_ref[sub, mode : mode + 1, cols] for sub, total in enumerate(totals)
            ]
        for sub in range(0, subs, 2):
            part = slice(base + sub * SUB, base + (sub + 2) * SUB)
            total = jnp.concatenate(totals[sub : sub + 2], axis=0)
            gated_ref[sub * SUB : (sub + 2) * SUB, cols] = (
                post_ref[part, cols].astype(F32) * total
            ).astype(BF16)
    first_ref[...] = jnp.dot(gated_ref[...], weight_ref[...], preferred_element_type=F32).astype(BF16)


def project_kernel(offsets, *refs):
    gated_refs, weight_ref, out_refs, gated_ref = refs[:PIECES], refs[PIECES], refs[PIECES + 1 : -1], refs[-1]
    height = gated_refs[0].shape[0]
    for piece in range(PIECES):
        gated_ref[piece * height : (piece + 1) * height, :] = gated_refs[piece][...]
    for slot, offset in enumerate(offsets):
        block = block_of(weight_ref, offset, out_refs[0].shape[1])[...]
        product = jnp.dot(gated_ref[...], block, preferred_element_type=F32)
        for piece in range(PIECES):
            out_ref = out_refs[slot * PIECES + piece]
            out_ref[...] = product[piece * height : (piece + 1) * height, :].astype(out_ref.dtype)


def finish_kernel(*refs):
    *done_refs, kept_ref, arrived_ref, out_hbm, last_ref, sems = refs
    height = kept_ref.shape[0]
    moves = []
    for piece in range(PIECES):
        if piece + 1 == PIECES:
            last_ref[...] = (kept_ref[...] + arrived_ref[...].astype(F32)).astype(BF16)
        moves.append(
            pltpu.make_async_copy(
                (*done_refs, last_ref)[piece],
                out_hbm.at[piece * height : (piece + 1) * height, :],
                sems.at[piece],
            )
        )
        moves[-1].start()
    for move in moves:
        move.wait()


def after(value, *earlier):
    return lax.optimization_barrier((value, *earlier))[0]


def body(post_gate, pre_gate, signal, decay_rates, residues, skip_gain, out_weight):
    rows, width = post_gate.shape
    modes = decay_rates.shape[1]
    subs = rows // SUB
    size = lax.axis_size("seq")
    groups = lax.axis_size("chan")
    columns = out_weight.shape[1] // groups
    height = rows // PIECES
    whole = ((modes, width), F32)
    mixed, starts, end, own, rates, residues, skip, post, weight = call(
        functools.partial(state_kernel, groups - 1),
        [HBM] * 7,
        [
            ((rows, width), F32),
            ((subs, modes, width), F32),
            whole,
            ((modes, width), BF16),
            whole,
            whole,
            ((1, width), F32),
            ((rows, width), BF16),
            ((width, columns), BF16),
        ],
        [pltpu.VMEM((rows, width), BF16), pltpu.VMEM((rows, width), BF16), DMA((7,))],
        4 * rows * modes * width,
        8 * rows * width,
    )(pre_gate, signal, decay_rates.T, residues.T, skip_gain.reshape(1, width), post_gate, out_weight)
    def swap(state, distance):
        return lax.ppermute(state, "seq", [(source, source ^ distance) for source in range(size)])

    levels = stages(size)
    arrived, total, before = [swap(end, 1)], [end], []
    mine = swap(own, 2)
    for level, (stride, radix) in enumerate(levels):
        paired = level == 1
        if paired:
            local, table = call(
                local_kernel,
                [VMEM] * 5,
                [((rows, width), F32), ((modes, SUB, width), F32)],
                [],
                2 * rows * (SUB + modes) * width,
                8 * rows * width,
            )(after(mixed, sent), starts, rates, residues, skip)
            others = [swap(sent, stride * hop) for hop in range(2, radix)]
            mine = after(mine, others[0], local)
            arrived = [mine, swap(mine, 1)] + others
        elif level:
            arrived = [swap(sent, stride * hop) for hop in range(1, radix)]
        if level + 1 < len(levels):
            outs = [whole, ((modes, width), BF16)] + [whole] * (level + 2 < len(levels))
            carry, sent, *total = call(
                functools.partial(join_kernel, stride, paired, rows, len(arrived), len(outs)),
                [VMEM] * (2 + len(arrived) + len(before)),
                outs,
                [],
                8 * radix * modes * width,
                16 * modes * width,
            )(*total, rates, *arrived, *before)
            before = [carry]

    gated, values = [], {groups - 1: []}
    for piece in range(PIECES):
        half, first = call(
            functools.partial(gate_kernel, piece, stride, paired),
            [VMEM] * (6 + len(arrived)),
            [((height, width), BF16), ((height, columns), BF16)],
            [pltpu.VMEM((subs // PIECES, modes, width), F32)],
            2 * height * modes * width,
            16 * height * width,
        )(post, local, table, rates, carry, weight, *arrived)
        gated.append(half)
        values[groups - 1].append(first)

    offsets = list(range(groups - 2, -1, -1))
    shares = call(
        functools.partial(project_kernel, offsets),
        [VMEM] * (PIECES + 1),
        [((height, columns), BF16 if offset % 2 else F32) for offset in offsets for piece in range(PIECES)],
        [pltpu.VMEM((rows, width), BF16)],
        2 * rows * width * columns * len(offsets),
        2 * width * columns * len(offsets),
    )(*gated, out_weight)
    for slot, offset in enumerate(offsets):
        values[offset] = list(shares[slot * PIECES : (slot + 1) * PIECES])

    sums = []
    for offset in range(groups - 1, 0, -1):
        stride = offset & -offset
        target = offset ^ stride
        pairs = [(source, source ^ stride) for source in range(groups)]
        for piece in range(PIECES):
            index = len(sums)
            sent = values[offset][piece].astype(BF16)
            if index >= 2 * PIECES:
                sent = after(sent, sums[index - 2 * PIECES])
            arrived = lax.ppermute(sent, "chan", pairs)
            kept = values[target][piece]
            if piece:
                kept = after(kept, values[target][piece - 1])
            if offset == 1 and piece + 1 == PIECES:
                break
            values[target][piece] = kept + arrived.astype(F32)
            sums.append(values[target][piece].astype(BF16))
    done = [value.astype(BF16) for value in values[0][:-1]]
    return pl.pallas_call(
        finish_kernel,
        in_specs=[VMEM] * (PIECES + 1),
        out_shape=jax.ShapeDtypeStruct((rows, columns), BF16),
        out_specs=HBM,
        scratch_shapes=[pltpu.VMEM((height, columns), BF16), DMA((PIECES,))],
        compiler_params=pltpu.CompilerParams(vmem_limit_bytes=24 * 2**20),
    )(*done, kept, arrived)


def solution(mesh):
    return jax.shard_map(
        body,
        mesh=mesh,
        in_specs=(
            P("seq", "chan"),
            P("seq", "chan"),
            P("seq", "chan"),
            P("chan", None),
            P("chan", None),
            P("chan"),
            P("chan", None),
        ),
        out_specs=P("seq", "chan"),
        check_vma=False,
    )
```

```python
import functools

import jax
import jax.numpy as jnp
from jax import lax
from jax.experimental import pallas as pl
from jax.experimental.pallas import tpu as pltpu
from jax.sharding import PartitionSpec as P

SUB = 8
LANES = 128
PIECES = 2
F32 = jnp.float32
BF16 = jnp.bfloat16
VMEM = pl.BlockSpec(memory_space=pltpu.VMEM)
HBM = pl.BlockSpec(memory_space=pltpu.HBM)
DMA = pltpu.SemaphoreType.DMA


def call(kernel, ins, outs, scratch, flops, moved):
    run = pl.pallas_call(
        kernel,
        in_specs=ins,
        out_shape=[jax.ShapeDtypeStruct(shape, kind) for shape, kind in outs],
        out_specs=[VMEM] * len(outs),
        scratch_shapes=scratch,
        compiler_params=pltpu.CompilerParams(vmem_limit_bytes=24 * 2**20),
        cost_estimate=pl.CostEstimate(flops=flops, bytes_accessed=moved, transcendentals=0),
    )
    return lambda *operands: run(
        *[
            pltpu.with_memory_space_constraint(operand, pltpu.HBM) if spec is HBM else operand
            for spec, operand in zip(ins, operands)
        ]
    )


def block_of(weight_ref, offset, columns):
    start = pl.multiple_of((lax.axis_index("chan") ^ offset) * columns, LANES)
    return weight_ref.at[:, pl.ds(start, columns)]


def state_kernel(
    offset, pre_hbm, signal_hbm, rates_hbm, residues_hbm, skip_hbm, post_hbm, weight_hbm,
    mixed_ref, starts_ref, end_ref, sent_ref, rates_ref, residues_ref, skip_ref, post_ref, weight_ref,
    pre_ref, signal_ref, sems,
):
    moves = [
        pltpu.make_async_copy(source, target, sems.at[index])
        for index, (source, target) in enumerate(
            [
                (pre_hbm, pre_ref),
                (signal_hbm, signal_ref),
                (rates_hbm, rates_ref),
                (residues_hbm, residues_ref),
                (skip_hbm, skip_ref),
                (post_hbm, post_ref),
                (block_of(weight_hbm, offset, weight_ref.shape[1]), weight_ref),
            ]
        )
    ]
    for move in moves:
        move.start()
    for move in moves[:3]:
        move.wait()
    mixed_ref[...] = pre_ref[...].astype(F32) * signal_ref[...].astype(F32)
    fade = jnp.exp(-rates_ref[...])
    state = jnp.zeros(rates_ref.shape, F32)
    for sub in range(starts_ref.shape[0]):
        starts_ref[sub] = state
        for token in range(sub * SUB, (sub + 1) * SUB):
            state = fade * state + mixed_ref[token : token + 1, :]
    end_ref[...] = state
    sent_ref[...] = state.astype(BF16)
    for move in moves[3:]:
        move.wait()


def local_kernel(mixed_ref, starts_ref, rates_ref, residues_ref, skip_ref, local_ref, table_ref):
    rows, width = mixed_ref.shape
    modes = rates_ref.shape[0]
    row_ids = lax.broadcasted_iota(jnp.int32, (SUB, LANES), 0)
    steps = row_ids.astype(F32) + 1.0
    for lane in range(0, width, LANES):
        cols = slice(lane, lane + LANES)
        weights = residues_ref[:, cols] * jnp.sqrt(2.0 * rates_ref[:, cols])
        taps = jnp.zeros((SUB, LANES), F32)
        for mode in range(modes):
            entry = weights[mode : mode + 1, :] * jnp.exp(-rates_ref[mode : mode + 1, cols] * steps)
            table_ref[mode, :, cols] = entry
            taps = taps + entry
        first = jnp.sum(weights, axis=0, keepdims=True) + skip_ref[:, cols]
        masked = [jnp.where(row_ids >= lag, taps[lag - 1 : lag, :], 0.0) for lag in range(1, SUB)]
        totals = []
        for sub in range(0, rows, SUB):
            mixed = mixed_ref[sub : sub + SUB, cols]
            total = first * mixed
            for lag in range(1, SUB):
                total = total + masked[lag - 1] * pltpu.roll(mixed, lag, 0)
            totals.append(total)
        for mode in range(modes):
            entry = table_ref[mode, :, cols]
            totals = [
                total + entry * starts_ref[sub, mode : mode + 1, cols] if sub else total
                for sub, total in enumerate(totals)
            ]
        for sub, total in enumerate(totals):
            local_ref[sub * SUB : (sub + 1) * SUB, cols] = total


def stages(size):
    steps, stride = [], 1
    while stride < size:
        radix = 4 if stride > 1 and size // stride % 4 == 0 else 2
        steps.append((stride, radix))
        stride *= radix
    return steps


def groups_of(paired, rows, arrived_refs, rates):
    states = [arrived_ref[...].astype(F32) for arrived_ref in arrived_refs]
    if paired:
        mine, other, *rest = states
        first = (lax.axis_index("seq") & 1) == 0
        fade = jnp.exp(rates * (-float(rows)))
        states = [fade * jnp.where(first, mine, other) + jnp.where(first, other, mine), *rest]
    return states


def entering(stride, rows, states, rates, place=None):
    me = lax.axis_index("seq")
    place = me % stride if place is None else place
    digit = (me // stride) % (len(states) + 1)
    total = jnp.zeros(rates.shape, F32)
    for index, state in enumerate(states):
        other = digit ^ (index + 1)
        blocks = place + stride * (digit - 1 - other)
        fade = jnp.exp(-rates * (rows * jnp.maximum(blocks, 0)).astype(F32))
        total = total + jnp.where(other < digit, fade, 0.0) * state
    return total


def join_kernel(stride, paired, rows, arrivals, outs, total_ref, rates_ref, *refs):
    arrived_refs, before_refs, out_refs = refs[:arrivals], refs[arrivals:-outs], refs[-outs:]
    rates = rates_ref[...]
    states = groups_of(paired, rows, arrived_refs, rates)
    carry = entering(stride, rows, states, rates)
    for before_ref in before_refs:
        carry = carry + before_ref[...]
    digit = (lax.axis_index("seq") // stride) % (len(states) + 1)
    joined = jnp.zeros(rates.shape, F32)
    for index, state in enumerate((total_ref[...], *states)):
        blocks = stride * (len(states) - (digit ^ index))
        joined = joined + jnp.exp(-rates * (rows * blocks).astype(F32)) * state
    for out_ref, value in zip(out_refs, (carry, joined, joined)):
        out_ref[...] = value.astype(out_ref.dtype)


def chip_kernel(stride, rows, rates_ref, *refs):
    rates = rates_ref[...]
    states = groups_of(True, rows, refs[:-1], rates)
    refs[-1][...] = entering(stride, rows, states, rates, 0)


def gate_kernel(
    piece, stride, paired,
    post_ref, local_ref, table_ref, rates_ref, carry_ref, weight_ref, *refs,
):
    *arrived_refs, gated_ref, first_ref, states_ref = refs
    height, width = gated_ref.shape
    modes = rates_ref.shape[0]
    subs = height // SUB
    base = piece * height
    rates = rates_ref[...]
    if stride is None:
        chip_ref, other_ref = arrived_refs
        own = jnp.exp(rates * (-float(post_ref.shape[0]))) * chip_ref[...]
        state = carry_ref[...] + jnp.where((lax.axis_index("seq") & 1) == 0, other_ref[...], own)
    else:
        states = groups_of(paired, post_ref.shape[0], arrived_refs, rates)
        state = carry_ref[...] + entering(stride, post_ref.shape[0], states, rates)
    if piece:
        state = state * jnp.exp(rates * (-float(base)))
    fade = jnp.exp(rates * (-float(SUB)))
    for sub in range(subs):
        states_ref[sub] = state
        state = state * fade
    for lane in range(0, width, LANES):
        cols = slice(lane, lane + LANES)
        totals = [local_ref[base + sub * SUB : base + (sub + 1) * SUB, cols] for sub in range(subs)]
        for mode in range(modes):
            entry = table_ref[mode, :, cols]
            totals = [
                total + entry * states_ref[sub, mode : mode + 1, cols] for sub, total in enumerate(totals)
            ]
        for sub in range(0, subs, 2):
            part = slice(base + sub * SUB, base + (sub + 2) * SUB)
            total = jnp.concatenate(totals[sub : sub + 2], axis=0)
            gated_ref[sub * SUB : (sub + 2) * SUB, cols] = (
                post_ref[part, cols].astype(F32) * total
            ).astype(BF16)
    first_ref[...] = jnp.dot(gated_ref[...], weight_ref[...], preferred_element_type=F32).astype(BF16)


def project_kernel(offsets, *refs):
    gated_refs, weight_ref, out_refs, gated_ref = refs[:PIECES], refs[PIECES], refs[PIECES + 1 : -1], refs[-1]
    height = gated_refs[0].shape[0]
    for piece in range(PIECES):
        gated_ref[piece * height : (piece + 1) * height, :] = gated_refs[piece][...]
    for slot, offset in enumerate(offsets):
        block = block_of(weight_ref, offset, out_refs[0].shape[1])[...]
        product = jnp.dot(gated_ref[...], block, preferred_element_type=F32)
        for piece in range(PIECES):
            out_ref = out_refs[slot * PIECES + piece]
            out_ref[...] = product[piece * height : (piece + 1) * height, :].astype(out_ref.dtype)


def finish_kernel(*refs):
    *done_refs, kept_ref, arrived_ref, out_hbm, last_ref, sems = refs
    height = kept_ref.shape[0]
    moves = []
    for piece in range(PIECES):
        if piece + 1 == PIECES:
            last_ref[...] = (kept_ref[...] + arrived_ref[...].astype(F32)).astype(BF16)
        moves.append(
            pltpu.make_async_copy(
                (*done_refs, last_ref)[piece],
                out_hbm.at[piece * height : (piece + 1) * height, :],
                sems.at[piece],
            )
        )
        moves[-1].start()
    for move in moves:
        move.wait()


def after(value, *earlier):
    return lax.optimization_barrier((value, *earlier))[0]


def body(post_gate, pre_gate, signal, decay_rates, residues, skip_gain, out_weight):
    rows, width = post_gate.shape
    modes = decay_rates.shape[1]
    subs = rows // SUB
    size = lax.axis_size("seq")
    groups = lax.axis_size("chan")
    columns = out_weight.shape[1] // groups
    height = rows // PIECES
    whole = ((modes, width), F32)
    mixed, starts, end, own, rates, residues, skip, post, weight = call(
        functools.partial(state_kernel, groups - 1),
        [HBM] * 7,
        [
            ((rows, width), F32),
            ((subs, modes, width), F32),
            whole,
            ((modes, width), BF16),
            whole,
            whole,
            ((1, width), F32),
            ((rows, width), BF16),
            ((width, columns), BF16),
        ],
        [pltpu.VMEM((rows, width), BF16), pltpu.VMEM((rows, width), BF16), DMA((7,))],
        4 * rows * modes * width,
        8 * rows * width,
    )(pre_gate, signal, decay_rates.T, residues.T, skip_gain.reshape(1, width), post_gate, out_weight)
    def swap(state, distance, first=0, step=1):
        sources = range(first, size, step)
        return lax.ppermute(state, "seq", [(source, source ^ distance) for source in sources])

    levels = stages(size)
    arrived, total, before = [swap(end, 1)], [end], []
    mine = swap(own, 2)
    for level, (stride, radix) in enumerate(levels):
        paired = level == 1
        if paired:
            local, table = call(
                local_kernel,
                [VMEM] * 5,
                [((rows, width), F32), ((modes, SUB, width), F32)],
                [],
                2 * rows * (SUB + modes) * width,
                8 * rows * width,
            )(after(mixed, sent), starts, rates, residues, skip)
            last = level + 1 == len(levels)
            senders = (1, 2) if last else (0, 1)
            others = [swap(sent, stride * hop, *senders) for hop in range(2, radix)]
            mine = after(mine, others[0], local)
            arrived = [mine, swap(mine, 1)] + others
        elif level:
            arrived = [swap(sent, stride * hop) for hop in range(1, radix)]
        if level + 1 < len(levels):
            outs = [whole, ((modes, width), BF16)] + [whole] * (level + 2 < len(levels))
            carry, sent, *total = call(
                functools.partial(join_kernel, stride, paired, rows, len(arrived), len(outs)),
                [VMEM] * (2 + len(arrived) + len(before)),
                outs,
                [],
                8 * radix * modes * width,
                16 * modes * width,
            )(*total, rates, *arrived, *before)
            before = [carry]

    if last:
        (chip,) = call(
            functools.partial(chip_kernel, stride, rows),
            [VMEM] * (1 + len(arrived)),
            [whole],
            [],
            8 * radix * modes * width,
            16 * modes * width,
        )(rates, *arrived)
        arrived, stride = [chip, swap(chip, 1, 1, 2)], None

    gated, values = [], {groups - 1: []}
    for piece in range(PIECES):
        half, first = call(
            functools.partial(gate_kernel, piece, stride, paired),
            [VMEM] * (6 + len(arrived)),
            [((height, width), BF16), ((height, columns), BF16)],
            [pltpu.VMEM((subs // PIECES, modes, width), F32)],
            2 * height * modes * width,
            16 * height * width,
        )(post, local, table, rates, carry, weight, *arrived)
        gated.append(half)
        values[groups - 1].append(first)

    offsets = list(range(groups - 2, -1, -1))
    shares = call(
        functools.partial(project_kernel, offsets),
        [VMEM] * (PIECES + 1),
        [((height, columns), BF16 if offset % 2 else F32) for offset in offsets for piece in range(PIECES)],
        [pltpu.VMEM((rows, width), BF16)],
        2 * rows * width * columns * len(offsets),
        2 * width * columns * len(offsets),
    )(*gated, out_weight)
    for slot, offset in enumerate(offsets):
        values[offset] = list(shares[slot * PIECES : (slot + 1) * PIECES])

    sums = []
    for offset in range(groups - 1, 0, -1):
        stride = offset & -offset
        target = offset ^ stride
        pairs = [(source, source ^ stride) for source in range(groups)]
        for piece in range(PIECES):
            index = len(sums)
            sent = values[offset][piece].astype(BF16)
            if index >= 2 * PIECES:
                sent = after(sent, sums[index - 2 * PIECES])
            arrived = lax.ppermute(sent, "chan", pairs)
            kept = values[target][piece]
            if piece:
                kept = after(kept, values[target][piece - 1])
            if offset == 1 and piece + 1 == PIECES:
                break
            values[target][piece] = kept + arrived.astype(F32)
            sums.append(values[target][piece].astype(BF16))
    done = [value.astype(BF16) for value in values[0][:-1]]
    return pl.pallas_call(
        finish_kernel,
        in_specs=[VMEM] * (PIECES + 1),
        out_shape=jax.ShapeDtypeStruct((rows, columns), BF16),
        out_specs=HBM,
        scratch_shapes=[pltpu.VMEM((height, columns), BF16), DMA((PIECES,))],
        compiler_params=pltpu.CompilerParams(vmem_limit_bytes=24 * 2**20),
    )(*done, kept, arrived)


def solution(mesh):
    return jax.shard_map(
        body,
        mesh=mesh,
        in_specs=(
            P("seq", "chan"),
            P("seq", "chan"),
            P("seq", "chan"),
            P("chan", None),
            P("chan", None),
            P("chan"),
            P("chan", None),
        ),
        out_specs=P("seq", "chan"),
        check_vma=False,
    )
```

```python
import functools

import jax
import jax.numpy as jnp
from jax import lax
from jax.experimental import pallas as pl
from jax.experimental.pallas import tpu as pltpu
from jax.sharding import PartitionSpec as P

SUB = 8
LANES = 128
DEPTH = 256
PIECES = 2
F32 = jnp.float32
BF16 = jnp.bfloat16
VMEM = pl.BlockSpec(memory_space=pltpu.VMEM)
HBM = pl.BlockSpec(memory_space=pltpu.HBM)
DMA = pltpu.SemaphoreType.DMA


def call(kernel, ins, outs, scratch, flops, moved):
    run = pl.pallas_call(
        kernel,
        in_specs=ins,
        out_shape=[jax.ShapeDtypeStruct(shape, kind) for shape, kind in outs],
        out_specs=[VMEM] * len(outs),
        scratch_shapes=scratch,
        compiler_params=pltpu.CompilerParams(vmem_limit_bytes=24 * 2**20),
        cost_estimate=pl.CostEstimate(flops=flops, bytes_accessed=moved, transcendentals=0),
    )
    return lambda *operands: run(
        *[
            pltpu.with_memory_space_constraint(operand, pltpu.HBM) if spec is HBM else operand
            for spec, operand in zip(ins, operands)
        ]
    )


def block_of(weight_ref, offset, columns):
    start = pl.multiple_of((lax.axis_index("chan") ^ offset) * columns, LANES)
    return weight_ref.at[:, pl.ds(start, columns)]


def state_kernel(
    offset, pre_hbm, signal_hbm, rates_hbm, residues_hbm, skip_hbm, post_hbm, weight_hbm,
    mixed_ref, starts_ref, end_ref, sent_ref, rates_ref, residues_ref, skip_ref, post_ref, weight_ref,
    pre_ref, signal_ref, sems,
):
    moves = [
        pltpu.make_async_copy(source, target, sems.at[index])
        for index, (source, target) in enumerate(
            [
                (pre_hbm, pre_ref),
                (signal_hbm, signal_ref),
                (rates_hbm, rates_ref),
                (residues_hbm, residues_ref),
                (skip_hbm, skip_ref),
                (post_hbm, post_ref),
                (block_of(weight_hbm, offset, weight_ref.shape[1]), weight_ref),
            ]
        )
    ]
    for move in moves:
        move.start()
    for move in moves[:3]:
        move.wait()
    mixed_ref[...] = pre_ref[...].astype(F32) * signal_ref[...].astype(F32)
    fade = jnp.exp(-rates_ref[...])
    fade_sub = jnp.exp(rates_ref[...] * (-float(SUB)))
    state = jnp.zeros(rates_ref.shape, F32)
    for sub in range(starts_ref.shape[0]):
        starts_ref[sub] = state
        own = fade * mixed_ref[sub * SUB : sub * SUB + 1, :]
        for token in range(sub * SUB + 1, (sub + 1) * SUB - 1):
            own = fade * (own + mixed_ref[token : token + 1, :])
        state = fade_sub * state + (own + mixed_ref[(sub + 1) * SUB - 1 : (sub + 1) * SUB, :])
    end_ref[...] = state
    sent_ref[...] = state.astype(BF16)
    for move in moves[3:]:
        move.wait()


def local_kernel(mixed_ref, starts_ref, rates_ref, residues_ref, skip_ref, local_ref, table_ref):
    rows, width = mixed_ref.shape
    modes = rates_ref.shape[0]
    row_ids = lax.broadcasted_iota(jnp.int32, (SUB, LANES), 0)
    steps = row_ids.astype(F32) + 1.0
    for lane in range(0, width, LANES):
        cols = slice(lane, lane + LANES)
        weights = residues_ref[:, cols] * jnp.sqrt(2.0 * rates_ref[:, cols])
        taps = jnp.zeros((SUB, LANES), F32)
        for mode in range(modes):
            entry = weights[mode : mode + 1, :] * jnp.exp(-rates_ref[mode : mode + 1, cols] * steps)
            table_ref[mode, :, cols] = entry
            taps = taps + entry
        first = jnp.sum(weights, axis=0, keepdims=True) + skip_ref[:, cols]
        masked = [jnp.where(row_ids >= lag, taps[lag - 1 : lag, :], 0.0) for lag in range(1, SUB)]
        totals = []
        for sub in range(0, rows, SUB):
            mixed = mixed_ref[sub : sub + SUB, cols]
            total = first * mixed
            for lag in range(1, SUB):
                total = total + masked[lag - 1] * pltpu.roll(mixed, lag, 0)
            totals.append(total)
        for mode in range(modes):
            entry = table_ref[mode, :, cols]
            totals = [
                total + entry * starts_ref[sub, mode : mode + 1, cols] if sub else total
                for sub, total in enumerate(totals)
            ]
        for sub, total in enumerate(totals):
            local_ref[sub * SUB : (sub + 1) * SUB, cols] = total


def stages(size):
    steps, stride = [], 1
    while stride < size:
        radix = 4 if stride > 1 and size // stride % 4 == 0 else 2
        steps.append((stride, radix))
        stride *= radix
    return steps


def groups_of(paired, rows, arrived_refs, rates):
    states = [arrived_ref[...].astype(F32) for arrived_ref in arrived_refs]
    if paired:
        mine, other, *rest = states
        first = (lax.axis_index("seq") & 1) == 0
        fade = jnp.exp(rates * (-float(rows)))
        states = [fade * jnp.where(first, mine, other) + jnp.where(first, other, mine), *rest]
    return states


def entering(stride, rows, states, rates):
    me = lax.axis_index("seq")
    digit = (me // stride) % (len(states) + 1)
    total = jnp.zeros(rates.shape, F32)
    for index, state in enumerate(states):
        other = digit ^ (index + 1)
        blocks = me % stride + stride * (digit - 1 - other)
        fade = jnp.exp(-rates * (rows * jnp.maximum(blocks, 0)).astype(F32))
        total = total + jnp.where(other < digit, fade, 0.0) * state
    return total


def join_kernel(stride, paired, rows, arrivals, outs, total_ref, rates_ref, *refs):
    arrived_refs, before_refs, out_refs = refs[:arrivals], refs[arrivals:-outs], refs[-outs:]
    rates = rates_ref[...]
    states = groups_of(paired, rows, arrived_refs, rates)
    carry = entering(stride, rows, states, rates)
    for before_ref in before_refs:
        carry = carry + before_ref[...]
    digit = (lax.axis_index("seq") // stride) % (len(states) + 1)
    joined = jnp.zeros(rates.shape, F32)
    for index, state in enumerate((total_ref[...], *states)):
        blocks = stride * (len(states) - (digit ^ index))
        joined = joined + jnp.exp(-rates * (rows * blocks).astype(F32)) * state
    for out_ref, value in zip(out_refs, (carry, joined, joined)):
        out_ref[...] = value.astype(out_ref.dtype)


def gate_kernel(
    piece, stride, paired,
    post_ref, local_ref, table_ref, rates_ref, carry_ref, weight_ref, *refs,
):
    *arrived_refs, gated_ref, first_ref, states_ref = refs
    height, width = gated_ref.shape
    modes = rates_ref.shape[0]
    subs = height // SUB
    base = piece * height
    rates = rates_ref[...]
    states = groups_of(paired, post_ref.shape[0], arrived_refs, rates)
    state = carry_ref[...] + entering(stride, post_ref.shape[0], states, rates)
    if piece:
        state = state * jnp.exp(rates * (-float(base)))
    fade = jnp.exp(rates * (-float(SUB)))
    for sub in range(subs):
        states_ref[sub] = state
        state = state * fade
    product = jnp.zeros(first_ref.shape, F32)
    for lane in range(0, width, LANES):
        cols = slice(lane, lane + LANES)
        totals = [local_ref[base + sub * SUB : base + (sub + 1) * SUB, cols] for sub in range(subs)]
        for mode in range(modes):
            entry = table_ref[mode, :, cols]
            totals = [
                total + entry * states_ref[sub, mode : mode + 1, cols] for sub, total in enumerate(totals)
            ]
        for sub in range(0, subs, 2):
            part = slice(base + sub * SUB, base + (sub + 2) * SUB)
            total = jnp.concatenate(totals[sub : sub + 2], axis=0)
            gated_ref[sub * SUB : (sub + 2) * SUB, cols] = (
                post_ref[part, cols].astype(F32) * total
            ).astype(BF16)
        if (lane + LANES) % DEPTH == 0:
            depth = slice(lane + LANES - DEPTH, lane + LANES)
            product = product + jnp.dot(
                gated_ref[:, depth], weight_ref[depth, :], preferred_element_type=F32
            )
    first_ref[...] = product.astype(BF16)


def project_kernel(offsets, *refs):
    gated_refs, weight_ref, out_refs, gated_ref = refs[:PIECES], refs[PIECES], refs[PIECES + 1 : -1], refs[-1]
    height = gated_refs[0].shape[0]
    for piece in range(PIECES):
        gated_ref[piece * height : (piece + 1) * height, :] = gated_refs[piece][...]
    for slot, offset in enumerate(offsets):
        block = block_of(weight_ref, offset, out_refs[0].shape[1])[...]
        product = jnp.dot(gated_ref[...], block, preferred_element_type=F32)
        for piece in range(PIECES):
            out_ref = out_refs[slot * PIECES + piece]
            out_ref[...] = product[piece * height : (piece + 1) * height, :].astype(out_ref.dtype)


def finish_kernel(*refs):
    *done_refs, kept_ref, arrived_ref, out_hbm, last_ref, sems = refs
    height = kept_ref.shape[0]
    moves = []
    for piece in range(PIECES):
        if piece + 1 == PIECES:
            last_ref[...] = (kept_ref[...] + arrived_ref[...].astype(F32)).astype(BF16)
        moves.append(
            pltpu.make_async_copy(
                (*done_refs, last_ref)[piece],
                out_hbm.at[piece * height : (piece + 1) * height, :],
                sems.at[piece],
            )
        )
        moves[-1].start()
    for move in moves:
        move.wait()


def after(value, *earlier):
    return lax.optimization_barrier((value, *earlier))[0]


def body(post_gate, pre_gate, signal, decay_rates, residues, skip_gain, out_weight):
    rows, width = post_gate.shape
    modes = decay_rates.shape[1]
    subs = rows // SUB
    size = lax.axis_size("seq")
    groups = lax.axis_size("chan")
    columns = out_weight.shape[1] // groups
    height = rows // PIECES
    whole = ((modes, width), F32)
    mixed, starts, end, own, rates, residues, skip, post, weight = call(
        functools.partial(state_kernel, groups - 1),
        [HBM] * 7,
        [
            ((rows, width), F32),
            ((subs, modes, width), F32),
            whole,
            ((modes, width), BF16),
            whole,
            whole,
            ((1, width), F32),
            ((rows, width), BF16),
            ((width, columns), BF16),
        ],
        [pltpu.VMEM((rows, width), BF16), pltpu.VMEM((rows, width), BF16), DMA((7,))],
        4 * rows * modes * width,
        8 * rows * width,
    )(pre_gate, signal, decay_rates.T, residues.T, skip_gain.reshape(1, width), post_gate, out_weight)
    def swap(state, distance):
        return lax.ppermute(state, "seq", [(source, source ^ distance) for source in range(size)])

    levels = stages(size)
    arrived, total, before = [swap(end, 1)], [end], []
    mine = swap(own, 2)
    for level, (stride, radix) in enumerate(levels):
        paired = level == 1
        if paired:
            local, table = call(
                local_kernel,
                [VMEM] * 5,
                [((rows, width), F32), ((modes, SUB, width), F32)],
                [],
                2 * rows * (SUB + modes) * width,
                8 * rows * width,
            )(after(mixed, sent), starts, rates, residues, skip)
            others = [swap(sent, stride * hop) for hop in range(2, radix)]
            mine = after(mine, others[0], local)
            arrived = [mine, swap(mine, 1)] + others
        elif level:
            arrived = [swap(sent, stride * hop) for hop in range(1, radix)]
        if level + 1 < len(levels):
            outs = [whole, ((modes, width), BF16)] + [whole] * (level + 2 < len(levels))
            carry, sent, *total = call(
                functools.partial(join_kernel, stride, paired, rows, len(arrived), len(outs)),
                [VMEM] * (2 + len(arrived) + len(before)),
                outs,
                [],
                8 * radix * modes * width,
                16 * modes * width,
            )(*total, rates, *arrived, *before)
            before = [carry]

    gated, values = [], {groups - 1: []}
    for piece in range(PIECES):
        half, first = call(
            functools.partial(gate_kernel, piece, stride, paired),
            [VMEM] * (6 + len(arrived)),
            [((height, width), BF16), ((height, columns), BF16)],
            [pltpu.VMEM((subs // PIECES, modes, width), F32)],
            2 * height * modes * width,
            16 * height * width,
        )(post, local, table, rates, carry, weight, *arrived)
        gated.append(half)
        values[groups - 1].append(first)

    offsets = list(range(groups - 2, -1, -1))
    shares = call(
        functools.partial(project_kernel, offsets),
        [VMEM] * (PIECES + 1),
        [((height, columns), BF16 if offset % 2 else F32) for offset in offsets for piece in range(PIECES)],
        [pltpu.VMEM((rows, width), BF16)],
        2 * rows * width * columns * len(offsets),
        2 * width * columns * len(offsets),
    )(*gated, out_weight)
    for slot, offset in enumerate(offsets):
        values[offset] = list(shares[slot * PIECES : (slot + 1) * PIECES])

    sums = []
    for offset in range(groups - 1, 0, -1):
        stride = offset & -offset
        target = offset ^ stride
        pairs = [(source, source ^ stride) for source in range(groups)]
        for piece in range(PIECES):
            index = len(sums)
            sent = values[offset][piece].astype(BF16)
            if index >= 2 * PIECES:
                sent = after(sent, sums[index - 2 * PIECES])
            arrived = lax.ppermute(sent, "chan", pairs)
            kept = values[target][piece]
            if piece:
                kept = after(kept, values[target][piece - 1])
            if offset == 1 and piece + 1 == PIECES:
                break
            values[target][piece] = kept + arrived.astype(F32)
            sums.append(values[target][piece].astype(BF16))
    done = [value.astype(BF16) for value in values[0][:-1]]
    return pl.pallas_call(
        finish_kernel,
        in_specs=[VMEM] * (PIECES + 1),
        out_shape=jax.ShapeDtypeStruct((rows, columns), BF16),
        out_specs=HBM,
        scratch_shapes=[pltpu.VMEM((height, columns), BF16), DMA((PIECES,))],
        compiler_params=pltpu.CompilerParams(vmem_limit_bytes=24 * 2**20),
    )(*done, kept, arrived)


def solution(mesh):
    return jax.shard_map(
        body,
        mesh=mesh,
        in_specs=(
            P("seq", "chan"),
            P("seq", "chan"),
            P("seq", "chan"),
            P("chan", None),
            P("chan", None),
            P("chan"),
            P("chan", None),
        ),
        out_specs=P("seq", "chan"),
        check_vma=False,
    )
```

```python
import functools

import jax
import jax.numpy as jnp
from jax import lax
from jax.experimental import pallas as pl
from jax.experimental.pallas import tpu as pltpu
from jax.sharding import PartitionSpec as P

SUB = 8
LANES = 128
DEPTH = 256
PIECES = 2
F32 = jnp.float32
BF16 = jnp.bfloat16
VMEM = pl.BlockSpec(memory_space=pltpu.VMEM)
HBM = pl.BlockSpec(memory_space=pltpu.HBM)
DMA = pltpu.SemaphoreType.DMA


def call(kernel, ins, outs, scratch, flops, moved):
    run = pl.pallas_call(
        kernel,
        in_specs=ins,
        out_shape=[jax.ShapeDtypeStruct(shape, kind) for shape, kind in outs],
        out_specs=[VMEM] * len(outs),
        scratch_shapes=scratch,
        compiler_params=pltpu.CompilerParams(vmem_limit_bytes=24 * 2**20),
        cost_estimate=pl.CostEstimate(flops=flops, bytes_accessed=moved, transcendentals=0),
    )
    return lambda *operands: run(
        *[
            pltpu.with_memory_space_constraint(operand, pltpu.HBM) if spec is HBM else operand
            for spec, operand in zip(ins, operands)
        ]
    )


def block_of(weight_ref, offset, columns):
    start = pl.multiple_of((lax.axis_index("chan") ^ offset) * columns, LANES)
    return weight_ref.at[:, pl.ds(start, columns)]


def state_kernel(
    pre_hbm, signal_hbm, rates_hbm, residues_hbm, skip_hbm, post_hbm,
    mixed_ref, starts_ref, end_ref, sent_ref, rates_ref, residues_ref, skip_ref, post_ref,
    pre_ref, signal_ref, sems,
):
    moves = [
        pltpu.make_async_copy(source, target, sems.at[index])
        for index, (source, target) in enumerate(
            [
                (pre_hbm, pre_ref),
                (signal_hbm, signal_ref),
                (rates_hbm, rates_ref),
                (residues_hbm, residues_ref),
                (skip_hbm, skip_ref),
                (post_hbm, post_ref),
            ]
        )
    ]
    for move in moves:
        move.start()
    for move in moves[:3]:
        move.wait()
    mixed_ref[...] = pre_ref[...].astype(F32) * signal_ref[...].astype(F32)
    fade = jnp.exp(-rates_ref[...])
    fade_sub = jnp.exp(rates_ref[...] * (-float(SUB)))
    state = jnp.zeros(rates_ref.shape, F32)
    for sub in range(starts_ref.shape[0]):
        starts_ref[sub] = state
        own = fade * mixed_ref[sub * SUB : sub * SUB + 1, :]
        for token in range(sub * SUB + 1, (sub + 1) * SUB - 1):
            own = fade * (own + mixed_ref[token : token + 1, :])
        state = fade_sub * state + (own + mixed_ref[(sub + 1) * SUB - 1 : (sub + 1) * SUB, :])
    end_ref[...] = state
    sent_ref[...] = state.astype(BF16)
    for move in moves[3:]:
        move.wait()


def local_kernel(
    offset, mixed_ref, starts_ref, rates_ref, residues_ref, skip_ref, weight_hbm,
    local_ref, table_ref, weight_ref,
    sem,
):
    move = pltpu.make_async_copy(block_of(weight_hbm, offset, weight_ref.shape[1]), weight_ref, sem)
    move.start()
    rows, width = mixed_ref.shape
    modes = rates_ref.shape[0]
    row_ids = lax.broadcasted_iota(jnp.int32, (SUB, LANES), 0)
    steps = row_ids.astype(F32) + 1.0
    for lane in range(0, width, LANES):
        cols = slice(lane, lane + LANES)
        weights = residues_ref[:, cols] * jnp.sqrt(2.0 * rates_ref[:, cols])
        taps = jnp.zeros((SUB, LANES), F32)
        for mode in range(modes):
            entry = weights[mode : mode + 1, :] * jnp.exp(-rates_ref[mode : mode + 1, cols] * steps)
            table_ref[mode, :, cols] = entry
            taps = taps + entry
        first = jnp.sum(weights, axis=0, keepdims=True) + skip_ref[:, cols]
        masked = [jnp.where(row_ids >= lag, taps[lag - 1 : lag, :], 0.0) for lag in range(1, SUB)]
        totals = []
        for sub in range(0, rows, SUB):
            mixed = mixed_ref[sub : sub + SUB, cols]
            total = first * mixed
            for lag in range(1, SUB):
                total = total + masked[lag - 1] * pltpu.roll(mixed, lag, 0)
            totals.append(total)
        for mode in range(modes):
            entry = table_ref[mode, :, cols]
            totals = [
                total + entry * starts_ref[sub, mode : mode + 1, cols] if sub else total
                for sub, total in enumerate(totals)
            ]
        for sub, total in enumerate(totals):
            local_ref[sub * SUB : (sub + 1) * SUB, cols] = total
    move.wait()


def stages(size):
    steps, stride = [], 1
    while stride < size:
        radix = 4 if stride > 1 and size // stride % 4 == 0 else 2
        steps.append((stride, radix))
        stride *= radix
    return steps


def groups_of(paired, rows, arrived_refs, rates):
    states = [arrived_ref[...].astype(F32) for arrived_ref in arrived_refs]
    if paired:
        mine, other, *rest = states
        first = (lax.axis_index("seq") & 1) == 0
        fade = jnp.exp(rates * (-float(rows)))
        states = [fade * jnp.where(first, mine, other) + jnp.where(first, other, mine), *rest]
    return states


def entering(stride, rows, states, rates):
    me = lax.axis_index("seq")
    digit = (me // stride) % (len(states) + 1)
    total = jnp.zeros(rates.shape, F32)
    for index, state in enumerate(states):
        other = digit ^ (index + 1)
        blocks = me % stride + stride * (digit - 1 - other)
        fade = jnp.exp(-rates * (rows * jnp.maximum(blocks, 0)).astype(F32))
        total = total + jnp.where(other < digit, fade, 0.0) * state
    return total


def join_kernel(stride, paired, rows, arrivals, outs, total_ref, rates_ref, *refs):
    arrived_refs, before_refs, out_refs = refs[:arrivals], refs[arrivals:-outs], refs[-outs:]
    rates = rates_ref[...]
    states = groups_of(paired, rows, arrived_refs, rates)
    carry = entering(stride, rows, states, rates)
    for before_ref in before_refs:
        carry = carry + before_ref[...]
    digit = (lax.axis_index("seq") // stride) % (len(states) + 1)
    joined = jnp.zeros(rates.shape, F32)
    for index, state in enumerate((total_ref[...], *states)):
        blocks = stride * (len(states) - (digit ^ index))
        joined = joined + jnp.exp(-rates * (rows * blocks).astype(F32)) * state
    for out_ref, value in zip(out_refs, (carry, joined, joined)):
        out_ref[...] = value.astype(out_ref.dtype)


def gate_kernel(
    piece, stride, paired,
    post_ref, local_ref, table_ref, rates_ref, carry_ref, weight_ref, *refs,
):
    *arrived_refs, gated_ref, first_ref, states_ref = refs
    height, width = gated_ref.shape
    modes = rates_ref.shape[0]
    subs = height // SUB
    base = piece * height
    rates = rates_ref[...]
    states = groups_of(paired, post_ref.shape[0], arrived_refs, rates)
    state = carry_ref[...] + entering(stride, post_ref.shape[0], states, rates)
    if piece:
        state = state * jnp.exp(rates * (-float(base)))
    fade = jnp.exp(rates * (-float(SUB)))
    for sub in range(subs):
        states_ref[sub] = state
        state = state * fade
    product = jnp.zeros(first_ref.shape, F32)
    for lane in range(0, width, LANES):
        cols = slice(lane, lane + LANES)
        totals = [local_ref[base + sub * SUB : base + (sub + 1) * SUB, cols] for sub in range(subs)]
        for mode in range(modes):
            entry = table_ref[mode, :, cols]
            totals = [
                total + entry * states_ref[sub, mode : mode + 1, cols] for sub, total in enumerate(totals)
            ]
        for sub in range(0, subs, 2):
            part = slice(base + sub * SUB, base + (sub + 2) * SUB)
            total = jnp.concatenate(totals[sub : sub + 2], axis=0)
            gated_ref[sub * SUB : (sub + 2) * SUB, cols] = (
                post_ref[part, cols].astype(F32) * total
            ).astype(BF16)
        if (lane + LANES) % DEPTH == 0:
            depth = slice(lane + LANES - DEPTH, lane + LANES)
            product = product + jnp.dot(
                gated_ref[:, depth], weight_ref[depth, :], preferred_element_type=F32
            )
    first_ref[...] = product.astype(BF16)


def project_kernel(offsets, *refs):
    gated_refs, weight_ref, out_refs, gated_ref = refs[:PIECES], refs[PIECES], refs[PIECES + 1 : -1], refs[-1]
    height = gated_refs[0].shape[0]
    for piece in range(PIECES):
        gated_ref[piece * height : (piece + 1) * height, :] = gated_refs[piece][...]
    for slot, offset in enumerate(offsets):
        block = block_of(weight_ref, offset, out_refs[0].shape[1])[...]
        product = jnp.dot(gated_ref[...], block, preferred_element_type=F32)
        for piece in range(PIECES):
            out_ref = out_refs[slot * PIECES + piece]
            out_ref[...] = product[piece * height : (piece + 1) * height, :].astype(out_ref.dtype)


def finish_kernel(*refs):
    *done_refs, kept_ref, arrived_ref, out_hbm, last_ref, sems = refs
    height = kept_ref.shape[0]
    moves = []
    for piece in range(PIECES):
        if piece + 1 == PIECES:
            last_ref[...] = (kept_ref[...] + arrived_ref[...].astype(F32)).astype(BF16)
        moves.append(
            pltpu.make_async_copy(
                (*done_refs, last_ref)[piece],
                out_hbm.at[piece * height : (piece + 1) * height, :],
                sems.at[piece],
            )
        )
        moves[-1].start()
    for move in moves:
        move.wait()


def after(value, *earlier):
    return lax.optimization_barrier((value, *earlier))[0]


def body(post_gate, pre_gate, signal, decay_rates, residues, skip_gain, out_weight):
    rows, width = post_gate.shape
    modes = decay_rates.shape[1]
    subs = rows // SUB
    size = lax.axis_size("seq")
    groups = lax.axis_size("chan")
    columns = out_weight.shape[1] // groups
    height = rows // PIECES
    whole = ((modes, width), F32)
    mixed, starts, end, own, rates, residues, skip, post = call(
        state_kernel,
        [HBM] * 6,
        [
            ((rows, width), F32),
            ((subs, modes, width), F32),
            whole,
            ((modes, width), BF16),
            whole,
            whole,
            ((1, width), F32),
            ((rows, width), BF16),
        ],
        [pltpu.VMEM((rows, width), BF16), pltpu.VMEM((rows, width), BF16), DMA((6,))],
        4 * rows * modes * width,
        8 * rows * width,
    )(pre_gate, signal, decay_rates.T, residues.T, skip_gain.reshape(1, width), post_gate)
    def swap(state, distance):
        return lax.ppermute(state, "seq", [(source, source ^ distance) for source in range(size)])

    levels = stages(size)
    arrived, total, before = [swap(end, 1)], [end], []
    mine = swap(own, 2)
    for level, (stride, radix) in enumerate(levels):
        paired = level == 1
        if paired:
            local, table, weight = call(
                functools.partial(local_kernel, groups - 1),
                [VMEM] * 5 + [HBM],
                [((rows, width), F32), ((modes, SUB, width), F32), ((width, columns), BF16)],
                [DMA],
                2 * rows * (SUB + modes) * width,
                8 * rows * width,
            )(after(mixed, sent), starts, rates, residues, skip, out_weight)
            others = [swap(sent, stride * hop) for hop in range(2, radix)]
            mine = after(mine, others[0], local)
            arrived = [mine, swap(mine, 1)] + others
        elif level:
            arrived = [swap(sent, stride * hop) for hop in range(1, radix)]
        if level + 1 < len(levels):
            outs = [whole, ((modes, width), BF16)] + [whole] * (level + 2 < len(levels))
            carry, sent, *total = call(
                functools.partial(join_kernel, stride, paired, rows, len(arrived), len(outs)),
                [VMEM] * (2 + len(arrived) + len(before)),
                outs,
                [],
                8 * radix * modes * width,
                16 * modes * width,
            )(*total, rates, *arrived, *before)
            before = [carry]

    gated, values = [], {groups - 1: []}
    for piece in range(PIECES):
        half, first = call(
            functools.partial(gate_kernel, piece, stride, paired),
            [VMEM] * (6 + len(arrived)),
            [((height, width), BF16), ((height, columns), BF16)],
            [pltpu.VMEM((subs // PIECES, modes, width), F32)],
            2 * height * modes * width,
            16 * height * width,
        )(post, local, table, rates, carry, weight, *arrived)
        gated.append(half)
        values[groups - 1].append(first)

    offsets = list(range(groups - 2, -1, -1))
    shares = call(
        functools.partial(project_kernel, offsets),
        [VMEM] * (PIECES + 1),
        [((height, columns), BF16 if offset % 2 else F32) for offset in offsets for piece in range(PIECES)],
        [pltpu.VMEM((rows, width), BF16)],
        2 * rows * width * columns * len(offsets),
        2 * width * columns * len(offsets),
    )(*gated, out_weight)
    for slot, offset in enumerate(offsets):
        values[offset] = list(shares[slot * PIECES : (slot + 1) * PIECES])

    sums = []
    for offset in range(groups - 1, 0, -1):
        stride = offset & -offset
        target = offset ^ stride
        pairs = [(source, source ^ stride) for source in range(groups)]
        for piece in range(PIECES):
            index = len(sums)
            sent = values[offset][piece].astype(BF16)
            if index >= 2 * PIECES:
                sent = after(sent, sums[index - 2 * PIECES])
            arrived = lax.ppermute(sent, "chan", pairs)
            kept = values[target][piece]
            if piece:
                kept = after(kept, values[target][piece - 1])
            if offset == 1 and piece + 1 == PIECES:
                break
            values[target][piece] = kept + arrived.astype(F32)
            sums.append(values[target][piece].astype(BF16))
    done = [value.astype(BF16) for value in values[0][:-1]]
    return pl.pallas_call(
        finish_kernel,
        in_specs=[VMEM] * (PIECES + 1),
        out_shape=jax.ShapeDtypeStruct((rows, columns), BF16),
        out_specs=HBM,
        scratch_shapes=[pltpu.VMEM((height, columns), BF16), DMA((PIECES,))],
        compiler_params=pltpu.CompilerParams(vmem_limit_bytes=24 * 2**20),
    )(*done, kept, arrived)


def solution(mesh):
    return jax.shard_map(
        body,
        mesh=mesh,
        in_specs=(
            P("seq", "chan"),
            P("seq", "chan"),
            P("seq", "chan"),
            P("chan", None),
            P("chan", None),
            P("chan"),
            P("chan", None),
        ),
        out_specs=P("seq", "chan"),
        check_vma=False,
    )
```

```python
import functools

import jax
import jax.numpy as jnp
from jax import lax
from jax.experimental import pallas as pl
from jax.experimental.pallas import tpu as pltpu
from jax.sharding import PartitionSpec as P

SUB = 8
LANES = 128
DEPTH = 256
PIECES = 2
F32 = jnp.float32
BF16 = jnp.bfloat16
VMEM = pl.BlockSpec(memory_space=pltpu.VMEM)
HBM = pl.BlockSpec(memory_space=pltpu.HBM)
DMA = pltpu.SemaphoreType.DMA


def call(kernel, ins, outs, scratch, flops, moved):
    run = pl.pallas_call(
        kernel,
        in_specs=ins,
        out_shape=[jax.ShapeDtypeStruct(shape, kind) for shape, kind in outs],
        out_specs=[VMEM] * len(outs),
        scratch_shapes=scratch,
        compiler_params=pltpu.CompilerParams(vmem_limit_bytes=24 * 2**20),
        cost_estimate=pl.CostEstimate(flops=flops, bytes_accessed=moved, transcendentals=0),
    )
    return lambda *operands: run(
        *[
            pltpu.with_memory_space_constraint(operand, pltpu.HBM) if spec is HBM else operand
            for spec, operand in zip(ins, operands)
        ]
    )


def block_of(weight_ref, offset, columns):
    start = pl.multiple_of((lax.axis_index("chan") ^ offset) * columns, LANES)
    return weight_ref.at[:, pl.ds(start, columns)]


def state_kernel(
    pre_hbm, signal_hbm, rates_hbm, residues_hbm, skip_hbm, post_hbm,
    mixed_ref, starts_ref, end_ref, rates_ref, residues_ref, skip_ref, post_ref,
    pre_ref, signal_ref, sems,
):
    moves = [
        pltpu.make_async_copy(source, target, sems.at[index])
        for index, (source, target) in enumerate(
            [
                (pre_hbm, pre_ref),
                (signal_hbm, signal_ref),
                (rates_hbm, rates_ref),
                (residues_hbm, residues_ref),
                (skip_hbm, skip_ref),
                (post_hbm, post_ref),
            ]
        )
    ]
    for move in moves:
        move.start()
    for move in moves[:3]:
        move.wait()
    mixed_ref[...] = pre_ref[...].astype(F32) * signal_ref[...].astype(F32)
    fade = jnp.exp(-rates_ref[...])
    fade_sub = jnp.exp(rates_ref[...] * (-float(SUB)))
    state = jnp.zeros(rates_ref.shape, F32)
    for sub in range(starts_ref.shape[0]):
        starts_ref[sub] = state
        own = fade * mixed_ref[sub * SUB : sub * SUB + 1, :]
        for token in range(sub * SUB + 1, (sub + 1) * SUB - 1):
            own = fade * (own + mixed_ref[token : token + 1, :])
        state = fade_sub * state + (own + mixed_ref[(sub + 1) * SUB - 1 : (sub + 1) * SUB, :])
    end_ref[...] = state
    for move in moves[3:]:
        move.wait()


def local_kernel(
    offset, mixed_ref, starts_ref, rates_ref, residues_ref, skip_ref, weight_hbm,
    local_ref, table_ref, weight_ref,
    sem,
):
    move = pltpu.make_async_copy(block_of(weight_hbm, offset, weight_ref.shape[1]), weight_ref, sem)
    move.start()
    rows, width = mixed_ref.shape
    modes = rates_ref.shape[0]
    row_ids = lax.broadcasted_iota(jnp.int32, (SUB, LANES), 0)
    steps = row_ids.astype(F32) + 1.0
    for lane in range(0, width, LANES):
        cols = slice(lane, lane + LANES)
        weights = residues_ref[:, cols] * jnp.sqrt(2.0 * rates_ref[:, cols])
        taps = jnp.zeros((SUB, LANES), F32)
        for mode in range(modes):
            entry = weights[mode : mode + 1, :] * jnp.exp(-rates_ref[mode : mode + 1, cols] * steps)
            table_ref[mode, :, cols] = entry
            taps = taps + entry
        first = jnp.sum(weights, axis=0, keepdims=True) + skip_ref[:, cols]
        masked = [jnp.where(row_ids >= lag, taps[lag - 1 : lag, :], 0.0) for lag in range(1, SUB)]
        totals = []
        for sub in range(0, rows, SUB):
            mixed = mixed_ref[sub : sub + SUB, cols]
            total = first * mixed
            for lag in range(1, SUB):
                total = total + masked[lag - 1] * pltpu.roll(mixed, lag, 0)
            totals.append(total)
        for mode in range(modes):
            entry = table_ref[mode, :, cols]
            totals = [
                total + entry * starts_ref[sub, mode : mode + 1, cols] if sub else total
                for sub, total in enumerate(totals)
            ]
        for sub, total in enumerate(totals):
            local_ref[sub * SUB : (sub + 1) * SUB, cols] = total
    move.wait()


def stages(size):
    steps, stride = [], 1
    while stride < size:
        radix = 4 if stride > 1 and size // stride % 4 == 0 else 2
        steps.append((stride, radix))
        stride *= radix
    return steps


def entering(stride, rows, states, rates):
    me = lax.axis_index("seq")
    digit = (me // stride) % (len(states) + 1)
    total = jnp.zeros(rates.shape, F32)
    for index, state in enumerate(states):
        other = digit ^ (index + 1)
        blocks = me % stride + stride * (digit - 1 - other)
        fade = jnp.exp(-rates * (rows * jnp.maximum(blocks, 0)).astype(F32))
        total = total + jnp.where(other < digit, fade, 0.0) * state
    return total


def join_kernel(stride, rows, arrivals, outs, total_ref, rates_ref, *refs):
    arrived_refs, before_refs, out_refs = refs[:arrivals], refs[arrivals:-outs], refs[-outs:]
    rates = rates_ref[...]
    states = [arrived_ref[...].astype(F32) for arrived_ref in arrived_refs[::-1]]
    carry = entering(stride, rows, states, rates)
    for before_ref in before_refs:
        carry = carry + before_ref[...]
    digit = (lax.axis_index("seq") // stride) % (len(states) + 1)
    joined = jnp.zeros(rates.shape, F32)
    for index, state in enumerate((total_ref[...], *states)):
        blocks = stride * (len(states) - (digit ^ index))
        joined = joined + jnp.exp(-rates * (rows * blocks).astype(F32)) * state
    for out_ref, value in zip(out_refs, (carry, joined, joined)):
        out_ref[...] = value.astype(out_ref.dtype)


def gate_kernel(
    piece, stride,
    post_ref, local_ref, table_ref, rates_ref, carry_ref, weight_ref, *refs,
):
    *arrived_refs, gated_ref, first_ref, states_ref = refs
    height, width = gated_ref.shape
    modes = rates_ref.shape[0]
    subs = height // SUB
    base = piece * height
    rates = rates_ref[...]
    states = [arrived_ref[...].astype(F32) for arrived_ref in arrived_refs[::-1]]
    state = carry_ref[...] + entering(stride, post_ref.shape[0], states, rates)
    if piece:
        state = state * jnp.exp(rates * (-float(base)))
    fade = jnp.exp(rates * (-float(SUB)))
    for sub in range(subs):
        states_ref[sub] = state
        state = state * fade
    product = jnp.zeros(first_ref.shape, F32)
    for lane in range(0, width, LANES):
        cols = slice(lane, lane + LANES)
        totals = [local_ref[base + sub * SUB : base + (sub + 1) * SUB, cols] for sub in range(subs)]
        for mode in range(modes):
            entry = table_ref[mode, :, cols]
            totals = [
                total + entry * states_ref[sub, mode : mode + 1, cols] for sub, total in enumerate(totals)
            ]
        for sub in range(0, subs, 2):
            part = slice(base + sub * SUB, base + (sub + 2) * SUB)
            total = jnp.concatenate(totals[sub : sub + 2], axis=0)
            gated_ref[sub * SUB : (sub + 2) * SUB, cols] = (
                post_ref[part, cols].astype(F32) * total
            ).astype(BF16)
        if (lane + LANES) % DEPTH == 0:
            depth = slice(lane + LANES - DEPTH, lane + LANES)
            product = product + jnp.dot(
                gated_ref[:, depth], weight_ref[depth, :], preferred_element_type=F32
            )
    first_ref[...] = product.astype(BF16)


def project_kernel(offsets, *refs):
    gated_refs, weight_ref, out_refs, gated_ref = refs[:PIECES], refs[PIECES], refs[PIECES + 1 : -1], refs[-1]
    height = gated_refs[0].shape[0]
    for piece in range(PIECES):
        gated_ref[piece * height : (piece + 1) * height, :] = gated_refs[piece][...]
    for slot, offset in enumerate(offsets):
        block = block_of(weight_ref, offset, out_refs[0].shape[1])[...]
        product = jnp.dot(gated_ref[...], block, preferred_element_type=F32)
        for piece in range(PIECES):
            out_ref = out_refs[slot * PIECES + piece]
            out_ref[...] = product[piece * height : (piece + 1) * height, :].astype(out_ref.dtype)


def finish_kernel(*refs):
    *done_refs, kept_ref, arrived_ref, out_hbm, last_ref, sems = refs
    height = kept_ref.shape[0]
    moves = []
    for piece in range(PIECES):
        if piece + 1 == PIECES:
            last_ref[...] = (kept_ref[...] + arrived_ref[...].astype(F32)).astype(BF16)
        moves.append(
            pltpu.make_async_copy(
                (*done_refs, last_ref)[piece],
                out_hbm.at[piece * height : (piece + 1) * height, :],
                sems.at[piece],
            )
        )
        moves[-1].start()
    for move in moves:
        move.wait()


def after(value, *earlier):
    return lax.optimization_barrier((value, *earlier))[0]


def body(post_gate, pre_gate, signal, decay_rates, residues, skip_gain, out_weight):
    rows, width = post_gate.shape
    modes = decay_rates.shape[1]
    subs = rows // SUB
    size = lax.axis_size("seq")
    groups = lax.axis_size("chan")
    columns = out_weight.shape[1] // groups
    height = rows // PIECES
    whole = ((modes, width), F32)
    mixed, starts, end, rates, residues, skip, post = call(
        state_kernel,
        [HBM] * 6,
        [
            ((rows, width), F32),
            ((subs, modes, width), F32),
            whole,
            whole,
            whole,
            ((1, width), F32),
            ((rows, width), BF16),
        ],
        [pltpu.VMEM((rows, width), BF16), pltpu.VMEM((rows, width), BF16), DMA((6,))],
        4 * rows * modes * width,
        8 * rows * width,
    )(pre_gate, signal, decay_rates.T, residues.T, skip_gain.reshape(1, width), post_gate)
    def swap(state, distance):
        return lax.ppermute(state, "seq", [(source, source ^ distance) for source in range(size)])

    levels = stages(size)
    arrived, total, before = [swap(end, 1)], [end], []
    for level, (stride, radix) in enumerate(levels):
        if level:
            arrived = [swap(sent, stride * hop) for hop in range(radix - 1, 0, -1)]
        if level + 1 < len(levels):
            outs = [whole, ((modes, width), BF16)] + [whole] * (level + 2 < len(levels))
            carry, sent, *total = call(
                functools.partial(join_kernel, stride, rows, len(arrived), len(outs)),
                [VMEM] * (2 + len(arrived) + len(before)),
                outs,
                [],
                8 * radix * modes * width,
                16 * modes * width,
            )(*total, rates, *arrived, *before)
            before = [carry]
    local, table, weight = call(
        functools.partial(local_kernel, groups - 1),
        [VMEM] * 5 + [HBM],
        [((rows, width), F32), ((modes, SUB, width), F32), ((width, columns), BF16)],
        [DMA],
        2 * rows * (SUB + modes) * width,
        8 * rows * width,
    )(after(mixed, sent), starts, rates, residues, skip, out_weight)
    arrived[0] = after(arrived[0], local)

    gated, values = [], {groups - 1: []}
    for piece in range(PIECES):
        half, first = call(
            functools.partial(gate_kernel, piece, stride),
            [VMEM] * (6 + len(arrived)),
            [((height, width), BF16), ((height, columns), BF16)],
            [pltpu.VMEM((subs // PIECES, modes, width), F32)],
            2 * height * modes * width,
            16 * height * width,
        )(post, local, table, rates, carry, weight, *arrived)
        gated.append(half)
        values[groups - 1].append(first)

    offsets = list(range(groups - 2, -1, -1))
    shares = call(
        functools.partial(project_kernel, offsets),
        [VMEM] * (PIECES + 1),
        [((height, columns), BF16 if offset % 2 else F32) for offset in offsets for piece in range(PIECES)],
        [pltpu.VMEM((rows, width), BF16)],
        2 * rows * width * columns * len(offsets),
        2 * width * columns * len(offsets),
    )(*gated, out_weight)
    for slot, offset in enumerate(offsets):
        values[offset] = list(shares[slot * PIECES : (slot + 1) * PIECES])

    sums = []
    for offset in range(groups - 1, 0, -1):
        stride = offset & -offset
        target = offset ^ stride
        pairs = [(source, source ^ stride) for source in range(groups)]
        for piece in range(PIECES):
            index = len(sums)
            sent = values[offset][piece].astype(BF16)
            if index >= 2 * PIECES:
                sent = after(sent, sums[index - 2 * PIECES])
            arrived = lax.ppermute(sent, "chan", pairs)
            kept = values[target][piece]
            if piece:
                kept = after(kept, values[target][piece - 1])
            if offset == 1 and piece + 1 == PIECES:
                break
            values[target][piece] = kept + arrived.astype(F32)
            sums.append(values[target][piece].astype(BF16))
    done = [value.astype(BF16) for value in values[0][:-1]]
    return pl.pallas_call(
        finish_kernel,
        in_specs=[VMEM] * (PIECES + 1),
        out_shape=jax.ShapeDtypeStruct((rows, columns), BF16),
        out_specs=HBM,
        scratch_shapes=[pltpu.VMEM((height, columns), BF16), DMA((PIECES,))],
        compiler_params=pltpu.CompilerParams(vmem_limit_bytes=24 * 2**20),
    )(*done, kept, arrived)


def solution(mesh):
    return jax.shard_map(
        body,
        mesh=mesh,
        in_specs=(
            P("seq", "chan"),
            P("seq", "chan"),
            P("seq", "chan"),
            P("chan", None),
            P("chan", None),
            P("chan"),
            P("chan", None),
        ),
        out_specs=P("seq", "chan"),
        check_vma=False,
    )
```

```python
import functools

import jax
import jax.numpy as jnp
from jax import lax
from jax.experimental import pallas as pl
from jax.experimental.pallas import tpu as pltpu
from jax.sharding import PartitionSpec as P

SUB = 8
LANES = 128
DEPTH = 256
PIECES = 2
F32 = jnp.float32
BF16 = jnp.bfloat16
VMEM = pl.BlockSpec(memory_space=pltpu.VMEM)
HBM = pl.BlockSpec(memory_space=pltpu.HBM)
DMA = pltpu.SemaphoreType.DMA


def call(kernel, ins, outs, scratch, flops, moved):
    run = pl.pallas_call(
        kernel,
        in_specs=ins,
        out_shape=[jax.ShapeDtypeStruct(shape, kind) for shape, kind in outs],
        out_specs=[VMEM] * len(outs),
        scratch_shapes=scratch,
        compiler_params=pltpu.CompilerParams(vmem_limit_bytes=24 * 2**20),
        cost_estimate=pl.CostEstimate(flops=flops, bytes_accessed=moved, transcendentals=0),
    )
    return lambda *operands: run(
        *[
            pltpu.with_memory_space_constraint(operand, pltpu.HBM) if spec is HBM else operand
            for spec, operand in zip(ins, operands)
        ]
    )


def block_of(weight_ref, offset, columns):
    start = pl.multiple_of((lax.axis_index("chan") ^ offset) * columns, LANES)
    return weight_ref.at[:, pl.ds(start, columns)]


def state_kernel(
    pre_hbm, signal_hbm, rates_hbm, residues_hbm, skip_hbm, post_hbm,
    mixed_ref, starts_ref, end_ref, rates_ref, residues_ref, skip_ref, post_ref,
    pre_ref, signal_ref, sems,
):
    moves = [
        pltpu.make_async_copy(source, target, sems.at[index])
        for index, (source, target) in enumerate(
            [
                (pre_hbm, pre_ref),
                (signal_hbm, signal_ref),
                (rates_hbm, rates_ref),
                (residues_hbm, residues_ref),
                (skip_hbm, skip_ref),
                (post_hbm, post_ref),
            ]
        )
    ]
    for move in moves:
        move.start()
    for move in moves[:3]:
        move.wait()
    for lane in range(0, rates_ref.shape[1], LANES):
        cols = slice(lane, lane + LANES)
        mixed_ref[:, cols] = pre_ref[:, cols].astype(F32) * signal_ref[:, cols].astype(F32)
        fade = jnp.exp(-rates_ref[:, cols])
        fade_sub = jnp.exp(rates_ref[:, cols] * (-float(SUB)))
        state = jnp.zeros(fade.shape, F32)
        for sub in range(starts_ref.shape[0]):
            starts_ref[sub, :, cols] = state
            base = sub * SUB
            own = fade * mixed_ref[base : base + 1, cols]
            for token in range(base + 1, base + SUB - 1):
                own = fade * (own + mixed_ref[token : token + 1, cols])
            state = fade_sub * state + (own + mixed_ref[base + SUB - 1 : base + SUB, cols])
        end_ref[:, cols] = state
    for move in moves[3:]:
        move.wait()


def local_kernel(
    offset, mixed_ref, starts_ref, rates_ref, residues_ref, skip_ref, weight_hbm,
    local_ref, table_ref, weight_ref,
    sem,
):
    move = pltpu.make_async_copy(block_of(weight_hbm, offset, weight_ref.shape[1]), weight_ref, sem)
    move.start()
    rows, width = mixed_ref.shape
    modes = rates_ref.shape[0]
    row_ids = lax.broadcasted_iota(jnp.int32, (SUB, LANES), 0)
    steps = row_ids.astype(F32) + 1.0
    for lane in range(0, width, LANES):
        cols = slice(lane, lane + LANES)
        weights = residues_ref[:, cols] * jnp.sqrt(2.0 * rates_ref[:, cols])
        taps = jnp.zeros((SUB, LANES), F32)
        for mode in range(modes):
            entry = weights[mode : mode + 1, :] * jnp.exp(-rates_ref[mode : mode + 1, cols] * steps)
            table_ref[mode, :, cols] = entry
            taps = taps + entry
        first = jnp.sum(weights, axis=0, keepdims=True) + skip_ref[:, cols]
        masked = [jnp.where(row_ids >= lag, taps[lag - 1 : lag, :], 0.0) for lag in range(1, SUB)]
        totals = []
        for sub in range(0, rows, SUB):
            mixed = mixed_ref[sub : sub + SUB, cols]
            total = first * mixed
            for lag in range(1, SUB):
                total = total + masked[lag - 1] * pltpu.roll(mixed, lag, 0)
            totals.append(total)
        for mode in range(modes):
            entry = table_ref[mode, :, cols]
            totals = [
                total + entry * starts_ref[sub, mode : mode + 1, cols] if sub else total
                for sub, total in enumerate(totals)
            ]
        for sub, total in enumerate(totals):
            local_ref[sub * SUB : (sub + 1) * SUB, cols] = total
    move.wait()


def stages(size):
    steps, stride = [], 1
    while stride < size:
        radix = 4 if stride > 1 and size // stride % 4 == 0 else 2
        steps.append((stride, radix))
        stride *= radix
    return steps


def entering(stride, rows, states, rates):
    me = lax.axis_index("seq")
    digit = (me // stride) % (len(states) + 1)
    total = jnp.zeros(rates.shape, F32)
    for index, state in enumerate(states):
        other = digit ^ (index + 1)
        blocks = me % stride + stride * (digit - 1 - other)
        fade = jnp.exp(-rates * (rows * jnp.maximum(blocks, 0)).astype(F32))
        total = total + jnp.where(other < digit, fade, 0.0) * state
    return total


def join_kernel(stride, rows, arrivals, outs, total_ref, rates_ref, *refs):
    arrived_refs, before_refs, out_refs = refs[:arrivals], refs[arrivals:-outs], refs[-outs:]
    rates = rates_ref[...]
    states = [arrived_ref[...].astype(F32) for arrived_ref in arrived_refs[::-1]]
    carry = entering(stride, rows, states, rates)
    for before_ref in before_refs:
        carry = carry + before_ref[...]
    digit = (lax.axis_index("seq") // stride) % (len(states) + 1)
    joined = jnp.zeros(rates.shape, F32)
    for index, state in enumerate((total_ref[...], *states)):
        blocks = stride * (len(states) - (digit ^ index))
        joined = joined + jnp.exp(-rates * (rows * blocks).astype(F32)) * state
    for out_ref, value in zip(out_refs, (carry, joined, joined)):
        out_ref[...] = value.astype(out_ref.dtype)


def gate_kernel(
    piece, stride,
    post_ref, local_ref, table_ref, rates_ref, carry_ref, weight_ref, *refs,
):
    *arrived_refs, gated_ref, first_ref, states_ref = refs
    height, width = gated_ref.shape
    modes = rates_ref.shape[0]
    subs = height // SUB
    base = piece * height
    rates = rates_ref[...]
    states = [arrived_ref[...].astype(F32) for arrived_ref in arrived_refs[::-1]]
    state = carry_ref[...] + entering(stride, post_ref.shape[0], states, rates)
    if piece:
        state = state * jnp.exp(rates * (-float(base)))
    fade = jnp.exp(rates * (-float(SUB)))
    for sub in range(subs):
        states_ref[sub] = state
        state = state * fade
    product = jnp.zeros(first_ref.shape, F32)
    for lane in range(0, width, LANES):
        cols = slice(lane, lane + LANES)
        totals = [local_ref[base + sub * SUB : base + (sub + 1) * SUB, cols] for sub in range(subs)]
        for mode in range(modes):
            entry = table_ref[mode, :, cols]
            totals = [
                total + entry * states_ref[sub, mode : mode + 1, cols] for sub, total in enumerate(totals)
            ]
        for sub in range(0, subs, 2):
            part = slice(base + sub * SUB, base + (sub + 2) * SUB)
            total = jnp.concatenate(totals[sub : sub + 2], axis=0)
            gated_ref[sub * SUB : (sub + 2) * SUB, cols] = (
                post_ref[part, cols].astype(F32) * total
            ).astype(BF16)
        if (lane + LANES) % DEPTH == 0:
            depth = slice(lane + LANES - DEPTH, lane + LANES)
            product = product + jnp.dot(
                gated_ref[:, depth], weight_ref[depth, :], preferred_element_type=F32
            )
    first_ref[...] = product.astype(BF16)


def project_kernel(offsets, *refs):
    gated_refs, weight_ref, out_refs, gated_ref = refs[:PIECES], refs[PIECES], refs[PIECES + 1 : -1], refs[-1]
    height = gated_refs[0].shape[0]
    for piece in range(PIECES):
        gated_ref[piece * height : (piece + 1) * height, :] = gated_refs[piece][...]
    for slot, offset in enumerate(offsets):
        block = block_of(weight_ref, offset, out_refs[0].shape[1])[...]
        product = jnp.dot(gated_ref[...], block, preferred_element_type=F32)
        for piece in range(PIECES):
            out_ref = out_refs[slot * PIECES + piece]
            out_ref[...] = product[piece * height : (piece + 1) * height, :].astype(out_ref.dtype)


def finish_kernel(*refs):
    *done_refs, kept_ref, arrived_ref, out_hbm, last_ref, sems = refs
    height = kept_ref.shape[0]
    moves = []
    for piece in range(PIECES):
        if piece + 1 == PIECES:
            last_ref[...] = (kept_ref[...] + arrived_ref[...].astype(F32)).astype(BF16)
        moves.append(
            pltpu.make_async_copy(
                (*done_refs, last_ref)[piece],
                out_hbm.at[piece * height : (piece + 1) * height, :],
                sems.at[piece],
            )
        )
        moves[-1].start()
    for move in moves:
        move.wait()


def after(value, *earlier):
    return lax.optimization_barrier((value, *earlier))[0]


def body(post_gate, pre_gate, signal, decay_rates, residues, skip_gain, out_weight):
    rows, width = post_gate.shape
    modes = decay_rates.shape[1]
    subs = rows // SUB
    size = lax.axis_size("seq")
    groups = lax.axis_size("chan")
    columns = out_weight.shape[1] // groups
    height = rows // PIECES
    whole = ((modes, width), F32)
    mixed, starts, end, rates, residues, skip, post = call(
        state_kernel,
        [HBM] * 6,
        [
            ((rows, width), F32),
            ((subs, modes, width), F32),
            whole,
            whole,
            whole,
            ((1, width), F32),
            ((rows, width), BF16),
        ],
        [pltpu.VMEM((rows, width), BF16), pltpu.VMEM((rows, width), BF16), DMA((6,))],
        4 * rows * modes * width,
        8 * rows * width,
    )(pre_gate, signal, decay_rates.T, residues.T, skip_gain.reshape(1, width), post_gate)
    def swap(state, distance):
        return lax.ppermute(state, "seq", [(source, source ^ distance) for source in range(size)])

    levels = stages(size)
    arrived, total, before = [swap(end, 1)], [end], []
    for level, (stride, radix) in enumerate(levels):
        if level:
            arrived = [swap(sent, stride * hop) for hop in range(radix - 1, 0, -1)]
        if level + 1 < len(levels):
            outs = [whole, ((modes, width), BF16)] + [whole] * (level + 2 < len(levels))
            carry, sent, *total = call(
                functools.partial(join_kernel, stride, rows, len(arrived), len(outs)),
                [VMEM] * (2 + len(arrived) + len(before)),
                outs,
                [],
                8 * radix * modes * width,
                16 * modes * width,
            )(*total, rates, *arrived, *before)
            before = [carry]
    local, table, weight = call(
        functools.partial(local_kernel, groups - 1),
        [VMEM] * 5 + [HBM],
        [((rows, width), F32), ((modes, SUB, width), F32), ((width, columns), BF16)],
        [DMA],
        2 * rows * (SUB + modes) * width,
        8 * rows * width,
    )(after(mixed, sent), starts, rates, residues, skip, out_weight)
    arrived[0] = after(arrived[0], local)

    gated, values = [], {groups - 1: []}
    for piece in range(PIECES):
        half, first = call(
            functools.partial(gate_kernel, piece, stride),
            [VMEM] * (6 + len(arrived)),
            [((height, width), BF16), ((height, columns), BF16)],
            [pltpu.VMEM((subs // PIECES, modes, width), F32)],
            2 * height * modes * width,
            16 * height * width,
        )(post, local, table, rates, carry, weight, *arrived)
        gated.append(half)
        values[groups - 1].append(first)

    offsets = list(range(groups - 2, -1, -1))
    shares = call(
        functools.partial(project_kernel, offsets),
        [VMEM] * (PIECES + 1),
        [((height, columns), BF16 if offset % 2 else F32) for offset in offsets for piece in range(PIECES)],
        [pltpu.VMEM((rows, width), BF16)],
        2 * rows * width * columns * len(offsets),
        2 * width * columns * len(offsets),
    )(*gated, out_weight)
    for slot, offset in enumerate(offsets):
        values[offset] = list(shares[slot * PIECES : (slot + 1) * PIECES])

    sums = []
    for offset in range(groups - 1, 0, -1):
        stride = offset & -offset
        target = offset ^ stride
        pairs = [(source, source ^ stride) for source in range(groups)]
        for piece in range(PIECES):
            index = len(sums)
            sent = values[offset][piece].astype(BF16)
            if index >= 2 * PIECES:
                sent = after(sent, sums[index - 2 * PIECES])
            arrived = lax.ppermute(sent, "chan", pairs)
            kept = values[target][piece]
            if piece:
                kept = after(kept, values[target][piece - 1])
            if offset == 1 and piece + 1 == PIECES:
                break
            values[target][piece] = kept + arrived.astype(F32)
            sums.append(values[target][piece].astype(BF16))
    done = [value.astype(BF16) for value in values[0][:-1]]
    return pl.pallas_call(
        finish_kernel,
        in_specs=[VMEM] * (PIECES + 1),
        out_shape=jax.ShapeDtypeStruct((rows, columns), BF16),
        out_specs=HBM,
        scratch_shapes=[pltpu.VMEM((height, columns), BF16), DMA((PIECES,))],
        compiler_params=pltpu.CompilerParams(vmem_limit_bytes=24 * 2**20),
    )(*done, kept, arrived)


def solution(mesh):
    return jax.shard_map(
        body,
        mesh=mesh,
        in_specs=(
            P("seq", "chan"),
            P("seq", "chan"),
            P("seq", "chan"),
            P("chan", None),
            P("chan", None),
            P("chan"),
            P("chan", None),
        ),
        out_specs=P("seq", "chan"),
        check_vma=False,
    )
```

```python
import functools

import jax
import jax.numpy as jnp
from jax import lax
from jax.experimental import pallas as pl
from jax.experimental.pallas import tpu as pltpu
from jax.sharding import PartitionSpec as P

SUB = 8
LANES = 128
DEPTH = 256
PIECES = 2
F32 = jnp.float32
BF16 = jnp.bfloat16
VMEM = pl.BlockSpec(memory_space=pltpu.VMEM)
HBM = pl.BlockSpec(memory_space=pltpu.HBM)
DMA = pltpu.SemaphoreType.DMA


def call(kernel, ins, outs, scratch, flops, moved):
    run = pl.pallas_call(
        kernel,
        in_specs=ins,
        out_shape=[jax.ShapeDtypeStruct(shape, kind) for shape, kind in outs],
        out_specs=[VMEM] * len(outs),
        scratch_shapes=scratch,
        compiler_params=pltpu.CompilerParams(vmem_limit_bytes=24 * 2**20),
        cost_estimate=pl.CostEstimate(flops=flops, bytes_accessed=moved, transcendentals=0),
    )
    return lambda *operands: run(
        *[
            pltpu.with_memory_space_constraint(operand, pltpu.HBM) if spec is HBM else operand
            for spec, operand in zip(ins, operands)
        ]
    )


def spans_of(rows):
    cut = rows * 5 // 8
    return [slice(0, cut), slice(cut, rows)]


def block_of(weight_ref, offset, columns):
    start = pl.multiple_of((lax.axis_index("chan") ^ offset) * columns, LANES)
    return weight_ref.at[:, pl.ds(start, columns)]


def state_kernel(
    pre_hbm, signal_hbm, rates_hbm, residues_hbm, skip_hbm, post_hbm,
    mixed_ref, starts_ref, end_ref, rates_ref, residues_ref, skip_ref, post_ref,
    pre_ref, signal_ref, sems,
):
    moves = [
        pltpu.make_async_copy(source, target, sems.at[index])
        for index, (source, target) in enumerate(
            [
                (pre_hbm, pre_ref),
                (signal_hbm, signal_ref),
                (rates_hbm, rates_ref),
                (residues_hbm, residues_ref),
                (skip_hbm, skip_ref),
                (post_hbm, post_ref),
            ]
        )
    ]
    for move in moves:
        move.start()
    for move in moves[:3]:
        move.wait()
    for lane in range(0, rates_ref.shape[1], LANES):
        cols = slice(lane, lane + LANES)
        mixed_ref[:, cols] = pre_ref[:, cols].astype(F32) * signal_ref[:, cols].astype(F32)
        fade = jnp.exp(-rates_ref[:, cols])
        fade_sub = jnp.exp(rates_ref[:, cols] * (-float(SUB)))
        state = jnp.zeros(fade.shape, F32)
        for sub in range(starts_ref.shape[0]):
            starts_ref[sub, :, cols] = state
            base = sub * SUB
            own = fade * mixed_ref[base : base + 1, cols]
            for token in range(base + 1, base + SUB - 1):
                own = fade * (own + mixed_ref[token : token + 1, cols])
            state = fade_sub * state + (own + mixed_ref[base + SUB - 1 : base + SUB, cols])
        end_ref[:, cols] = state
    for move in moves[3:]:
        move.wait()


def local_kernel(
    offset, mixed_ref, starts_ref, rates_ref, residues_ref, skip_ref, weight_hbm,
    local_ref, table_ref, weight_ref,
    sem,
):
    move = pltpu.make_async_copy(block_of(weight_hbm, offset, weight_ref.shape[1]), weight_ref, sem)
    move.start()
    rows, width = mixed_ref.shape
    modes = rates_ref.shape[0]
    row_ids = lax.broadcasted_iota(jnp.int32, (SUB, LANES), 0)
    steps = row_ids.astype(F32) + 1.0
    for lane in range(0, width, LANES):
        cols = slice(lane, lane + LANES)
        weights = residues_ref[:, cols] * jnp.sqrt(2.0 * rates_ref[:, cols])
        taps = jnp.zeros((SUB, LANES), F32)
        for mode in range(modes):
            entry = weights[mode : mode + 1, :] * jnp.exp(-rates_ref[mode : mode + 1, cols] * steps)
            table_ref[mode, :, cols] = entry
            taps = taps + entry
        first = jnp.sum(weights, axis=0, keepdims=True) + skip_ref[:, cols]
        masked = [jnp.where(row_ids >= lag, taps[lag - 1 : lag, :], 0.0) for lag in range(1, SUB)]
        totals = []
        for sub in range(0, rows, SUB):
            mixed = mixed_ref[sub : sub + SUB, cols]
            total = first * mixed
            for lag in range(1, SUB):
                total = total + masked[lag - 1] * pltpu.roll(mixed, lag, 0)
            totals.append(total)
        for mode in range(modes):
            entry = table_ref[mode, :, cols]
            totals = [
                total + entry * starts_ref[sub, mode : mode + 1, cols] if sub else total
                for sub, total in enumerate(totals)
            ]
        for sub, total in enumerate(totals):
            local_ref[sub * SUB : (sub + 1) * SUB, cols] = total
    move.wait()


def stages(size):
    steps, stride = [], 1
    while stride < size:
        radix = 4 if stride > 1 and size // stride % 4 == 0 else 2
        steps.append((stride, radix))
        stride *= radix
    return steps


def entering(stride, rows, states, rates):
    me = lax.axis_index("seq")
    digit = (me // stride) % (len(states) + 1)
    total = jnp.zeros(rates.shape, F32)
    for index, state in enumerate(states):
        other = digit ^ (index + 1)
        blocks = me % stride + stride * (digit - 1 - other)
        fade = jnp.exp(-rates * (rows * jnp.maximum(blocks, 0)).astype(F32))
        total = total + jnp.where(other < digit, fade, 0.0) * state
    return total


def join_kernel(stride, rows, arrivals, outs, total_ref, rates_ref, *refs):
    arrived_refs, before_refs, out_refs = refs[:arrivals], refs[arrivals:-outs], refs[-outs:]
    rates = rates_ref[...]
    states = [arrived_ref[...].astype(F32) for arrived_ref in arrived_refs[::-1]]
    carry = entering(stride, rows, states, rates)
    for before_ref in before_refs:
        carry = carry + before_ref[...]
    digit = (lax.axis_index("seq") // stride) % (len(states) + 1)
    joined = jnp.zeros(rates.shape, F32)
    for index, state in enumerate((total_ref[...], *states)):
        blocks = stride * (len(states) - (digit ^ index))
        joined = joined + jnp.exp(-rates * (rows * blocks).astype(F32)) * state
    for out_ref, value in zip(out_refs, (carry, joined, joined)):
        out_ref[...] = value.astype(out_ref.dtype)


def gate_kernel(
    base, stride,
    post_ref, local_ref, table_ref, rates_ref, carry_ref, weight_ref, *refs,
):
    *arrived_refs, gated_ref, first_ref, states_ref = refs
    height, width = gated_ref.shape
    modes = rates_ref.shape[0]
    subs = height // SUB
    rates = rates_ref[...]
    states = [arrived_ref[...].astype(F32) for arrived_ref in arrived_refs[::-1]]
    state = carry_ref[...] + entering(stride, post_ref.shape[0], states, rates)
    if base:
        state = state * jnp.exp(rates * (-float(base)))
    fade = jnp.exp(rates * (-float(SUB)))
    for sub in range(subs):
        states_ref[sub] = state
        state = state * fade
    product = jnp.zeros(first_ref.shape, F32)
    for lane in range(0, width, LANES):
        cols = slice(lane, lane + LANES)
        totals = [local_ref[base + sub * SUB : base + (sub + 1) * SUB, cols] for sub in range(subs)]
        for mode in range(modes):
            entry = table_ref[mode, :, cols]
            totals = [
                total + entry * states_ref[sub, mode : mode + 1, cols] for sub, total in enumerate(totals)
            ]
        for sub in range(0, subs, 2):
            part = slice(base + sub * SUB, base + (sub + 2) * SUB)
            total = jnp.concatenate(totals[sub : sub + 2], axis=0)
            gated_ref[sub * SUB : (sub + 2) * SUB, cols] = (
                post_ref[part, cols].astype(F32) * total
            ).astype(BF16)
        if (lane + LANES) % DEPTH == 0:
            depth = slice(lane + LANES - DEPTH, lane + LANES)
            product = product + jnp.dot(
                gated_ref[:, depth], weight_ref[depth, :], preferred_element_type=F32
            )
    first_ref[...] = product.astype(BF16)


def project_kernel(offsets, *refs):
    gated_refs, weight_ref, out_refs, gated_ref = refs[:PIECES], refs[PIECES], refs[PIECES + 1 : -1], refs[-1]
    spans = spans_of(gated_ref.shape[0])
    for span, half_ref in zip(spans, gated_refs):
        gated_ref[span, :] = half_ref[...]
    for slot, offset in enumerate(offsets):
        block = block_of(weight_ref, offset, out_refs[0].shape[1])[...]
        product = jnp.dot(gated_ref[...], block, preferred_element_type=F32)
        for piece, span in enumerate(spans):
            out_ref = out_refs[slot * PIECES + piece]
            out_ref[...] = product[span, :].astype(out_ref.dtype)


def finish_kernel(*refs):
    *done_refs, kept_ref, arrived_ref, out_hbm, last_ref, sems = refs
    moves = []
    for piece, span in enumerate(spans_of(out_hbm.shape[0])):
        if piece + 1 == PIECES:
            last_ref[...] = (kept_ref[...] + arrived_ref[...].astype(F32)).astype(BF16)
        moves.append(
            pltpu.make_async_copy(
                (*done_refs, last_ref)[piece],
                out_hbm.at[span, :],
                sems.at[piece],
            )
        )
        moves[-1].start()
    for move in moves:
        move.wait()


def after(value, *earlier):
    return lax.optimization_barrier((value, *earlier))[0]


def body(post_gate, pre_gate, signal, decay_rates, residues, skip_gain, out_weight):
    rows, width = post_gate.shape
    modes = decay_rates.shape[1]
    subs = rows // SUB
    size = lax.axis_size("seq")
    groups = lax.axis_size("chan")
    columns = out_weight.shape[1] // groups
    spans = spans_of(rows)
    heights = [span.stop - span.start for span in spans]
    whole = ((modes, width), F32)
    mixed, starts, end, rates, residues, skip, post = call(
        state_kernel,
        [HBM] * 6,
        [
            ((rows, width), F32),
            ((subs, modes, width), F32),
            whole,
            whole,
            whole,
            ((1, width), F32),
            ((rows, width), BF16),
        ],
        [pltpu.VMEM((rows, width), BF16), pltpu.VMEM((rows, width), BF16), DMA((6,))],
        4 * rows * modes * width,
        8 * rows * width,
    )(pre_gate, signal, decay_rates.T, residues.T, skip_gain.reshape(1, width), post_gate)
    def swap(state, distance):
        return lax.ppermute(state, "seq", [(source, source ^ distance) for source in range(size)])

    levels = stages(size)
    arrived, total, before = [swap(end, 1)], [end], []
    for level, (stride, radix) in enumerate(levels):
        if level:
            arrived = [swap(sent, stride * hop) for hop in range(radix - 1, 0, -1)]
        if level + 1 < len(levels):
            outs = [whole, ((modes, width), BF16)] + [whole] * (level + 2 < len(levels))
            carry, sent, *total = call(
                functools.partial(join_kernel, stride, rows, len(arrived), len(outs)),
                [VMEM] * (2 + len(arrived) + len(before)),
                outs,
                [],
                8 * radix * modes * width,
                16 * modes * width,
            )(*total, rates, *arrived, *before)
            before = [carry]
    local, table, weight = call(
        functools.partial(local_kernel, groups - 1),
        [VMEM] * 5 + [HBM],
        [((rows, width), F32), ((modes, SUB, width), F32), ((width, columns), BF16)],
        [DMA],
        2 * rows * (SUB + modes) * width,
        8 * rows * width,
    )(after(mixed, sent), starts, rates, residues, skip, out_weight)
    arrived[0] = after(arrived[0], local)

    gated, values = [], {groups - 1: []}
    for span, height in zip(spans, heights):
        half, first = call(
            functools.partial(gate_kernel, span.start, stride),
            [VMEM] * (6 + len(arrived)),
            [((height, width), BF16), ((height, columns), BF16)],
            [pltpu.VMEM((height // SUB, modes, width), F32)],
            2 * height * modes * width,
            16 * height * width,
        )(post, local, table, rates, carry, weight, *arrived)
        gated.append(half)
        values[groups - 1].append(first)

    offsets = list(range(groups - 2, -1, -1))
    shares = call(
        functools.partial(project_kernel, offsets),
        [VMEM] * (PIECES + 1),
        [((height, columns), BF16 if offset % 2 else F32) for offset in offsets for height in heights],
        [pltpu.VMEM((rows, width), BF16)],
        2 * rows * width * columns * len(offsets),
        2 * width * columns * len(offsets),
    )(*gated, out_weight)
    for slot, offset in enumerate(offsets):
        values[offset] = list(shares[slot * PIECES : (slot + 1) * PIECES])

    sums = []
    for offset in range(groups - 1, 0, -1):
        stride = offset & -offset
        target = offset ^ stride
        pairs = [(source, source ^ stride) for source in range(groups)]
        for piece in range(PIECES):
            index = len(sums)
            sent = values[offset][piece].astype(BF16)
            if index >= 2 * PIECES:
                sent = after(sent, sums[index - 2 * PIECES])
            arrived = lax.ppermute(sent, "chan", pairs)
            kept = values[target][piece]
            if piece:
                kept = after(kept, values[target][piece - 1])
            if offset == 1 and piece + 1 == PIECES:
                break
            values[target][piece] = kept + arrived.astype(F32)
            sums.append(values[target][piece].astype(BF16))
    done = [value.astype(BF16) for value in values[0][:-1]]
    return pl.pallas_call(
        finish_kernel,
        in_specs=[VMEM] * (PIECES + 1),
        out_shape=jax.ShapeDtypeStruct((rows, columns), BF16),
        out_specs=HBM,
        scratch_shapes=[pltpu.VMEM((heights[-1], columns), BF16), DMA((PIECES,))],
        compiler_params=pltpu.CompilerParams(vmem_limit_bytes=24 * 2**20),
    )(*done, kept, arrived)


def solution(mesh):
    return jax.shard_map(
        body,
        mesh=mesh,
        in_specs=(
            P("seq", "chan"),
            P("seq", "chan"),
            P("seq", "chan"),
            P("chan", None),
            P("chan", None),
            P("chan"),
            P("chan", None),
        ),
        out_specs=P("seq", "chan"),
        check_vma=False,
    )
```

```python
import functools

import jax
import jax.numpy as jnp
from jax import lax
from jax.experimental import pallas as pl
from jax.experimental.pallas import tpu as pltpu
from jax.sharding import PartitionSpec as P

SUB = 8
LANES = 128
DEPTH = 256
PIECES = 2
F32 = jnp.float32
BF16 = jnp.bfloat16
VMEM = pl.BlockSpec(memory_space=pltpu.VMEM)
HBM = pl.BlockSpec(memory_space=pltpu.HBM)
DMA = pltpu.SemaphoreType.DMA


def call(kernel, ins, outs, scratch, flops, moved):
    run = pl.pallas_call(
        kernel,
        in_specs=ins,
        out_shape=[jax.ShapeDtypeStruct(shape, kind) for shape, kind in outs],
        out_specs=[VMEM] * len(outs),
        scratch_shapes=scratch,
        compiler_params=pltpu.CompilerParams(vmem_limit_bytes=24 * 2**20),
        cost_estimate=pl.CostEstimate(flops=flops, bytes_accessed=moved, transcendentals=0),
    )
    return lambda *operands: run(
        *[
            pltpu.with_memory_space_constraint(operand, pltpu.HBM) if spec is HBM else operand
            for spec, operand in zip(ins, operands)
        ]
    )


def spans_of(rows):
    cut = rows * 3 // 4
    return [slice(0, cut), slice(cut, rows)]


def block_of(weight_ref, offset, columns):
    start = pl.multiple_of((lax.axis_index("chan") ^ offset) * columns, LANES)
    return weight_ref.at[:, pl.ds(start, columns)]


def state_kernel(
    pre_hbm, signal_hbm, rates_hbm, residues_hbm, skip_hbm, post_hbm,
    mixed_ref, starts_ref, end_ref, rates_ref, residues_ref, skip_ref, post_ref,
    pre_ref, signal_ref, sems,
):
    moves = [
        pltpu.make_async_copy(source, target, sems.at[index])
        for index, (source, target) in enumerate(
            [
                (pre_hbm, pre_ref),
                (signal_hbm, signal_ref),
                (rates_hbm, rates_ref),
                (residues_hbm, residues_ref),
                (skip_hbm, skip_ref),
                (post_hbm, post_ref),
            ]
        )
    ]
    for move in moves:
        move.start()
    for move in moves[:3]:
        move.wait()
    for lane in range(0, rates_ref.shape[1], LANES):
        cols = slice(lane, lane + LANES)
        mixed_ref[:, cols] = pre_ref[:, cols].astype(F32) * signal_ref[:, cols].astype(F32)
        fade = jnp.exp(-rates_ref[:, cols])
        fade_sub = jnp.exp(rates_ref[:, cols] * (-float(SUB)))
        state = jnp.zeros(fade.shape, F32)
        for sub in range(starts_ref.shape[0]):
            starts_ref[sub, :, cols] = state
            base = sub * SUB
            own = fade * mixed_ref[base : base + 1, cols]
            for token in range(base + 1, base + SUB - 1):
                own = fade * (own + mixed_ref[token : token + 1, cols])
            state = fade_sub * state + (own + mixed_ref[base + SUB - 1 : base + SUB, cols])
        end_ref[:, cols] = state
    for move in moves[3:]:
        move.wait()


def local_kernel(
    offset, mixed_ref, starts_ref, rates_ref, residues_ref, skip_ref, weight_hbm,
    local_ref, table_ref, weight_ref,
    sem,
):
    move = pltpu.make_async_copy(block_of(weight_hbm, offset, weight_ref.shape[1]), weight_ref, sem)
    move.start()
    rows, width = mixed_ref.shape
    modes = rates_ref.shape[0]
    row_ids = lax.broadcasted_iota(jnp.int32, (SUB, LANES), 0)
    steps = row_ids.astype(F32) + 1.0
    for lane in range(0, width, LANES):
        cols = slice(lane, lane + LANES)
        weights = residues_ref[:, cols] * jnp.sqrt(2.0 * rates_ref[:, cols])
        taps = jnp.zeros((SUB, LANES), F32)
        for mode in range(modes):
            entry = weights[mode : mode + 1, :] * jnp.exp(-rates_ref[mode : mode + 1, cols] * steps)
            table_ref[mode, :, cols] = entry
            taps = taps + entry
        first = jnp.sum(weights, axis=0, keepdims=True) + skip_ref[:, cols]
        masked = [jnp.where(row_ids >= lag, taps[lag - 1 : lag, :], 0.0) for lag in range(1, SUB)]
        totals = []
        for sub in range(0, rows, SUB):
            mixed = mixed_ref[sub : sub + SUB, cols]
            total = first * mixed
            for lag in range(1, SUB):
                total = total + masked[lag - 1] * pltpu.roll(mixed, lag, 0)
            totals.append(total)
        for mode in range(modes):
            entry = table_ref[mode, :, cols]
            totals = [
                total + entry * starts_ref[sub, mode : mode + 1, cols] if sub else total
                for sub, total in enumerate(totals)
            ]
        for sub, total in enumerate(totals):
            local_ref[sub * SUB : (sub + 1) * SUB, cols] = total
    move.wait()


def stages(size):
    steps, stride = [], 1
    while stride < size:
        radix = 4 if stride > 1 and size // stride % 4 == 0 else 2
        steps.append((stride, radix))
        stride *= radix
    return steps


def entering(stride, rows, states, rates):
    me = lax.axis_index("seq")
    digit = (me // stride) % (len(states) + 1)
    total = jnp.zeros(rates.shape, F32)
    for index, state in enumerate(states):
        other = digit ^ (index + 1)
        blocks = me % stride + stride * (digit - 1 - other)
        fade = jnp.exp(-rates * (rows * jnp.maximum(blocks, 0)).astype(F32))
        total = total + jnp.where(other < digit, fade, 0.0) * state
    return total


def join_kernel(stride, rows, arrivals, outs, total_ref, rates_ref, *refs):
    arrived_refs, before_refs, out_refs = refs[:arrivals], refs[arrivals:-outs], refs[-outs:]
    rates = rates_ref[...]
    states = [arrived_ref[...].astype(F32) for arrived_ref in arrived_refs[::-1]]
    carry = entering(stride, rows, states, rates)
    for before_ref in before_refs:
        carry = carry + before_ref[...]
    digit = (lax.axis_index("seq") // stride) % (len(states) + 1)
    joined = jnp.zeros(rates.shape, F32)
    for index, state in enumerate((total_ref[...], *states)):
        blocks = stride * (len(states) - (digit ^ index))
        joined = joined + jnp.exp(-rates * (rows * blocks).astype(F32)) * state
    for out_ref, value in zip(out_refs, (carry, joined, joined)):
        out_ref[...] = value.astype(out_ref.dtype)


def gate_kernel(
    base, stride,
    post_ref, local_ref, table_ref, rates_ref, carry_ref, weight_ref, *refs,
):
    *arrived_refs, gated_ref, first_ref, states_ref = refs
    height, width = gated_ref.shape
    modes = rates_ref.shape[0]
    subs = height // SUB
    rates = rates_ref[...]
    states = [arrived_ref[...].astype(F32) for arrived_ref in arrived_refs[::-1]]
    state = carry_ref[...] + entering(stride, post_ref.shape[0], states, rates)
    if base:
        state = state * jnp.exp(rates * (-float(base)))
    fade = jnp.exp(rates * (-float(SUB)))
    for sub in range(subs):
        states_ref[sub] = state
        state = state * fade
    product = jnp.zeros(first_ref.shape, F32)
    for lane in range(0, width, LANES):
        cols = slice(lane, lane + LANES)
        totals = [local_ref[base + sub * SUB : base + (sub + 1) * SUB, cols] for sub in range(subs)]
        for mode in range(modes):
            entry = table_ref[mode, :, cols]
            totals = [
                total + entry * states_ref[sub, mode : mode + 1, cols] for sub, total in enumerate(totals)
            ]
        for sub in range(0, subs, 2):
            part = slice(base + sub * SUB, base + (sub + 2) * SUB)
            total = jnp.concatenate(totals[sub : sub + 2], axis=0)
            gated_ref[sub * SUB : (sub + 2) * SUB, cols] = (
                post_ref[part, cols].astype(F32) * total
            ).astype(BF16)
        if (lane + LANES) % DEPTH == 0:
            depth = slice(lane + LANES - DEPTH, lane + LANES)
            product = product + jnp.dot(
                gated_ref[:, depth], weight_ref[depth, :], preferred_element_type=F32
            )
    first_ref[...] = product.astype(BF16)


def project_kernel(offsets, *refs):
    gated_refs, weight_ref, out_refs, gated_ref = refs[:PIECES], refs[PIECES], refs[PIECES + 1 : -1], refs[-1]
    spans = spans_of(gated_ref.shape[0])
    for span, half_ref in zip(spans, gated_refs):
        gated_ref[span, :] = half_ref[...]
    for slot, offset in enumerate(offsets):
        block = block_of(weight_ref, offset, out_refs[0].shape[1])[...]
        product = jnp.dot(gated_ref[...], block, preferred_element_type=F32)
        for piece, span in enumerate(spans):
            out_ref = out_refs[slot * PIECES + piece]
            out_ref[...] = product[span, :].astype(out_ref.dtype)


def finish_kernel(*refs):
    *done_refs, kept_ref, arrived_ref, out_hbm, last_ref, sems = refs
    moves = []
    for piece, span in enumerate(spans_of(out_hbm.shape[0])):
        if piece + 1 == PIECES:
            last_ref[...] = (kept_ref[...] + arrived_ref[...].astype(F32)).astype(BF16)
        moves.append(
            pltpu.make_async_copy(
                (*done_refs, last_ref)[piece],
                out_hbm.at[span, :],
                sems.at[piece],
            )
        )
        moves[-1].start()
    for move in moves:
        move.wait()


def after(value, *earlier):
    return lax.optimization_barrier((value, *earlier))[0]


def body(post_gate, pre_gate, signal, decay_rates, residues, skip_gain, out_weight):
    rows, width = post_gate.shape
    modes = decay_rates.shape[1]
    subs = rows // SUB
    size = lax.axis_size("seq")
    groups = lax.axis_size("chan")
    columns = out_weight.shape[1] // groups
    spans = spans_of(rows)
    heights = [span.stop - span.start for span in spans]
    whole = ((modes, width), F32)
    mixed, starts, end, rates, residues, skip, post = call(
        state_kernel,
        [HBM] * 6,
        [
            ((rows, width), F32),
            ((subs, modes, width), F32),
            whole,
            whole,
            whole,
            ((1, width), F32),
            ((rows, width), BF16),
        ],
        [pltpu.VMEM((rows, width), BF16), pltpu.VMEM((rows, width), BF16), DMA((6,))],
        4 * rows * modes * width,
        8 * rows * width,
    )(pre_gate, signal, decay_rates.T, residues.T, skip_gain.reshape(1, width), post_gate)
    def swap(state, distance):
        return lax.ppermute(state, "seq", [(source, source ^ distance) for source in range(size)])

    levels = stages(size)
    arrived, total, before = [swap(end, 1)], [end], []
    for level, (stride, radix) in enumerate(levels):
        if level:
            arrived = [swap(sent, stride * hop) for hop in range(radix - 1, 0, -1)]
        if level + 1 < len(levels):
            outs = [whole, ((modes, width), BF16)] + [whole] * (level + 2 < len(levels))
            carry, sent, *total = call(
                functools.partial(join_kernel, stride, rows, len(arrived), len(outs)),
                [VMEM] * (2 + len(arrived) + len(before)),
                outs,
                [],
                8 * radix * modes * width,
                16 * modes * width,
            )(*total, rates, *arrived, *before)
            before = [carry]
    local, table, weight = call(
        functools.partial(local_kernel, groups - 1),
        [VMEM] * 5 + [HBM],
        [((rows, width), F32), ((modes, SUB, width), F32), ((width, columns), BF16)],
        [DMA],
        2 * rows * (SUB + modes) * width,
        8 * rows * width,
    )(after(mixed, sent), starts, rates, residues, skip, out_weight)
    arrived[0] = after(arrived[0], local)

    gated, values = [], {groups - 1: []}
    for span, height in zip(spans, heights):
        half, first = call(
            functools.partial(gate_kernel, span.start, stride),
            [VMEM] * (6 + len(arrived)),
            [((height, width), BF16), ((height, columns), BF16)],
            [pltpu.VMEM((height // SUB, modes, width), F32)],
            2 * height * modes * width,
            16 * height * width,
        )(post, local, table, rates, carry, weight, *arrived)
        gated.append(half)
        values[groups - 1].append(first)

    offsets = list(range(groups - 2, -1, -1))
    shares = call(
        functools.partial(project_kernel, offsets),
        [VMEM] * (PIECES + 1),
        [((height, columns), BF16 if offset % 2 else F32) for offset in offsets for height in heights],
        [pltpu.VMEM((rows, width), BF16)],
        2 * rows * width * columns * len(offsets),
        2 * width * columns * len(offsets),
    )(*gated, out_weight)
    for slot, offset in enumerate(offsets):
        values[offset] = list(shares[slot * PIECES : (slot + 1) * PIECES])

    sums = []
    for offset in range(groups - 1, 0, -1):
        stride = offset & -offset
        target = offset ^ stride
        pairs = [(source, source ^ stride) for source in range(groups)]
        for piece in range(PIECES):
            index = len(sums)
            sent = values[offset][piece].astype(BF16)
            if index >= 2 * PIECES:
                sent = after(sent, sums[index - 2 * PIECES])
            arrived = lax.ppermute(sent, "chan", pairs)
            kept = values[target][piece]
            if piece:
                kept = after(kept, values[target][piece - 1])
            if offset == 1 and piece + 1 == PIECES:
                break
            values[target][piece] = kept + arrived.astype(F32)
            sums.append(values[target][piece].astype(BF16))
    done = [value.astype(BF16) for value in values[0][:-1]]
    return pl.pallas_call(
        finish_kernel,
        in_specs=[VMEM] * (PIECES + 1),
        out_shape=jax.ShapeDtypeStruct((rows, columns), BF16),
        out_specs=HBM,
        scratch_shapes=[pltpu.VMEM((heights[-1], columns), BF16), DMA((PIECES,))],
        compiler_params=pltpu.CompilerParams(vmem_limit_bytes=24 * 2**20),
    )(*done, kept, arrived)


def solution(mesh):
    return jax.shard_map(
        body,
        mesh=mesh,
        in_specs=(
            P("seq", "chan"),
            P("seq", "chan"),
            P("seq", "chan"),
            P("chan", None),
            P("chan", None),
            P("chan"),
            P("chan", None),
        ),
        out_specs=P("seq", "chan"),
        check_vma=False,
    )
```

```python
import functools

import jax
import jax.numpy as jnp
from jax import lax
from jax.experimental import pallas as pl
from jax.experimental.pallas import tpu as pltpu
from jax.sharding import PartitionSpec as P

SUB = 8
LANES = 128
DEPTH = 256
PIECES = 2
F32 = jnp.float32
BF16 = jnp.bfloat16
VMEM = pl.BlockSpec(memory_space=pltpu.VMEM)
HBM = pl.BlockSpec(memory_space=pltpu.HBM)
DMA = pltpu.SemaphoreType.DMA


def call(kernel, ins, outs, scratch, flops, moved):
    run = pl.pallas_call(
        kernel,
        in_specs=ins,
        out_shape=[jax.ShapeDtypeStruct(shape, kind) for shape, kind in outs],
        out_specs=[VMEM] * len(outs),
        scratch_shapes=scratch,
        compiler_params=pltpu.CompilerParams(vmem_limit_bytes=24 * 2**20),
        cost_estimate=pl.CostEstimate(flops=flops, bytes_accessed=moved, transcendentals=0),
    )
    return lambda *operands: run(
        *[
            pltpu.with_memory_space_constraint(operand, pltpu.HBM) if spec is HBM else operand
            for spec, operand in zip(ins, operands)
        ]
    )


def spans_of(rows):
    cut = rows * 3 // 4
    return [slice(0, cut), slice(cut, rows)]


def block_of(weight_ref, offset, columns):
    start = pl.multiple_of((lax.axis_index("chan") ^ offset) * columns, LANES)
    return weight_ref.at[:, pl.ds(start, columns)]


def state_kernel(
    pre_hbm, signal_hbm, rates_hbm, residues_hbm, skip_hbm, post_hbm,
    mixed_ref, starts_ref, end_ref, rates_ref, residues_ref, skip_ref, post_ref,
    pre_ref, signal_ref, sems,
):
    moves = [
        pltpu.make_async_copy(source, target, sems.at[index])
        for index, (source, target) in enumerate(
            [
                (pre_hbm, pre_ref),
                (signal_hbm, signal_ref),
                (rates_hbm, rates_ref),
                (residues_hbm, residues_ref),
                (skip_hbm, skip_ref),
                (post_hbm, post_ref),
            ]
        )
    ]
    for move in moves:
        move.start()
    for move in moves[:3]:
        move.wait()
    for lane in range(0, rates_ref.shape[1], LANES):
        cols = slice(lane, lane + LANES)
        mixed_ref[:, cols] = pre_ref[:, cols].astype(F32) * signal_ref[:, cols].astype(F32)
        fade = jnp.exp(-rates_ref[:, cols])
        fade_sub = jnp.exp(rates_ref[:, cols] * (-float(SUB)))
        state = jnp.zeros(fade.shape, F32)
        for sub in range(starts_ref.shape[0]):
            starts_ref[sub, :, cols] = state
            base = sub * SUB
            own = fade * mixed_ref[base : base + 1, cols]
            for token in range(base + 1, base + SUB - 1):
                own = fade * (own + mixed_ref[token : token + 1, cols])
            state = fade_sub * state + (own + mixed_ref[base + SUB - 1 : base + SUB, cols])
        end_ref[:, cols] = state
    for move in moves[3:]:
        move.wait()


def local_kernel(
    offset, mixed_ref, starts_ref, rates_ref, residues_ref, skip_ref, weight_hbm,
    local_ref, table_ref, weight_ref,
    sem,
):
    move = pltpu.make_async_copy(block_of(weight_hbm, offset, weight_ref.shape[1]), weight_ref, sem)
    move.start()
    rows, width = mixed_ref.shape
    modes = rates_ref.shape[0]
    row_ids = lax.broadcasted_iota(jnp.int32, (SUB, LANES), 0)
    steps = row_ids.astype(F32) + 1.0
    for lane in range(0, width, LANES):
        cols = slice(lane, lane + LANES)
        weights = residues_ref[:, cols] * jnp.sqrt(2.0 * rates_ref[:, cols])
        taps = jnp.zeros((SUB, LANES), F32)
        for mode in range(modes):
            entry = weights[mode : mode + 1, :] * jnp.exp(-rates_ref[mode : mode + 1, cols] * steps)
            table_ref[mode, :, cols] = entry
            taps = taps + entry
        first = jnp.sum(weights, axis=0, keepdims=True) + skip_ref[:, cols]
        masked = [jnp.where(row_ids >= lag, taps[lag - 1 : lag, :], 0.0) for lag in range(1, SUB)]
        totals = []
        for sub in range(0, rows, SUB):
            mixed = mixed_ref[sub : sub + SUB, cols]
            total = first * mixed
            for lag in range(1, SUB):
                total = total + masked[lag - 1] * pltpu.roll(mixed, lag, 0)
            totals.append(total)
        for mode in range(modes):
            entry = table_ref[mode, :, cols]
            totals = [
                total + entry * starts_ref[sub, mode : mode + 1, cols] if sub else total
                for sub, total in enumerate(totals)
            ]
        for sub, total in enumerate(totals):
            local_ref[sub * SUB : (sub + 1) * SUB, cols] = total
    move.wait()


def stages(size):
    steps, stride = [], 1
    while stride < size:
        radix = 4 if stride > 1 and size // stride % 4 == 0 else 2
        steps.append((stride, radix))
        stride *= radix
    return steps


def entering(stride, rows, states, rates):
    me = lax.axis_index("seq")
    digit = (me // stride) % (len(states) + 1)
    total = jnp.zeros(rates.shape, F32)
    for index, state in enumerate(states):
        other = digit ^ (index + 1)
        blocks = me % stride + stride * (digit - 1 - other)
        fade = jnp.exp(-rates * (rows * jnp.maximum(blocks, 0)).astype(F32))
        total = total + jnp.where(other < digit, fade, 0.0) * state
    return total


def join_kernel(stride, rows, arrivals, outs, total_ref, rates_ref, *refs):
    arrived_refs, before_refs, out_refs = refs[:arrivals], refs[arrivals:-outs], refs[-outs:]
    rates = rates_ref[...]
    states = [arrived_ref[...].astype(F32) for arrived_ref in arrived_refs[::-1]]
    carry = entering(stride, rows, states, rates)
    for before_ref in before_refs:
        carry = carry + before_ref[...]
    digit = (lax.axis_index("seq") // stride) % (len(states) + 1)
    joined = jnp.zeros(rates.shape, F32)
    for index, state in enumerate((total_ref[...], *states)):
        blocks = stride * (len(states) - (digit ^ index))
        joined = joined + jnp.exp(-rates * (rows * blocks).astype(F32)) * state
    for out_ref, value in zip(out_refs, (carry, joined, joined)):
        out_ref[...] = value.astype(out_ref.dtype)


def gate_kernel(
    base, stride,
    post_ref, local_ref, table_ref, rates_ref, carry_ref, weight_ref, *refs,
):
    *arrived_refs, gated_ref, first_ref, states_ref = refs
    height, width = gated_ref.shape
    modes = rates_ref.shape[0]
    subs = height // SUB
    rates = rates_ref[...]
    states = [arrived_ref[...].astype(F32) for arrived_ref in arrived_refs[::-1]]
    state = carry_ref[...] + entering(stride, post_ref.shape[0], states, rates)
    if base:
        state = state * jnp.exp(rates * (-float(base)))
    fade = jnp.exp(rates * (-float(SUB)))
    for sub in range(subs):
        states_ref[sub] = state
        state = state * fade
    product = jnp.zeros(first_ref.shape, F32)
    for lane in range(0, width, LANES):
        cols = slice(lane, lane + LANES)
        totals = [local_ref[base + sub * SUB : base + (sub + 1) * SUB, cols] for sub in range(subs)]
        for mode in range(modes):
            entry = table_ref[mode, :, cols]
            totals = [
                total + entry * states_ref[sub, mode : mode + 1, cols] for sub, total in enumerate(totals)
            ]
        for sub in range(0, subs, 2):
            part = slice(base + sub * SUB, base + (sub + 2) * SUB)
            total = jnp.concatenate(totals[sub : sub + 2], axis=0)
            gated_ref[sub * SUB : (sub + 2) * SUB, cols] = (
                post_ref[part, cols].astype(F32) * total
            ).astype(BF16)
        if (lane + LANES) % DEPTH == 0:
            depth = slice(lane + LANES - DEPTH, lane + LANES)
            product = product + jnp.dot(
                gated_ref[:, depth], weight_ref[depth, :], preferred_element_type=F32
            )
    first_ref[...] = product.astype(BF16)


def project_kernel(offsets, *refs):
    gated_refs, weight_ref, out_refs, gated_ref = refs[:PIECES], refs[PIECES], refs[PIECES + 1 : -1], refs[-1]
    spans = spans_of(gated_ref.shape[0])
    for span, half_ref in zip(spans, gated_refs):
        gated_ref[span, :] = half_ref[...]
    for slot, offset in enumerate(offsets):
        block = block_of(weight_ref, offset, out_refs[0].shape[1])[...]
        product = jnp.dot(gated_ref[...], block, preferred_element_type=F32)
        for piece, span in enumerate(spans):
            out_ref = out_refs[slot * PIECES + piece]
            out_ref[...] = product[span, :].astype(out_ref.dtype)


def finish_kernel(*refs):
    *done_refs, kept_ref, arrived_ref, out_hbm, last_ref, sems = refs
    last_ref[...] = (kept_ref[...] + arrived_ref[...].astype(F32)).astype(BF16)
    moves = [
        pltpu.make_async_copy(piece_ref, out_hbm.at[span, :], sems.at[piece])
        for piece, (piece_ref, span) in enumerate(zip((last_ref, *done_refs), spans_of(out_hbm.shape[0])))
    ]
    for move in moves:
        move.start()
    for move in moves:
        move.wait()


def after(value, *earlier):
    return lax.optimization_barrier((value, *earlier))[0]


def body(post_gate, pre_gate, signal, decay_rates, residues, skip_gain, out_weight):
    rows, width = post_gate.shape
    modes = decay_rates.shape[1]
    subs = rows // SUB
    size = lax.axis_size("seq")
    groups = lax.axis_size("chan")
    columns = out_weight.shape[1] // groups
    spans = spans_of(rows)
    heights = [span.stop - span.start for span in spans]
    whole = ((modes, width), F32)
    mixed, starts, end, rates, residues, skip, post = call(
        state_kernel,
        [HBM] * 6,
        [
            ((rows, width), F32),
            ((subs, modes, width), F32),
            whole,
            whole,
            whole,
            ((1, width), F32),
            ((rows, width), BF16),
        ],
        [pltpu.VMEM((rows, width), BF16), pltpu.VMEM((rows, width), BF16), DMA((6,))],
        4 * rows * modes * width,
        8 * rows * width,
    )(pre_gate, signal, decay_rates.T, residues.T, skip_gain.reshape(1, width), post_gate)
    def swap(state, distance):
        return lax.ppermute(state, "seq", [(source, source ^ distance) for source in range(size)])

    levels = stages(size)
    arrived, total, before = [swap(end, 1)], [end], []
    for level, (stride, radix) in enumerate(levels):
        if level:
            arrived = [swap(sent, stride * hop) for hop in range(radix - 1, 0, -1)]
        if level + 1 < len(levels):
            outs = [whole, ((modes, width), BF16)] + [whole] * (level + 2 < len(levels))
            carry, sent, *total = call(
                functools.partial(join_kernel, stride, rows, len(arrived), len(outs)),
                [VMEM] * (2 + len(arrived) + len(before)),
                outs,
                [],
                8 * radix * modes * width,
                16 * modes * width,
            )(*total, rates, *arrived, *before)
            before = [carry]
    local, table, weight = call(
        functools.partial(local_kernel, groups - 1),
        [VMEM] * 5 + [HBM],
        [((rows, width), F32), ((modes, SUB, width), F32), ((width, columns), BF16)],
        [DMA],
        2 * rows * (SUB + modes) * width,
        8 * rows * width,
    )(after(mixed, sent), starts, rates, residues, skip, out_weight)
    arrived[0] = after(arrived[0], local)

    gated, values = [], {groups - 1: []}
    for span, height in zip(spans, heights):
        half, first = call(
            functools.partial(gate_kernel, span.start, stride),
            [VMEM] * (6 + len(arrived)),
            [((height, width), BF16), ((height, columns), BF16)],
            [pltpu.VMEM((height // SUB, modes, width), F32)],
            2 * height * modes * width,
            16 * height * width,
        )(post, local, table, rates, carry, weight, *arrived)
        gated.append(half)
        values[groups - 1].append(first)

    offsets = list(range(groups - 2, -1, -1))
    shares = call(
        functools.partial(project_kernel, offsets),
        [VMEM] * (PIECES + 1),
        [((height, columns), BF16 if offset % 2 else F32) for offset in offsets for height in heights],
        [pltpu.VMEM((rows, width), BF16)],
        2 * rows * width * columns * len(offsets),
        2 * width * columns * len(offsets),
    )(*gated, out_weight)
    for slot, offset in enumerate(offsets):
        values[offset] = list(shares[slot * PIECES : (slot + 1) * PIECES])

    sums = []
    for offset in range(groups - 1, 0, -1):
        stride = offset & -offset
        target = offset ^ stride
        pairs = [(source, source ^ stride) for source in range(groups)]
        pieces = list(range(PIECES))
        if offset == 1:
            pieces.reverse()
        for turn, piece in enumerate(pieces):
            index = len(sums)
            sent = values[offset][piece].astype(BF16)
            if index >= 2 * PIECES:
                sent = after(sent, sums[index - 2 * PIECES])
            arrived = lax.ppermute(sent, "chan", pairs)
            kept = values[target][piece]
            if turn:
                kept = after(kept, values[target][pieces[turn - 1]])
            if offset == 1 and turn + 1 == PIECES:
                break
            values[target][piece] = kept + arrived.astype(F32)
            sums.append(values[target][piece].astype(BF16))
    done = [value.astype(BF16) for value in values[0][1:]]
    return pl.pallas_call(
        finish_kernel,
        in_specs=[VMEM] * (PIECES + 1),
        out_shape=jax.ShapeDtypeStruct((rows, columns), BF16),
        out_specs=HBM,
        scratch_shapes=[pltpu.VMEM((heights[0], columns), BF16), DMA((PIECES,))],
        compiler_params=pltpu.CompilerParams(vmem_limit_bytes=24 * 2**20),
    )(*done, kept, arrived)


def solution(mesh):
    return jax.shard_map(
        body,
        mesh=mesh,
        in_specs=(
            P("seq", "chan"),
            P("seq", "chan"),
            P("seq", "chan"),
            P("chan", None),
            P("chan", None),
            P("chan"),
            P("chan", None),
        ),
        out_specs=P("seq", "chan"),
        check_vma=False,
    )
```

```python
import functools

import jax
import jax.numpy as jnp
from jax import lax
from jax.experimental import pallas as pl
from jax.experimental.pallas import tpu as pltpu
from jax.sharding import PartitionSpec as P

SUB = 8
LANES = 128
DEPTH = 256
PIECES = 2
F32 = jnp.float32
BF16 = jnp.bfloat16
VMEM = pl.BlockSpec(memory_space=pltpu.VMEM)
HBM = pl.BlockSpec(memory_space=pltpu.HBM)
DMA = pltpu.SemaphoreType.DMA


def call(kernel, ins, outs, scratch, flops, moved):
    run = pl.pallas_call(
        kernel,
        in_specs=ins,
        out_shape=[jax.ShapeDtypeStruct(shape, kind) for shape, kind in outs],
        out_specs=[VMEM] * len(outs),
        scratch_shapes=scratch,
        compiler_params=pltpu.CompilerParams(vmem_limit_bytes=24 * 2**20),
        cost_estimate=pl.CostEstimate(flops=flops, bytes_accessed=moved, transcendentals=0),
    )
    return lambda *operands: run(
        *[
            pltpu.with_memory_space_constraint(operand, pltpu.HBM) if spec is HBM else operand
            for spec, operand in zip(ins, operands)
        ]
    )


def spans_of(rows):
    cut = rows * 7 // 8
    return [slice(0, cut), slice(cut, rows)]


def block_of(weight_ref, offset, columns):
    start = pl.multiple_of((lax.axis_index("chan") ^ offset) * columns, LANES)
    return weight_ref.at[:, pl.ds(start, columns)]


def state_kernel(
    pre_hbm, signal_hbm, rates_hbm, residues_hbm, skip_hbm, post_hbm,
    mixed_ref, starts_ref, end_ref, rates_ref, residues_ref, skip_ref, post_ref,
    pre_ref, signal_ref, sems,
):
    moves = [
        pltpu.make_async_copy(source, target, sems.at[index])
        for index, (source, target) in enumerate(
            [
                (pre_hbm, pre_ref),
                (signal_hbm, signal_ref),
                (rates_hbm, rates_ref),
                (residues_hbm, residues_ref),
                (skip_hbm, skip_ref),
                (post_hbm, post_ref),
            ]
        )
    ]
    for move in moves:
        move.start()
    for move in moves[:3]:
        move.wait()
    for lane in range(0, rates_ref.shape[1], LANES):
        cols = slice(lane, lane + LANES)
        mixed_ref[:, cols] = pre_ref[:, cols].astype(F32) * signal_ref[:, cols].astype(F32)
        fade = jnp.exp(-rates_ref[:, cols])
        fade_sub = jnp.exp(rates_ref[:, cols] * (-float(SUB)))
        state = jnp.zeros(fade.shape, F32)
        for sub in range(starts_ref.shape[0]):
            starts_ref[sub, :, cols] = state
            base = sub * SUB
            own = fade * mixed_ref[base : base + 1, cols]
            for token in range(base + 1, base + SUB - 1):
                own = fade * (own + mixed_ref[token : token + 1, cols])
            state = fade_sub * state + (own + mixed_ref[base + SUB - 1 : base + SUB, cols])
        end_ref[:, cols] = state
    for move in moves[3:]:
        move.wait()


def local_kernel(
    offset, mixed_ref, starts_ref, rates_ref, residues_ref, skip_ref, weight_hbm,
    local_ref, table_ref, weight_ref,
    sem,
):
    move = pltpu.make_async_copy(block_of(weight_hbm, offset, weight_ref.shape[1]), weight_ref, sem)
    move.start()
    rows, width = mixed_ref.shape
    modes = rates_ref.shape[0]
    row_ids = lax.broadcasted_iota(jnp.int32, (SUB, LANES), 0)
    steps = row_ids.astype(F32) + 1.0
    for lane in range(0, width, LANES):
        cols = slice(lane, lane + LANES)
        weights = residues_ref[:, cols] * jnp.sqrt(2.0 * rates_ref[:, cols])
        taps = jnp.zeros((SUB, LANES), F32)
        for mode in range(modes):
            entry = weights[mode : mode + 1, :] * jnp.exp(-rates_ref[mode : mode + 1, cols] * steps)
            table_ref[mode, :, cols] = entry
            taps = taps + entry
        first = jnp.sum(weights, axis=0, keepdims=True) + skip_ref[:, cols]
        masked = [jnp.where(row_ids >= lag, taps[lag - 1 : lag, :], 0.0) for lag in range(1, SUB)]
        totals = []
        for sub in range(0, rows, SUB):
            mixed = mixed_ref[sub : sub + SUB, cols]
            total = first * mixed
            for lag in range(1, SUB):
                total = total + masked[lag - 1] * pltpu.roll(mixed, lag, 0)
            totals.append(total)
        for mode in range(modes):
            entry = table_ref[mode, :, cols]
            totals = [
                total + entry * starts_ref[sub, mode : mode + 1, cols] if sub else total
                for sub, total in enumerate(totals)
            ]
        for sub, total in enumerate(totals):
            local_ref[sub * SUB : (sub + 1) * SUB, cols] = total
    move.wait()


def stages(size):
    steps, stride = [], 1
    while stride < size:
        radix = 4 if stride > 1 and size // stride % 4 == 0 else 2
        steps.append((stride, radix))
        stride *= radix
    return steps


def entering(stride, rows, states, rates):
    me = lax.axis_index("seq")
    digit = (me // stride) % (len(states) + 1)
    total = jnp.zeros(rates.shape, F32)
    for index, state in enumerate(states):
        other = digit ^ (index + 1)
        blocks = me % stride + stride * (digit - 1 - other)
        fade = jnp.exp(-rates * (rows * jnp.maximum(blocks, 0)).astype(F32))
        total = total + jnp.where(other < digit, fade, 0.0) * state
    return total


def join_kernel(stride, rows, arrivals, outs, total_ref, rates_ref, *refs):
    arrived_refs, before_refs, out_refs = refs[:arrivals], refs[arrivals:-outs], refs[-outs:]
    rates = rates_ref[...]
    states = [arrived_ref[...].astype(F32) for arrived_ref in arrived_refs[::-1]]
    carry = entering(stride, rows, states, rates)
    for before_ref in before_refs:
        carry = carry + before_ref[...]
    digit = (lax.axis_index("seq") // stride) % (len(states) + 1)
    joined = jnp.zeros(rates.shape, F32)
    for index, state in enumerate((total_ref[...], *states)):
        blocks = stride * (len(states) - (digit ^ index))
        joined = joined + jnp.exp(-rates * (rows * blocks).astype(F32)) * state
    for out_ref, value in zip(out_refs, (carry, joined, joined)):
        out_ref[...] = value.astype(out_ref.dtype)


def gate_kernel(
    base, stride,
    post_ref, local_ref, table_ref, rates_ref, carry_ref, weight_ref, *refs,
):
    *arrived_refs, gated_ref, first_ref, states_ref = refs
    height, width = gated_ref.shape
    modes = rates_ref.shape[0]
    subs = height // SUB
    rates = rates_ref[...]
    states = [arrived_ref[...].astype(F32) for arrived_ref in arrived_refs[::-1]]
    state = carry_ref[...] + entering(stride, post_ref.shape[0], states, rates)
    if base:
        state = state * jnp.exp(rates * (-float(base)))
    fade = jnp.exp(rates * (-float(SUB)))
    for sub in range(subs):
        states_ref[sub] = state
        state = state * fade
    product = jnp.zeros(first_ref.shape, F32)
    for lane in range(0, width, LANES):
        cols = slice(lane, lane + LANES)
        totals = [local_ref[base + sub * SUB : base + (sub + 1) * SUB, cols] for sub in range(subs)]
        for mode in range(modes):
            entry = table_ref[mode, :, cols]
            totals = [
                total + entry * states_ref[sub, mode : mode + 1, cols] for sub, total in enumerate(totals)
            ]
        for sub in range(0, subs, 2):
            part = slice(base + sub * SUB, base + (sub + 2) * SUB)
            total = jnp.concatenate(totals[sub : sub + 2], axis=0)
            gated_ref[sub * SUB : (sub + 2) * SUB, cols] = (
                post_ref[part, cols].astype(F32) * total
            ).astype(BF16)
        if (lane + LANES) % DEPTH == 0:
            depth = slice(lane + LANES - DEPTH, lane + LANES)
            product = product + jnp.dot(
                gated_ref[:, depth], weight_ref[depth, :], preferred_element_type=F32
            )
    first_ref[...] = product.astype(BF16)


def project_kernel(offsets, *refs):
    gated_refs, weight_ref, out_refs, gated_ref = refs[:PIECES], refs[PIECES], refs[PIECES + 1 : -1], refs[-1]
    spans = spans_of(gated_ref.shape[0])
    for span, half_ref in zip(spans, gated_refs):
        gated_ref[span, :] = half_ref[...]
    for slot, offset in enumerate(offsets):
        block = block_of(weight_ref, offset, out_refs[0].shape[1])[...]
        product = jnp.dot(gated_ref[...], block, preferred_element_type=F32)
        for piece, span in enumerate(spans):
            out_ref = out_refs[slot * PIECES + piece]
            out_ref[...] = product[span, :].astype(out_ref.dtype)


def finish_kernel(*refs):
    *done_refs, kept_ref, arrived_ref, out_hbm, last_ref, sems = refs
    moves = []
    for piece, span in enumerate(spans_of(out_hbm.shape[0])):
        if piece + 1 == PIECES:
            last_ref[...] = (kept_ref[...] + arrived_ref[...].astype(F32)).astype(BF16)
        moves.append(
            pltpu.make_async_copy(
                (*done_refs, last_ref)[piece],
                out_hbm.at[span, :],
                sems.at[piece],
            )
        )
        moves[-1].start()
    for move in moves:
        move.wait()


def after(value, *earlier):
    return lax.optimization_barrier((value, *earlier))[0]


def body(post_gate, pre_gate, signal, decay_rates, residues, skip_gain, out_weight):
    rows, width = post_gate.shape
    modes = decay_rates.shape[1]
    subs = rows // SUB
    size = lax.axis_size("seq")
    groups = lax.axis_size("chan")
    columns = out_weight.shape[1] // groups
    spans = spans_of(rows)
    heights = [span.stop - span.start for span in spans]
    whole = ((modes, width), F32)
    mixed, starts, end, rates, residues, skip, post = call(
        state_kernel,
        [HBM] * 6,
        [
            ((rows, width), F32),
            ((subs, modes, width), F32),
            whole,
            whole,
            whole,
            ((1, width), F32),
            ((rows, width), BF16),
        ],
        [pltpu.VMEM((rows, width), BF16), pltpu.VMEM((rows, width), BF16), DMA((6,))],
        4 * rows * modes * width,
        8 * rows * width,
    )(pre_gate, signal, decay_rates.T, residues.T, skip_gain.reshape(1, width), post_gate)
    def swap(state, distance):
        return lax.ppermute(state, "seq", [(source, source ^ distance) for source in range(size)])

    levels = stages(size)
    arrived, total, before = [swap(end, 1)], [end], []
    for level, (stride, radix) in enumerate(levels):
        if level:
            arrived = [swap(sent, stride * hop) for hop in range(radix - 1, 0, -1)]
        if level + 1 < len(levels):
            outs = [whole, ((modes, width), BF16)] + [whole] * (level + 2 < len(levels))
            carry, sent, *total = call(
                functools.partial(join_kernel, stride, rows, len(arrived), len(outs)),
                [VMEM] * (2 + len(arrived) + len(before)),
                outs,
                [],
                8 * radix * modes * width,
                16 * modes * width,
            )(*total, rates, *arrived, *before)
            before = [carry]
    local, table, weight = call(
        functools.partial(local_kernel, groups - 1),
        [VMEM] * 5 + [HBM],
        [((rows, width), F32), ((modes, SUB, width), F32), ((width, columns), BF16)],
        [DMA],
        2 * rows * (SUB + modes) * width,
        8 * rows * width,
    )(after(mixed, sent), starts, rates, residues, skip, out_weight)
    arrived[0] = after(arrived[0], local)

    gated, values = [], {groups - 1: []}
    for span, height in zip(spans, heights):
        half, first = call(
            functools.partial(gate_kernel, span.start, stride),
            [VMEM] * (6 + len(arrived)),
            [((height, width), BF16), ((height, columns), BF16)],
            [pltpu.VMEM((height // SUB, modes, width), F32)],
            2 * height * modes * width,
            16 * height * width,
        )(post, local, table, rates, carry, weight, *arrived)
        gated.append(half)
        values[groups - 1].append(first)

    offsets = list(range(groups - 2, -1, -1))
    shares = call(
        functools.partial(project_kernel, offsets),
        [VMEM] * (PIECES + 1),
        [((height, columns), BF16 if offset % 2 else F32) for offset in offsets for height in heights],
        [pltpu.VMEM((rows, width), BF16)],
        2 * rows * width * columns * len(offsets),
        2 * width * columns * len(offsets),
    )(*gated, out_weight)
    for slot, offset in enumerate(offsets):
        values[offset] = list(shares[slot * PIECES : (slot + 1) * PIECES])

    sums = []
    for offset in range(groups - 1, 0, -1):
        stride = offset & -offset
        target = offset ^ stride
        pairs = [(source, source ^ stride) for source in range(groups)]
        for piece in range(PIECES):
            index = len(sums)
            sent = values[offset][piece].astype(BF16)
            if index >= 2 * PIECES:
                sent = after(sent, sums[index - 2 * PIECES])
            arrived = lax.ppermute(sent, "chan", pairs)
            kept = values[target][piece]
            if piece:
                kept = after(kept, values[target][piece - 1])
            if offset == 1 and piece + 1 == PIECES:
                break
            values[target][piece] = kept + arrived.astype(F32)
            sums.append(values[target][piece].astype(BF16))
    done = [value.astype(BF16) for value in values[0][:-1]]
    return pl.pallas_call(
        finish_kernel,
        in_specs=[VMEM] * (PIECES + 1),
        out_shape=jax.ShapeDtypeStruct((rows, columns), BF16),
        out_specs=HBM,
        scratch_shapes=[pltpu.VMEM((heights[-1], columns), BF16), DMA((PIECES,))],
        compiler_params=pltpu.CompilerParams(vmem_limit_bytes=24 * 2**20),
    )(*done, kept, arrived)


def solution(mesh):
    return jax.shard_map(
        body,
        mesh=mesh,
        in_specs=(
            P("seq", "chan"),
            P("seq", "chan"),
            P("seq", "chan"),
            P("chan", None),
            P("chan", None),
            P("chan"),
            P("chan", None),
        ),
        out_specs=P("seq", "chan"),
        check_vma=False,
    )
```

```python
import functools

import jax
import jax.numpy as jnp
from jax import lax
from jax.experimental import pallas as pl
from jax.experimental.pallas import tpu as pltpu
from jax.sharding import PartitionSpec as P

SUB = 8
LANES = 128
PIECES = 2
F32 = jnp.float32
BF16 = jnp.bfloat16
VMEM = pl.BlockSpec(memory_space=pltpu.VMEM)
HBM = pl.BlockSpec(memory_space=pltpu.HBM)
DMA = pltpu.SemaphoreType.DMA


def call(kernel, ins, outs, scratch, flops, moved):
    run = pl.pallas_call(
        kernel,
        in_specs=ins,
        out_shape=[jax.ShapeDtypeStruct(shape, kind) for shape, kind in outs],
        out_specs=[VMEM] * len(outs),
        scratch_shapes=scratch,
        compiler_params=pltpu.CompilerParams(vmem_limit_bytes=24 * 2**20),
        cost_estimate=pl.CostEstimate(flops=flops, bytes_accessed=moved, transcendentals=0),
    )
    return lambda *operands: run(
        *[
            pltpu.with_memory_space_constraint(operand, pltpu.HBM) if spec is HBM else operand
            for spec, operand in zip(ins, operands)
        ]
    )


def spans_of(rows):
    cut = rows * 3 // 4
    return [slice(0, cut), slice(cut, rows)]


def block_of(weight_ref, offset, columns):
    start = pl.multiple_of((lax.axis_index("chan") ^ offset) * columns, LANES)
    return weight_ref.at[:, pl.ds(start, columns)]


def state_kernel(
    pre_hbm, signal_hbm, rates_hbm, residues_hbm, skip_hbm, post_hbm,
    mixed_ref, starts_ref, end_ref, rates_ref, residues_ref, skip_ref, post_ref,
    pre_ref, signal_ref, sems,
):
    moves = [
        pltpu.make_async_copy(source, target, sems.at[index])
        for index, (source, target) in enumerate(
            [
                (pre_hbm, pre_ref),
                (signal_hbm, signal_ref),
                (rates_hbm, rates_ref),
                (residues_hbm, residues_ref),
                (skip_hbm, skip_ref),
                (post_hbm, post_ref),
            ]
        )
    ]
    for move in moves:
        move.start()
    for move in moves[:3]:
        move.wait()
    for lane in range(0, rates_ref.shape[1], LANES):
        cols = slice(lane, lane + LANES)
        mixed_ref[:, cols] = pre_ref[:, cols].astype(F32) * signal_ref[:, cols].astype(F32)
        fade = jnp.exp(-rates_ref[:, cols])
        fade_sub = jnp.exp(rates_ref[:, cols] * (-float(SUB)))
        state = jnp.zeros(fade.shape, F32)
        for sub in range(starts_ref.shape[0]):
            starts_ref[sub, :, cols] = state
            base = sub * SUB
            own = fade * mixed_ref[base : base + 1, cols]
            for token in range(base + 1, base + SUB - 1):
                own = fade * (own + mixed_ref[token : token + 1, cols])
            state = fade_sub * state + (own + mixed_ref[base + SUB - 1 : base + SUB, cols])
        end_ref[:, cols] = state
    for move in moves[3:]:
        move.wait()


def local_kernel(
    offset, mixed_ref, starts_ref, rates_ref, residues_ref, skip_ref, weight_hbm,
    local_ref, table_ref, weight_ref,
    sem,
):
    move = pltpu.make_async_copy(block_of(weight_hbm, offset, weight_ref.shape[1]), weight_ref, sem)
    move.start()
    rows, width = mixed_ref.shape
    modes = rates_ref.shape[0]
    row_ids = lax.broadcasted_iota(jnp.int32, (SUB, LANES), 0)
    steps = row_ids.astype(F32) + 1.0
    for lane in range(0, width, LANES):
        cols = slice(lane, lane + LANES)
        weights = residues_ref[:, cols] * jnp.sqrt(2.0 * rates_ref[:, cols])
        taps = jnp.zeros((SUB, LANES), F32)
        for mode in range(modes):
            entry = weights[mode : mode + 1, :] * jnp.exp(-rates_ref[mode : mode + 1, cols] * steps)
            table_ref[mode, :, cols] = entry
            taps = taps + entry
        first = jnp.sum(weights, axis=0, keepdims=True) + skip_ref[:, cols]
        masked = [jnp.where(row_ids >= lag, taps[lag - 1 : lag, :], 0.0) for lag in range(1, SUB)]
        totals = []
        for sub in range(0, rows, SUB):
            mixed = mixed_ref[sub : sub + SUB, cols]
            total = first * mixed
            for lag in range(1, SUB):
                total = total + masked[lag - 1] * pltpu.roll(mixed, lag, 0)
            totals.append(total)
        for mode in range(modes):
            entry = table_ref[mode, :, cols]
            totals = [
                total + entry * starts_ref[sub, mode : mode + 1, cols] if sub else total
                for sub, total in enumerate(totals)
            ]
        for sub, total in enumerate(totals):
            local_ref[sub * SUB : (sub + 1) * SUB, cols] = total
    move.wait()


def stages(size):
    steps, stride = [], 1
    while stride < size:
        radix = 4 if stride > 1 and size // stride % 4 == 0 else 2
        steps.append((stride, radix))
        stride *= radix
    return steps


def entering(stride, rows, states, rates):
    me = lax.axis_index("seq")
    digit = (me // stride) % (len(states) + 1)
    total = jnp.zeros(rates.shape, F32)
    for index, state in enumerate(states):
        other = digit ^ (index + 1)
        blocks = me % stride + stride * (digit - 1 - other)
        fade = jnp.exp(-rates * (rows * jnp.maximum(blocks, 0)).astype(F32))
        total = total + jnp.where(other < digit, fade, 0.0) * state
    return total


def join_kernel(stride, rows, arrivals, outs, total_ref, rates_ref, *refs):
    arrived_refs, before_refs, out_refs = refs[:arrivals], refs[arrivals:-outs], refs[-outs:]
    rates = rates_ref[...]
    states = [arrived_ref[...].astype(F32) for arrived_ref in arrived_refs[::-1]]
    carry = entering(stride, rows, states, rates)
    for before_ref in before_refs:
        carry = carry + before_ref[...]
    digit = (lax.axis_index("seq") // stride) % (len(states) + 1)
    joined = jnp.zeros(rates.shape, F32)
    for index, state in enumerate((total_ref[...], *states)):
        blocks = stride * (len(states) - (digit ^ index))
        joined = joined + jnp.exp(-rates * (rows * blocks).astype(F32)) * state
    for out_ref, value in zip(out_refs, (carry, joined, joined)):
        out_ref[...] = value.astype(out_ref.dtype)


def gate_kernel(
    base, stride,
    post_ref, local_ref, table_ref, rates_ref, carry_ref, weight_ref, *refs,
):
    *arrived_refs, gated_ref, first_ref, states_ref = refs
    height, width = gated_ref.shape
    modes = rates_ref.shape[0]
    subs = height // SUB
    rates = rates_ref[...]
    states = [arrived_ref[...].astype(F32) for arrived_ref in arrived_refs[::-1]]
    state = carry_ref[...] + entering(stride, post_ref.shape[0], states, rates)
    if base:
        state = state * jnp.exp(rates * (-float(base)))
    fade = jnp.exp(rates * (-float(SUB)))
    for sub in range(subs):
        states_ref[sub] = state
        state = state * fade
    for lane in range(0, width, LANES):
        cols = slice(lane, lane + LANES)
        totals = [local_ref[base + sub * SUB : base + (sub + 1) * SUB, cols] for sub in range(subs)]
        for mode in range(modes):
            entry = table_ref[mode, :, cols]
            totals = [
                total + entry * states_ref[sub, mode : mode + 1, cols] for sub, total in enumerate(totals)
            ]
        for sub in range(0, subs, 2):
            part = slice(base + sub * SUB, base + (sub + 2) * SUB)
            total = jnp.concatenate(totals[sub : sub + 2], axis=0)
            gated_ref[sub * SUB : (sub + 2) * SUB, cols] = (
                post_ref[part, cols].astype(F32) * total
            ).astype(BF16)
    first_ref[...] = jnp.dot(gated_ref[...], weight_ref[...], preferred_element_type=F32).astype(BF16)


def project_kernel(offsets, *refs):
    gated_refs, weight_ref, out_refs, gated_ref = refs[:PIECES], refs[PIECES], refs[PIECES + 1 : -1], refs[-1]
    spans = spans_of(gated_ref.shape[0])
    for span, half_ref in zip(spans, gated_refs):
        gated_ref[span, :] = half_ref[...]
    for slot, offset in enumerate(offsets):
        block = block_of(weight_ref, offset, out_refs[0].shape[1])[...]
        product = jnp.dot(gated_ref[...], block, preferred_element_type=F32)
        for piece, span in enumerate(spans):
            out_ref = out_refs[slot * PIECES + piece]
            out_ref[...] = product[span, :].astype(out_ref.dtype)


def finish_kernel(*refs):
    *done_refs, kept_ref, arrived_ref, out_hbm, last_ref, sems = refs
    moves = []
    for piece, span in enumerate(spans_of(out_hbm.shape[0])):
        if piece + 1 == PIECES:
            last_ref[...] = (kept_ref[...] + arrived_ref[...].astype(F32)).astype(BF16)
        moves.append(
            pltpu.make_async_copy(
                (*done_refs, last_ref)[piece],
                out_hbm.at[span, :],
                sems.at[piece],
            )
        )
        moves[-1].start()
    for move in moves:
        move.wait()


def after(value, *earlier):
    return lax.optimization_barrier((value, *earlier))[0]


def body(post_gate, pre_gate, signal, decay_rates, residues, skip_gain, out_weight):
    rows, width = post_gate.shape
    modes = decay_rates.shape[1]
    subs = rows // SUB
    size = lax.axis_size("seq")
    groups = lax.axis_size("chan")
    columns = out_weight.shape[1] // groups
    spans = spans_of(rows)
    heights = [span.stop - span.start for span in spans]
    whole = ((modes, width), F32)
    mixed, starts, end, rates, residues, skip, post = call(
        state_kernel,
        [HBM] * 6,
        [
            ((rows, width), F32),
            ((subs, modes, width), F32),
            whole,
            whole,
            whole,
            ((1, width), F32),
            ((rows, width), BF16),
        ],
        [pltpu.VMEM((rows, width), BF16), pltpu.VMEM((rows, width), BF16), DMA((6,))],
        4 * rows * modes * width,
        8 * rows * width,
    )(pre_gate, signal, decay_rates.T, residues.T, skip_gain.reshape(1, width), post_gate)
    def swap(state, distance):
        return lax.ppermute(state, "seq", [(source, source ^ distance) for source in range(size)])

    levels = stages(size)
    arrived, total, before = [swap(end, 1)], [end], []
    for level, (stride, radix) in enumerate(levels):
        if level:
            arrived = [swap(sent, stride * hop) for hop in range(radix - 1, 0, -1)]
        if level + 1 < len(levels):
            outs = [whole, ((modes, width), BF16)] + [whole] * (level + 2 < len(levels))
            carry, sent, *total = call(
                functools.partial(join_kernel, stride, rows, len(arrived), len(outs)),
                [VMEM] * (2 + len(arrived) + len(before)),
                outs,
                [],
                8 * radix * modes * width,
                16 * modes * width,
            )(*total, rates, *arrived, *before)
            before = [carry]
    local, table, weight = call(
        functools.partial(local_kernel, groups - 1),
        [VMEM] * 5 + [HBM],
        [((rows, width), F32), ((modes, SUB, width), F32), ((width, columns), BF16)],
        [DMA],
        2 * rows * (SUB + modes) * width,
        8 * rows * width,
    )(after(mixed, sent), starts, rates, residues, skip, out_weight)
    arrived[0] = after(arrived[0], local)

    gated, values = [], {groups - 1: []}
    for span, height in zip(spans, heights):
        half, first = call(
            functools.partial(gate_kernel, span.start, stride),
            [VMEM] * (6 + len(arrived)),
            [((height, width), BF16), ((height, columns), BF16)],
            [pltpu.VMEM((height // SUB, modes, width), F32)],
            2 * height * modes * width,
            16 * height * width,
        )(post, local, table, rates, carry, weight, *arrived)
        gated.append(half)
        values[groups - 1].append(first)

    offsets = list(range(groups - 2, -1, -1))
    shares = call(
        functools.partial(project_kernel, offsets),
        [VMEM] * (PIECES + 1),
        [((height, columns), BF16 if offset % 2 else F32) for offset in offsets for height in heights],
        [pltpu.VMEM((rows, width), BF16)],
        2 * rows * width * columns * len(offsets),
        2 * width * columns * len(offsets),
    )(*gated, out_weight)
    for slot, offset in enumerate(offsets):
        values[offset] = list(shares[slot * PIECES : (slot + 1) * PIECES])

    sums = []
    for offset in range(groups - 1, 0, -1):
        stride = offset & -offset
        target = offset ^ stride
        pairs = [(source, source ^ stride) for source in range(groups)]
        for piece in range(PIECES):
            index = len(sums)
            sent = values[offset][piece].astype(BF16)
            if index >= 2 * PIECES:
                sent = after(sent, sums[index - 2 * PIECES])
            arrived = lax.ppermute(sent, "chan", pairs)
            kept = values[target][piece]
            if piece:
                kept = after(kept, values[target][piece - 1])
            if offset == 1 and piece + 1 == PIECES:
                break
            values[target][piece] = kept + arrived.astype(F32)
            sums.append(values[target][piece].astype(BF16))
    done = [value.astype(BF16) for value in values[0][:-1]]
    return pl.pallas_call(
        finish_kernel,
        in_specs=[VMEM] * (PIECES + 1),
        out_shape=jax.ShapeDtypeStruct((rows, columns), BF16),
        out_specs=HBM,
        scratch_shapes=[pltpu.VMEM((heights[-1], columns), BF16), DMA((PIECES,))],
        compiler_params=pltpu.CompilerParams(vmem_limit_bytes=24 * 2**20),
    )(*done, kept, arrived)


def solution(mesh):
    return jax.shard_map(
        body,
        mesh=mesh,
        in_specs=(
            P("seq", "chan"),
            P("seq", "chan"),
            P("seq", "chan"),
            P("chan", None),
            P("chan", None),
            P("chan"),
            P("chan", None),
        ),
        out_specs=P("seq", "chan"),
        check_vma=False,
    )
```
